32 devices in a mesh: expert: 8 (over z, x), hidden: 4 (over y, core).
Axes of the slice: x: 2, y: 2, z: 4, core: 2. Of those that a mesh axis runs over, the one named last changes fastest.
Arguments:
- tokens: bfloat16 [2048, 1152], P('expert'), may hold values from -6 to 6
- cotangent: bfloat16 [2048, 1152], P('expert'), may hold values from -6 to 6
- seq_lengths: int32 [8, 2], P('expert'), may hold values from 128 to 128, as said below
- routes: int32 [2048, 1], P('expert'), may hold values from 0 to 7; in each aligned block of 256 rows (0 to 255, 256 to 511, ...) at most 48 rows name the same one
- mixer_gain: bfloat16 [1152], P('expert'), may hold values from 0.5 to 1.5
- proj_x: bfloat16 [1152, 2304], P(None, ('expert', 'hidden')), may hold values from -0.1875 to 0.1875
- proj_z: bfloat16 [1152, 2304], P(None, ('expert', 'hidden')), may hold values from -0.1875 to 0.1875
- conv_weight: bfloat16 [4, 2304], P(None, ('expert', 'hidden')), may hold values from -3 to 3
- conv_bias: bfloat16 [2304], P(('expert', 'hidden')), may hold values from -3 to 3
- state_proj: bfloat16 [2304, 104], P(('expert', 'hidden')), may hold values from -0.125 to 0.125
- step_proj: bfloat16 [72, 2304], P(None, ('expert', 'hidden')), may hold values from -0.75 to 0.75
- step_bias: bfloat16 [2304], P(('expert', 'hidden')), may hold values from -6 to -2
- decay_log: bfloat16 [16, 2304], P(None, ('expert', 'hidden')), may hold values from 0 to 2.765625
- skip_gain: bfloat16 [2304], P(('expert', 'hidden')), may hold values from 0.5 to 1.5
- out_proj: bfloat16 [2304, 1152], P(('expert', 'hidden')), may hold values from -0.125 to 0.125
- moe_gain: bfloat16 [1152], P('expert'), may hold values from 0.5 to 1.5
- router: bfloat16 [1152, 8], P('expert'), may hold values from -0.09375 to 0.09375
- expert_up: bfloat16 [8, 1152, 3072], P(None, None, 'hidden'), may hold values from -0.1875 to 0.1875
- expert_down: bfloat16 [8, 3072, 1152], P(None, 'hidden'), may hold values from -0.15625 to 0.15625
Outputs:
- layer_out: bfloat16 [2048, 1152], P('expert')
- tokens_grad: float32 [2048, 1152], P('expert')
- mixer_gain_grad: float32 [1152], P('expert')
- proj_x_grad: float32 [1152, 2304], P(None, ('expert', 'hidden'))
- proj_z_grad: float32 [1152, 2304], P(None, ('expert', 'hidden'))
- conv_weight_grad: float32 [4, 2304], P(None, ('expert', 'hidden'))
- conv_bias_grad: float32 [2304], P(('expert', 'hidden'))
- state_proj_grad: float32 [2304, 104], P(('expert', 'hidden'))
- step_proj_grad: float32 [72, 2304], P(None, ('expert', 'hidden'))
- step_bias_grad: float32 [2304], P(('expert', 'hidden'))
- decay_log_grad: float32 [16, 2304], P(None, ('expert', 'hidden'))
- skip_gain_grad: float32 [2304], P(('expert', 'hidden'))
- out_proj_grad: float32 [2304, 1152], P(('expert', 'hidden'))
- moe_gain_grad: float32 [1152], P('expert')
- router_grad: float32 [1152, 8], P('expert')
- expert_up_grad: float32 [8, 1152, 3072], P(None, 'expert', 'hidden')
- expert_down_grad: float32 [8, 3072, 1152], P(None, 'hidden', 'expert')
The draws below stay inside these ranges and needn't reach their ends.
Inputs may be any that keep to these rules, and one draw needn't show every extreme that they name: `seq_lengths`: on each index of expert the two lengths sum to at most 256, and to exactly 256 on some index. `routes`: among the 256 rows of one device no expert is named by more than 48 rows.
All inputs are finite; a program needn't handle non-finite values.
Results may differ from the reference program's by a relative error of at most 0.015.
Values may be sent and summed in bfloat16 or wider, within the bound.
No kernel may reach another device: no remote copies, remote signals or barrier semaphores. Data moves between devices by JAX's collectives and lax.ppermute only.
A program may use at most 256 MiB of HBM per device.

```python
import math
import jax
import jax.numpy as jnp
import numpy as np
from jax import lax

D = 1152
DI = 2304
FF = 3072
STEP_SIZE_RANK = 72
STATE = 16
EXPERTS = 8
CONV = 4
SINK_ITERS = 8
MIN_LEN = 128
TOK_DEV = 256
CAP = 48
TOKENS = 2048
N_EXPERT = 8


def draw_seq_lengths(key, part):
    blocks = TOKENS // TOK_DEV
    first_key = jax.random.fold_in(key, 11)
    total_key = jax.random.fold_in(key, 23)
    pick_key = jax.random.fold_in(key, 37)
    first = jax.random.randint(first_key, (blocks,), MIN_LEN, TOK_DEV - MIN_LEN + 1)
    ending = jax.random.randint(total_key, (blocks,), first + MIN_LEN, TOK_DEV + 1)
    chosen = jax.random.randint(pick_key, (), 0, blocks)
    marked = jnp.arange(blocks) == chosen
    first = jnp.where(marked, MIN_LEN, first)
    ending = jnp.where(marked, TOK_DEV, ending)
    return jnp.stack([first, ending - first], axis=1).astype(jnp.int32)


def block_levels(rng, dims, shards, smallest, high):
    def one(dim, shards_of):
        steps = jax.random.uniform(jax.random.fold_in(jax.random.fold_in(rng, 6), dim), (shards_of,), jnp.float32, smallest / len(shards), high / len(shards))
        return jnp.repeat(jnp.exp(steps), dims[dim] // shards_of).reshape((-1,) + (1,) * (len(dims) - dim - 1))

    loudness = one(*shards[0])
    for cut in shards[1:]:
        loudness = loudness * one(*cut)
    return loudness


def deal_out(rng, own, number, rows, count, top, most, slope):
    order = jax.random.permutation(rng, count)
    heavy_load, common = portions_of(count, rows * top, most, slope, True), portions_of(count, rows * top, most, slope, False)
    places = jnp.arange(count)

    def named(tallies, rotation):
        used = int((tallies > 0).sum())
        fixed = max(1, used // 4)
        shifted = fixed + (places - fixed + rotation * (used - fixed)) % max(1, count - fixed)
        return jnp.zeros((count,), jnp.int32).at[order[jnp.where(places < fixed, places, shifted)]].set(jnp.asarray(tallies, jnp.int32))

    tallies = jnp.where(number % 4 == 0, named(heavy_load, number // 4), named(common, number - number // 4 - 1))
    mixed = jax.random.permutation(jax.random.fold_in(own, 3), count)
    giver, sink = mixed[0:count // 2 * 2:2], mixed[1:count // 2 * 2:2]
    room = jnp.minimum(tallies[giver] - 1, most - tallies[sink]) // 2
    room = jnp.where((giver == order[0]) | (sink == order[0]) | (tallies[sink] == 0), 0, jnp.maximum(room, 0))
    shifted = jax.random.randint(jax.random.fold_in(own, 4), (count // 2,), 0, 1 << 20) % (room + 1)
    tallies = tallies.at[giver].add(-shifted).at[sink].add(shifted)
    items = jnp.searchsorted(jnp.cumsum(tallies), jnp.arange(rows * top), side="right").astype(jnp.int32)
    table = items.reshape(top, rows).T
    table = table[jax.random.permutation(jax.random.fold_in(own, 1), rows)]
    rotation = jax.random.randint(jax.random.fold_in(own, 2), (rows, 1), 0, top)
    return jnp.take_along_axis(table, (jnp.arange(top)[None, :] + rotation) % top, axis=1)


def portions_of(number_of, total, reach, slope, full):
    portions = [(1 << 20) // math.isqrt(rank ** slope) + 1 for rank in range(1, number_of + 1)]
    largest = reach if full else min(reach, max(-(-total // number_of), total * portions[0] // sum(portions)))
    least = 1 if total - largest >= number_of - 1 else 0
    given, spare = [largest] + [least] * (number_of - 1), total - largest - least * (number_of - 1)
    while spare > 0:
        free = [i for i in range(1, number_of) if given[i] < largest] or [i for i in range(1, number_of) if given[i] < reach]
        whole, budget = sum([portions[i] for i in free]), spare
        for i in free:
            extra = min(reach - given[i], max(1, budget * portions[i] // whole), spare)
            given[i] = given[i] + extra
            spare = spare - extra
    return np.array(given)


def centred(rng, shape, width, most, cuts=(), kind=jnp.bfloat16):
    level = block_levels(rng, shape, cuts, -0.22, 0.18) if cuts else 1.0
    values = jax.random.normal(rng, shape, jnp.float32) * width * level
    return jnp.minimum(jnp.maximum(values, -most), most).astype(kind)


def setup_inputs(seed: int = 0) -> dict:
    seeds = jax.random.split(jax.random.key(seed), 20)
    tokens = centred(seeds[0], (TOKENS, D), 1.0, 6.0, ((0, 8),))
    cotangent = centred(seeds[1], (TOKENS, D), 1.0, 6.0, ((0, 8),))
    seq_lengths = draw_seq_lengths(jax.random.fold_in(seeds[19], 71), 0)
    routes_keys = jax.random.split(jax.random.fold_in(seeds[3], 1), TOKENS // TOK_DEV)
    routes_turns = jax.random.permutation(jax.random.fold_in(seeds[3], 3), TOKENS // TOK_DEV)
    routes = jax.vmap(lambda own, number: deal_out(jax.random.fold_in(seeds[3], 2), own, number, TOK_DEV, EXPERTS, 1, CAP, 2))(routes_keys, routes_turns).reshape((TOKENS, 1))
    mixer_gain = jnp.clip(1.0 + 0.1 * jax.random.normal(seeds[4], (D,), jnp.float32), 0.5, 1.5).astype(jnp.bfloat16)
    proj_x = centred(seeds[5], (D, DI), D ** -0.5, 0.1875, ((1, 32),))
    proj_z = centred(seeds[6], (D, DI), D ** -0.5, 0.1875, ((1, 32),))
    conv_weight = centred(seeds[7], (CONV, DI), CONV ** -0.5, 3.0, ((1, 32),))
    conv_bias = centred(seeds[8], (DI,), 0.5, 3.0, ((0, 32),))
    state_proj = centred(seeds[9], (DI, STEP_SIZE_RANK + 2 * STATE), DI ** -0.5, 0.125, ((0, 32),))
    step_proj = centred(seeds[10], (STEP_SIZE_RANK, DI), STEP_SIZE_RANK ** -0.5, 0.75, ((1, 32),))
    step_bias = jnp.clip(-6.0 + 4.0 * jax.random.uniform(seeds[11], (DI,), jnp.float32) ** block_levels(seeds[11], (DI,), ((0, 32),), -0.2, 0.2), -6.0, -2.0).astype(jnp.bfloat16)
    decay_log = jnp.clip(2.765625 * jax.random.uniform(seeds[12], (STATE, DI), jnp.float32) ** block_levels(seeds[12], (STATE, DI), ((1, 32),), -0.2, 0.2), 0.0, 2.765625).astype(jnp.bfloat16)
    skip_gain = jnp.clip(0.5 + 1.0 * jax.random.uniform(seeds[13], (DI,), jnp.float32) ** block_levels(seeds[13], (DI,), ((0, 32),), -0.2, 0.2), 0.5, 1.5).astype(jnp.bfloat16)
    out_proj = centred(seeds[14], (DI, D), DI ** -0.5, 0.125, ((0, 32),))
    moe_gain = jnp.clip(1.0 + 0.1 * jax.random.normal(seeds[15], (D,), jnp.float32), 0.5, 1.5).astype(jnp.bfloat16)
    router = centred(seeds[16], (D, EXPERTS), (4 * D) ** -0.5, 0.09375, ((0, 8),))
    expert_up = centred(seeds[17], (EXPERTS, D, FF), D ** -0.5, 0.1875, ((2, 4),))
    expert_down = centred(seeds[18], (EXPERTS, FF, D), (FF // 2) ** -0.5, 0.15625, ((1, 4),))
    return {"tokens": tokens, "cotangent": cotangent, "seq_lengths": seq_lengths, "routes": routes, "mixer_gain": mixer_gain, "proj_x": proj_x, "proj_z": proj_z, "conv_weight": conv_weight, "conv_bias": conv_bias, "state_proj": state_proj, "step_proj": step_proj, "step_bias": step_bias, "decay_log": decay_log, "skip_gain": skip_gain, "out_proj": out_proj, "moe_gain": moe_gain, "router": router, "expert_up": expert_up, "expert_down": expert_down}


epsilon = 1e-05

@jax.custom_vjp
def low(v):
    return lax.optimization_barrier(v.astype(jnp.bfloat16)).astype(jnp.float32)

@jax.custom_vjp
def low_back(v):
    return v

def low_keep(v):
    return (low(v), None)

def low_pass(kept, grad):
    return (grad,)

def back_keep(v):
    return (v, None)

def back_low(kept, grad):
    return (low(grad),)
low.defvjp(low_keep, low_pass)
low_back.defvjp(back_keep, back_low)

def matmul(left, right):
    return jnp.dot(left, right, precision=lax.Precision.HIGHEST)

def rms_scale(values):
    return lax.rsqrt(lax.optimization_barrier(jnp.mean(values * values, axis=-1, keepdims=True)) + epsilon)

def causal_conv(values, segment, kernel, offset):
    taps = kernel.shape[0]
    length = values.shape[0]
    result = offset[None, :] + kernel[taps - 1][None, :] * values
    for delay in range(1, taps):
        moved = jnp.concatenate([jnp.zeros((delay, values.shape[1]), values.dtype), values[:length - delay]], axis=0)
        moved_seg = jnp.concatenate([jnp.full((delay,), -1, jnp.int32), segment[:length - delay]])
        same = (moved_seg == segment).astype(values.dtype)
        result = result + kernel[taps - 1 - delay][None, :] * moved * same[:, None]
    return result

def scan_block(pieces, step_bias, decay_log, skip_gain):
    activity, gate_z, step_pre, in_b, in_c, segment = pieces
    step_size = jax.nn.softplus(step_pre + step_bias[None, :])
    decay_rates = -jnp.exp(decay_log)
    earlier = jnp.concatenate([jnp.full((1,), -1, jnp.int32), segment[:-1]])
    persist = (segment == earlier).astype(step_size.dtype)

    def advance(memory, current):
        step_row, act_row, b_row, c_row, keep_row = current
        memory = keep_row * jnp.exp(step_row[None, :] * decay_rates) * memory + (step_row * act_row)[None, :] * b_row[:, None]
        return (memory, lax.optimization_barrier(jnp.sum(c_row[:, None] * memory, axis=0)))
    initial = jnp.zeros(decay_rates.shape, step_size.dtype)
    _, outputs = lax.scan(advance, initial, (step_size, activity, in_b, in_c, persist))
    return (outputs + skip_gain[None, :] * activity) * jax.nn.silu(gate_z)

def balanced_normalize(router_logits, valid_float, flattened_routes):
    weights = jnp.exp(router_logits)
    for sweep_index in range(SINK_ITERS):
        columns = lax.optimization_barrier(jnp.sum(weights * valid_float[:, None], axis=0))
        scaled = weights / columns[None, :]
        weights = scaled / lax.optimization_barrier(jnp.sum(scaled, axis=1, keepdims=True))
    onehot = (flattened_routes[:, None] == jnp.arange(EXPERTS)[None, :]).astype(weights.dtype)
    return EXPERTS * lax.optimization_barrier(jnp.sum(weights * onehot, axis=1))

def experts_apply(expert_in, flattened_routes, valid, expert_up, expert_down):
    limit = N_EXPERT * CAP

    def visit(running, pieces):
        number, up_weight, down_weight = pieces
        chosen = (flattened_routes == number) & valid
        index = jnp.nonzero(chosen, size=limit, fill_value=0)[0].astype(jnp.int32)
        present = (jnp.arange(limit) < jnp.sum(chosen.astype(jnp.int32))).astype(expert_in.dtype)
        selected = jnp.take(expert_in, index, axis=0)
        pre_act = low_back(matmul(selected, up_weight))
        active = low(jax.nn.gelu(pre_act))
        result = matmul(active, down_weight) * present[:, None]
        return (running.at[index].add(result), None)
    start = jnp.zeros(expert_in.shape, expert_in.dtype)
    running, _ = lax.scan(jax.checkpoint(visit), start, (jnp.arange(EXPERTS), expert_up, expert_down))
    return running

def forward_pass(resid, params, valid_float, valid, segment, flattened_routes):
    mixer_gain, proj_x, proj_z, conv_weight, conv_bias, state_proj, step_proj, step_bias, decay_log, skip_gain, out_proj, moe_gain, router, expert_up, expert_down = params
    normed = low(resid * rms_scale(resid) * mixer_gain[None, :])
    inner_x = low_back(matmul(normed, proj_x))
    inner_z = low_back(matmul(normed, proj_z))
    blocks_x = inner_x.reshape(-1, TOK_DEV, DI)
    convolved = jax.vmap(causal_conv, in_axes=(0, 0, None, None))(blocks_x, segment, conv_weight, conv_bias)
    activity = low(jax.nn.silu(convolved)).reshape(TOKENS, DI)
    projected = low_back(matmul(activity, state_proj))
    step_rank = low(projected[:, :STEP_SIZE_RANK])
    in_b = projected[:, STEP_SIZE_RANK:STEP_SIZE_RANK + STATE]
    in_c = projected[:, STEP_SIZE_RANK + STATE:]
    step_pre = low_back(matmul(step_rank, step_proj))

    def block_fn(pieces):
        return scan_block(pieces, step_bias, decay_log, skip_gain)

    def shaped(values):
        return values.reshape(-1, TOK_DEV, values.shape[-1])
    gated = lax.map(jax.checkpoint(block_fn), (shaped(activity), shaped(inner_z), shaped(step_pre), shaped(in_b), shaped(in_c), segment))
    mixed = low(gated.reshape(TOKENS, DI))
    branch = low_back(matmul(mixed, out_proj))
    hidden_res = resid + branch
    normed_two = low(hidden_res * rms_scale(hidden_res) * moe_gain[None, :])
    router_logits = low_back(matmul(normed_two, router))
    gate_values = balanced_normalize(router_logits, valid_float, flattened_routes)
    expert_in = low_back(normed_two)
    expert_out = experts_apply(expert_in, flattened_routes, valid, expert_up, expert_down)
    returned = low_back(low(expert_out))
    return valid_float[:, None] * (hidden_res + gate_values[:, None] * returned)

def reference(tokens, cotangent, seq_lengths, routes, mixer_gain, proj_x, proj_z, conv_weight, conv_bias, state_proj, step_proj, step_bias, decay_log, skip_gain, out_proj, moe_gain, router, expert_up, expert_down):
    places = jnp.arange(TOK_DEV, dtype=jnp.int32)
    first = seq_lengths[:, 0:1]
    ending = first + seq_lengths[:, 1:2]
    segment = (places[None, :] >= first).astype(jnp.int32) + (places[None, :] >= ending).astype(jnp.int32)
    valid = (places[None, :] < ending).reshape(TOKENS)
    valid_float = valid.astype(jnp.float32)
    flattened_routes = routes[:, 0]
    params = (mixer_gain.astype(jnp.float32), proj_x.astype(jnp.float32), proj_z.astype(jnp.float32), conv_weight.astype(jnp.float32), conv_bias.astype(jnp.float32), state_proj.astype(jnp.float32), step_proj.astype(jnp.float32), step_bias.astype(jnp.float32), decay_log.astype(jnp.float32), skip_gain.astype(jnp.float32), out_proj.astype(jnp.float32), moe_gain.astype(jnp.float32), router.astype(jnp.float32), expert_up.astype(jnp.float32), expert_down.astype(jnp.float32))

    def wrapped_function(resid, weights):
        return forward_pass(resid, weights, valid_float, valid, segment, flattened_routes)
    result, pullback = jax.vjp(wrapped_function, tokens.astype(jnp.float32), params)
    tokens_grad, grads = pullback(cotangent.astype(jnp.float32))
    return (result.astype(jnp.bfloat16), tokens_grad, grads[0], grads[1], grads[2], grads[3], grads[4], grads[5], grads[6], grads[7], grads[8], grads[9], grads[10], grads[11], grads[12], grads[13], grads[14])
```

```python
import jax
import jax.numpy as jnp
from jax import lax
from jax.experimental import pallas as pl
from jax.experimental.pallas import tpu as pltpu
from jax.sharding import PartitionSpec as P

SINK_ITERS = 8
GROUP = 8
LANES = 128
ROWS = 8
FAR = 1e30
LOG2E = 1.4426950408889634
epsilon = 1e-05
f32 = jnp.float32
bf16 = jnp.bfloat16


def product(left, right):
    return jnp.dot(left, right, preferred_element_type=f32)


def ein(spec, left, right):
    return jnp.einsum(spec, left, right, preferred_element_type=f32)


def rms_scale(values):
    return lax.rsqrt(jnp.mean(values * values, axis=-1, keepdims=True) + epsilon)


def swap(values, axis, bits):
    size = lax.axis_size(axis)
    return lax.ppermute(values, axis, [(i, i ^ bits) for i in range(size)])


def gather_doubling(values, axis):
    held = values[None]
    bits = 1
    while bits < lax.axis_size(axis):
        held = jnp.concatenate([held, swap(held, axis, bits)])
        bits *= 2
    return held


def gather_direct(values, axis):
    size = lax.axis_size(axis)
    if size > GROUP:
        return gather_doubling(values, axis)
    return jnp.stack([values] + [swap(values, axis, r) for r in range(1, size)])


def scatter_sum(values, axis):
    size = values.shape[0]
    while size > 1:
        size //= 2
        values = values[:size] + swap(values[size:].astype(bf16), axis, size).astype(f32)
    return values[0]


def exchange(values, axis):
    size = values.shape[0]
    if size > GROUP:
        order = jnp.arange(size) ^ lax.axis_index(axis)
        moved = lax.all_to_all(jnp.take(values, order, axis=0), axis, 0, 0, tiled=True)
        return jnp.take(moved, order, axis=0)
    return jnp.stack([values[0]] + [swap(values[r], axis, r) for r in range(1, size)])


def hidden_sum(values):
    half = values.shape[0] // 2
    place = lax.axis_index("hidden") % 2
    kept = lax.dynamic_slice_in_dim(values, place * half, half, 0)
    given = lax.dynamic_slice_in_dim(values, (1 - place) * half, half, 0)
    total = kept.astype(bf16).astype(f32) + swap(given.astype(bf16), "hidden", 1).astype(f32)
    low = total.astype(bf16)
    low = (low.astype(f32) + swap(low, "hidden", 2).astype(f32)).astype(bf16)
    other = swap(low, "hidden", 1)
    return jnp.where(
        place == 0, jnp.concatenate([low, other]), jnp.concatenate([other, low])
    ).astype(f32)


def hidden_sum_small(values):
    values = values + swap(values, "hidden", 1)
    return values + swap(values, "hidden", 2)


def gather_tokens(values, base):
    place = lax.axis_index("hidden")
    size = values.shape[0] // 4
    own = lax.dynamic_slice_in_dim(values, place * size, size, 0)
    if base > 0:
        own = swap(own, "expert", base)
    group = min(lax.axis_size("expert"), GROUP)
    held = jnp.stack([own] + [swap(own, "expert", r) for r in range(1, group)])
    far = swap(held, "hidden", 2)
    near = swap(held, "hidden", 1)
    both = swap(far, "hidden", 1)
    count = held.shape[0]
    whole = jnp.zeros((count, 4 * size, values.shape[1]), values.dtype)
    for r, piece in ((0, held), (1, near), (2, far), (3, both)):
        whole = lax.dynamic_update_slice(whole, piece, (0, (place ^ r) * size, 0))
    return whole


def causal_conv(values, segment, kernel, offset):
    taps = kernel.shape[0]
    length = values.shape[0]
    result = offset[None, :] + kernel[taps - 1][None, :] * values
    for delay in range(1, taps):
        moved = jnp.concatenate(
            [jnp.zeros((delay, values.shape[1]), values.dtype), values[: length - delay]], axis=0
        )
        moved_seg = jnp.concatenate([jnp.full((delay,), -1, jnp.int32), segment[: length - delay]])
        same = (moved_seg == segment).astype(values.dtype)
        result = result + kernel[taps - 1 - delay][None, :] * moved * same[:, None]
    return result


def softplus(values):
    return jnp.maximum(values, 0.0) + jnp.log1p(jnp.exp(-jnp.abs(values)))


def sigmoid(values):
    return 1.0 / (1.0 + jnp.exp(-values))


def put(ref, values):
    width = values.shape[1]
    ref[:, :width] = values
    if ref.shape[1] > width:
        ref[:, width:] = jnp.zeros((values.shape[0], ref.shape[1] - width), ref.dtype)


def widen(tile, width):
    return jnp.concatenate([tile] * (width // LANES), axis=1)


def fold(values):
    total = values[:, :LANES]
    for k in range(1, values.shape[1] // LANES):
        total = total + values[:, k * LANES : (k + 1) * LANES]
    return total


def scan_forward_body(
    pre, act, gate, basis_b, basis_c, bias, decay, skip, keep,
    mixed, out, states, far_steps, inputs, rates, sums,
):
    width = far_steps.shape[1]
    channels = pre.shape[1]
    step = softplus(pre[...] + bias[...])
    put(far_steps, jnp.where(keep[...] > 0, step, FAR))
    put(inputs, step * act[...])
    put(rates, -LOG2E * jnp.exp(decay[...]))
    rate = rates[...]

    def block(i, memory):
        base = pl.multiple_of(i * ROWS, ROWS)
        step_rows = far_steps[pl.ds(base, ROWS), :]
        input_rows = inputs[pl.ds(base, ROWS), :]
        rows = []
        for j in range(ROWS):
            factor = jnp.exp2(step_rows[j : j + 1] * rate)
            memory = factor * memory + input_rows[j : j + 1] * widen(basis_b[base + j], width)
            states[base + j] = memory
            rows.append(jnp.sum(widen(basis_c[base + j], width) * memory, axis=0, keepdims=True))
        sums[pl.ds(base, ROWS), :] = jnp.concatenate(rows, axis=0)
        return memory

    lax.fori_loop(0, pre.shape[0] // ROWS, block, jnp.zeros(rate.shape, f32))
    total = sums[:, :channels]
    out[...] = total
    silu = gate[...] * sigmoid(gate[...])
    mixed[...] = ((total + skip[...] * act[...]) * silu).astype(bf16)


def scan_backward_body(
    grad, out, act, gate, pre, bias, decay, skip, keep, basis_b, basis_c, states,
    grad_act, grad_gate, grad_pre, part_b, part_c, grad_bias, grad_decay, grad_skip,
    far_steps, steps, inputs, outer, rates, sum_input, sum_step,
):
    width = far_steps.shape[1]
    channels = pre.shape[1]
    step = softplus(pre[...] + bias[...])
    put(far_steps, jnp.where(keep[...] > 0, step, FAR))
    put(steps, step)
    put(inputs, step * act[...])
    put(rates, -jnp.exp(decay[...]))
    shade = sigmoid(gate[...])
    through = grad[...] * gate[...] * shade
    put(outer, through)
    grad_gate[...] = (
        grad[...]
        * (out[...] + skip[...] * act[...])
        * (shade * (1.0 + gate[...] * (1.0 - shade)))
    ).astype(bf16)
    grad_skip[...] = jnp.sum(through * act[...], axis=0, keepdims=True)
    rate = rates[...]
    quick = rate * LOG2E
    blocks = pre.shape[0] // ROWS

    def block(i, carried):
        later, rate_sum = carried
        base = pl.multiple_of((blocks - 1 - i) * ROWS, ROWS)
        far_rows = far_steps[pl.ds(base, ROWS), :]
        step_rows = steps[pl.ds(base, ROWS), :]
        input_rows = inputs[pl.ds(base, ROWS), :]
        outer_rows = outer[pl.ds(base, ROWS), :]
        input_sums = [None] * ROWS
        step_sums = [None] * ROWS
        for j in reversed(range(ROWS)):
            tile_b = widen(basis_b[base + j], width)
            outside = outer_rows[j : j + 1]
            inside = input_rows[j : j + 1]
            state = states[base + j]
            flow = widen(basis_c[base + j], width) * outside + later
            later = jnp.exp2(far_rows[j : j + 1] * quick) * flow
            part_c[base + j] = fold(outside * state)
            part_b[base + j] = fold(flow * inside)
            input_sums[j] = jnp.sum(flow * tile_b, axis=0, keepdims=True)
            turned = flow * (state - inside * tile_b)
            step_sums[j] = jnp.sum(turned * rate, axis=0, keepdims=True)
            rate_sum = rate_sum + turned * step_rows[j : j + 1]
        sum_input[pl.ds(base, ROWS), :] = jnp.concatenate(input_sums, axis=0)
        sum_step[pl.ds(base, ROWS), :] = jnp.concatenate(step_sums, axis=0)
        return later, rate_sum

    zero = jnp.zeros(rate.shape, f32)
    _, rate_sum = lax.fori_loop(0, blocks, block, (zero, zero))
    grad_decay[...] = (rate_sum * rate)[:, :channels]
    back_input = sum_input[:, :channels]
    grad_act[...] = outer[:, :channels] * skip[...] + back_input * step
    grad_step = (back_input * act[...] + sum_step[:, :channels]) * sigmoid(pre[...] + bias[...])
    grad_pre[...] = grad_step.astype(bf16)
    grad_bias[...] = jnp.sum(grad_step, axis=0, keepdims=True)


def shape_of(*dims):
    return jax.ShapeDtypeStruct(dims, f32)


def scan_forward(pre, act, gate, basis_b, basis_c, bias, decay, skip, keep):
    positions, channels = pre.shape
    entries = decay.shape[0]
    width = -(-channels // LANES) * LANES
    return pl.pallas_call(
        scan_forward_body,
        out_shape=(
            jax.ShapeDtypeStruct((positions, channels), bf16),
            shape_of(positions, channels),
            shape_of(positions, entries, width),
        ),
        scratch_shapes=[
            pltpu.VMEM((positions, width), f32),
            pltpu.VMEM((positions, width), f32),
            pltpu.VMEM((entries, width), f32),
            pltpu.VMEM((positions, width), f32),
        ],
        compiler_params=pltpu.CompilerParams(vmem_limit_bytes=48 * 2**20),
        name="scan_forward",
    )(pre, act, gate, basis_b, basis_c, bias, decay, skip, keep)


def scan_backward(
    grad, out, act, gate, pre, bias, decay, skip, keep, basis_b, basis_c, states
):
    positions, channels = pre.shape
    entries, width = states.shape[1:]
    wide = pltpu.VMEM((positions, width), f32)
    return pl.pallas_call(
        scan_backward_body,
        out_shape=(
            shape_of(positions, channels),
            jax.ShapeDtypeStruct((positions, channels), bf16),
            jax.ShapeDtypeStruct((positions, channels), bf16),
            shape_of(positions, entries, LANES),
            shape_of(positions, entries, LANES),
            shape_of(1, channels),
            shape_of(entries, channels),
            shape_of(1, channels),
        ),
        scratch_shapes=[wide, wide, wide, wide, pltpu.VMEM((entries, width), f32), wide, wide],
        compiler_params=pltpu.CompilerParams(vmem_limit_bytes=56 * 2**20),
        name="scan_backward",
    )(grad, out, act, gate, pre, bias, decay, skip, keep, basis_b, basis_c, states)


def sweeps(start, valid):
    weights = start
    history = []
    for _ in range(SINK_ITERS):
        columns = jnp.sum(jnp.sum(weights * valid, axis=2, keepdims=True), axis=0, keepdims=True)
        scaled = weights / columns
        row_sums = jnp.sum(scaled, axis=1, keepdims=True)
        weights = scaled / row_sums
        history.append((columns, scaled, row_sums, weights))
    return weights, history


def chosen(codes, shape):
    return (lax.broadcasted_iota(jnp.int32, shape, 1).astype(f32) == codes).astype(f32)


def sinkhorn_body(logits, routes, gates):
    start = jnp.exp(logits[...])
    valid = (routes[:, 1:2, :] > 0).astype(f32)
    weights, _ = sweeps(start, valid)
    onehot = chosen(routes[:, 0:1, :], start.shape)
    gates[...] = start.shape[1] * jnp.sum(weights * onehot, axis=1, keepdims=True)


def sinkhorn_back_body(logits, routes, grad_gates, grad_logits):
    start = jnp.exp(logits[...])
    valid = (routes[:, 1:2, :] > 0).astype(f32)
    _, history = sweeps(start, valid)
    onehot = chosen(routes[:, 0:1, :], start.shape)
    grads = start.shape[1] * grad_gates[...] * onehot
    for columns, scaled, row_sums, result in reversed(history):
        grads = (grads - jnp.sum(grads * result, axis=1, keepdims=True)) / row_sums
        term = jnp.sum(jnp.sum(grads * scaled, axis=2, keepdims=True), axis=0, keepdims=True)
        grads = (grads - valid * term) / columns
    grad_logits[...] = (grads * start)[0]


def sinkhorn(logits, routes):
    count, experts, positions = logits.shape
    return pl.pallas_call(
        sinkhorn_body,
        out_shape=shape_of(count, 1, positions),
        compiler_params=pltpu.CompilerParams(vmem_limit_bytes=48 * 2**20),
        name="sinkhorn_forward",
    )(logits, routes)


def sinkhorn_back(logits, routes, grad_gates):
    count, experts, positions = logits.shape
    return pl.pallas_call(
        sinkhorn_back_body,
        out_shape=shape_of(experts, positions),
        compiler_params=pltpu.CompilerParams(vmem_limit_bytes=48 * 2**20),
        name="sinkhorn_backward",
    )(logits, routes, grad_gates)


def expert_grads(picker, rows, grad_rows, up, down, place, block):
    count, slots, _ = picker.shape
    experts, width, _ = up.shape

    def spread(values):
        picked = ein("nst,ntd->nsd", picker, values).astype(bf16)
        picked = picked.reshape(count, experts, slots // experts, width)
        return picked.transpose(1, 0, 2, 3).reshape(experts, count * slots // experts, width)

    arrived = spread(rows)
    arrived_grad = spread(grad_rows)
    active, back = jax.vjp(jax.nn.gelu, ein("erd,edf->erf", arrived, up))
    grad_pre = back(ein("erd,efd->erf", arrived_grad, down))[0].astype(bf16)
    own = lax.dynamic_slice_in_dim(arrived, place * block, block, 2)
    own_grad = lax.dynamic_slice_in_dim(arrived_grad, place * block, block, 2)
    return (
        ein("erd,erf->edf", own, grad_pre),
        ein("erf,erd->efd", active.astype(bf16), own_grad),
    )


def local(
    tokens,
    cotangent,
    seq_lengths,
    routes,
    mixer_gain,
    proj_x,
    proj_z,
    conv_weight,
    conv_bias,
    state_proj,
    step_proj,
    step_bias,
    decay_log,
    skip_gain,
    out_proj,
    moe_gain,
    router,
    expert_up,
    expert_down,
):
    devices = lax.axis_size("expert")
    index = lax.axis_index("expert")
    order = jnp.arange(devices) ^ index
    positions, width = tokens.shape
    block = mixer_gain.shape[0]
    experts = expert_up.shape[0]
    own_channels = proj_x.shape[1]
    channels = devices * own_channels
    rank = step_proj.shape[0]
    entries = decay_log.shape[0]
    taps = conv_weight.shape[0]
    capacity = 3 * positions // (2 * experts)

    places = jnp.arange(positions, dtype=jnp.int32)
    first = seq_lengths[0, 0]
    ending = first + seq_lengths[0, 1]
    segment = (places >= first).astype(jnp.int32) + (places >= ending).astype(jnp.int32)
    valid = places < ending
    valid_float = valid.astype(f32)
    earlier = jnp.concatenate([jnp.full((1,), -1, jnp.int32), segment[:-1]])
    persist = (segment == earlier).astype(f32)

    vectors = jnp.concatenate([mixer_gain[None], moe_gain[None], router.T])
    vectors = jnp.take(gather_doubling(vectors, "expert"), order, axis=0)
    vectors = vectors.transpose(1, 0, 2).reshape(2 + experts, width)
    gain_one = vectors[0].astype(f32)
    gain_two = vectors[1].astype(f32)
    router_full = vectors[2:]
    small = jnp.concatenate(
        [
            conv_weight,
            conv_bias[None],
            step_bias[None],
            skip_gain[None],
            decay_log,
            step_proj,
            state_proj.T,
        ]
    )
    small = gather_doubling(small, "expert").transpose(1, 0, 2).reshape(-1, channels)
    conv_kernel = small[:taps].astype(f32)
    conv_offset = small[taps].astype(f32)
    step_shift = small[taps + 1 : taps + 2].astype(f32)
    skip_full = small[taps + 2 : taps + 3].astype(f32)
    decay_full = small[taps + 3 : taps + 3 + entries].astype(f32)
    step_full = small[taps + 3 + entries : taps + 3 + entries + rank]
    state_full = small[taps + 3 + entries + rank :]
    weight_x = gather_direct(proj_x.T, "expert").reshape(channels, width)
    proj_z, weight_x = lax.optimization_barrier((proj_z, weight_x))
    weight_z = gather_direct(proj_z.T, "expert").reshape(channels, width)
    out_proj, weight_z = lax.optimization_barrier((out_proj, weight_z))
    out_full = gather_direct(out_proj, "expert").reshape(channels, width)
    codes = jnp.stack([routes[:, 0].astype(f32), valid_float])
    codes = gather_doubling(codes, "expert")

    resid = tokens.astype(f32)
    scale_one = rms_scale(resid)
    unit_one = resid * scale_one
    normed = (unit_one * gain_one[None, :]).astype(bf16)
    inner_x = ein("td,cd->tc", normed, weight_x)
    activity_low = jax.nn.silu(causal_conv(inner_x, segment, conv_kernel, conv_offset)).astype(bf16)
    activity = activity_low.astype(f32)
    projected = hidden_sum_small(ein("tc,kc->tk", activity_low, state_full))
    inner_z = ein("td,cd->tc", normed, weight_z)
    rank_low = projected[:, :rank].astype(bf16)
    in_b = projected[:, rank : rank + entries]
    in_c = projected[:, rank + entries :]
    basis_b = jnp.broadcast_to(in_b[:, :, None], (positions, entries, LANES))
    basis_c = jnp.broadcast_to(in_c[:, :, None], (positions, entries, LANES))
    step_pre = product(rank_low, step_full)
    keep = persist[:, None]
    mixed, scanned, states = scan_forward(
        step_pre, activity, inner_z, basis_b, basis_c, step_shift, decay_full, skip_full, keep
    )
    branch = hidden_sum(product(mixed, out_full))
    hidden_res = resid + branch
    scale_two = rms_scale(hidden_res)
    unit_two = hidden_res * scale_two
    normed_two = (unit_two * gain_two[None, :]).astype(bf16)
    logits = gather_doubling(ein("ed,td->et", router_full, normed_two), "expert")
    gates = sinkhorn(logits, codes)
    gate_values = gates[0, 0]

    prior = (places[:, None] > places[None, :]).astype(bf16)
    slot_ids = jnp.arange(experts * capacity, dtype=f32)

    def pick(some):
        member = (some[:, 0, :, None] == jnp.arange(experts, dtype=f32)) & (some[:, 1, :, None] > 0)
        member = member.astype(bf16)
        slot = jnp.sum(ein("pt,nte->npe", prior, member) * member.astype(f32), axis=2)
        target = jnp.where(some[:, 1] > 0, some[:, 0] * capacity + slot, -1.0)
        return (slot_ids[None, :, None] == target[:, None, :]).astype(bf16)

    group = min(devices, GROUP)
    picker = pick(codes[:group])
    own_picker = picker[0]

    def spread(values):
        return product(own_picker, values).astype(bf16).reshape(experts, capacity, width)

    def collect(values):
        return ein("st,sd->td", own_picker, values.astype(bf16).reshape(-1, width)).astype(bf16)

    sent = spread(normed_two)
    sent_grad = spread(cotangent)
    active, gelu_back = jax.vjp(jax.nn.gelu, ein("erd,edf->erf", sent, expert_up))
    active_low = active.astype(bf16)
    plain_active = ein("erd,efd->erf", sent_grad, expert_down)
    plain_pre = gelu_back(plain_active)[0].astype(bf16)
    gate_slots = jnp.sum(active_low.astype(f32) * plain_active, axis=2).reshape(-1)
    grad_gate = jnp.sum(own_picker.astype(f32) * gate_slots[:, None], axis=0)
    grad_gate = gather_doubling(hidden_sum_small(grad_gate[None]), "expert")
    plain_in = hidden_sum(collect(ein("erf,edf->erd", plain_pre, expert_up)))
    returned = hidden_sum(collect(ein("erf,efd->erd", active_low, expert_down)))
    layer_out = (valid_float[:, None] * (hidden_res + gate_values[:, None] * returned)).astype(bf16)
    grad_expert_in = plain_in * (gate_values * valid_float)[:, None]

    grad_logits = sinkhorn_back(logits, codes, grad_gate).astype(bf16)
    router_grad = ein("td,et->ed", normed_two, grad_logits)
    grad_normed_two = ein("et,ed->td", grad_logits, router_full) + grad_expert_in
    grad_out = cotangent.astype(f32) * valid_float[:, None]
    gain_two_grad = jnp.sum(grad_normed_two * unit_two, axis=0)
    grad_unit_two = grad_normed_two * gain_two[None, :]
    grad_hidden = grad_out + scale_two * (
        grad_unit_two - unit_two * jnp.mean(grad_unit_two * unit_two, axis=-1, keepdims=True)
    )
    grad_branch = grad_hidden.astype(bf16)
    out_grad = ein("tc,td->cd", mixed, grad_branch).reshape(devices, own_channels, width)
    out_grad = scatter_sum(out_grad, "expert")
    grad_mixed = ein("td,cd->tc", grad_branch, out_full)
    (
        grad_act_scan,
        grad_z_low,
        grad_step_low,
        part_b,
        part_c,
        step_bias_grad,
        decay_grad,
        skip_grad,
    ) = scan_backward(
        grad_mixed,
        scanned,
        activity,
        inner_z,
        step_pre,
        step_shift,
        decay_full,
        skip_full,
        keep,
        basis_b,
        basis_c,
        states,
    )
    step_proj_grad = ein("tr,tc->rc", rank_low, grad_step_low)
    grad_rank = ein("tc,rc->tr", grad_step_low, step_full)
    grad_projected = hidden_sum_small(
        jnp.concatenate([grad_rank, jnp.sum(part_b, axis=2), jnp.sum(part_c, axis=2)], axis=1)
    )
    grad_proj_low = grad_projected.astype(bf16)
    state_grad = ein("tc,tk->kc", activity_low, grad_proj_low)
    grad_activity = grad_act_scan + ein("tk,kc->tc", grad_proj_low, state_full)

    def conv_fn(values, kernel, offset):
        return jax.nn.silu(causal_conv(values, segment, kernel, offset))

    _, conv_back = jax.vjp(conv_fn, inner_x, conv_kernel, conv_offset)
    grad_inner_x, conv_weight_grad, conv_bias_grad = conv_back(grad_activity)
    grad_x_low = grad_inner_x.astype(bf16)
    both = jnp.stack([grad_x_low, grad_z_low]).reshape(2, positions, devices, own_channels)
    both = exchange(both.transpose(2, 0, 1, 3), "expert")
    grad_normed = hidden_sum(product(grad_x_low, weight_x) + product(grad_z_low, weight_z))
    gain_one_grad = jnp.sum(grad_normed * unit_one, axis=0)
    grad_unit_one = grad_normed * gain_one[None, :]
    tokens_grad = grad_hidden + scale_one * (
        grad_unit_one - unit_one * jnp.mean(grad_unit_one * unit_one, axis=-1, keepdims=True)
    )

    totals = None
    sources = (normed, normed_two, cotangent)
    for base in range(0, devices, group):
        if base > 0:
            sources, totals = lax.optimization_barrier((sources, totals))
            picker = pick(codes[base : base + group])
        normed_all, rows_all, cotangent_all = [gather_tokens(v, base) for v in sources]
        grad_all = cotangent_all.astype(f32) * gates[base : base + group, 0, :, None]
        parts = expert_grads(
            picker, rows_all, grad_all.astype(bf16), expert_up, expert_down, index, block
        ) + (
            ein("ntd,ntc->dc", normed_all, both[base : base + group, 0]),
            ein("ntd,ntc->dc", normed_all, both[base : base + group, 1]),
        )
        totals = parts if base == 0 else tuple(a + b for a, b in zip(totals, parts))
    up_grad, down_grad, proj_x_grad, proj_z_grad = totals

    vector_grads = jnp.concatenate([gain_one_grad[None], gain_two_grad[None], router_grad])
    vector_grads = vector_grads.reshape(2 + experts, devices, block).transpose(1, 0, 2)
    vector_grads = scatter_sum(jnp.take(vector_grads, order, axis=0), "expert")
    small_grads = jnp.concatenate(
        [
            conv_weight_grad,
            conv_bias_grad[None],
            step_bias_grad,
            skip_grad,
            decay_grad,
            step_proj_grad,
            state_grad,
        ]
    )
    small_grads = small_grads.reshape(-1, devices, own_channels).transpose(1, 0, 2)
    small_grads = scatter_sum(small_grads, "expert")
    return (
        layer_out,
        tokens_grad,
        vector_grads[0],
        proj_x_grad,
        proj_z_grad,
        small_grads[:taps],
        small_grads[taps],
        small_grads[taps + 3 + entries + rank :].T,
        small_grads[taps + 3 + entries : taps + 3 + entries + rank],
        small_grads[taps + 1],
        small_grads[taps + 3 : taps + 3 + entries],
        small_grads[taps + 2],
        out_grad,
        vector_grads[1],
        vector_grads[2:].T,
        up_grad,
        down_grad,
    )


def solution(mesh):
    in_specs = (
        P("expert", None),
        P("expert", None),
        P("expert", None),
        P("expert", None),
        P("expert"),
        P(None, ("expert", "hidden")),
        P(None, ("expert", "hidden")),
        P(None, ("expert", "hidden")),
        P(("expert", "hidden")),
        P(("expert", "hidden"), None),
        P(None, ("expert", "hidden")),
        P(("expert", "hidden")),
        P(None, ("expert", "hidden")),
        P(("expert", "hidden")),
        P(("expert", "hidden"), None),
        P("expert"),
        P("expert", None),
        P(None, None, "hidden"),
        P(None, "hidden", None),
    )
    out_specs = (
        P("expert", None),
        P("expert", None),
        P("expert"),
        P(None, ("expert", "hidden")),
        P(None, ("expert", "hidden")),
        P(None, ("expert", "hidden")),
        P(("expert", "hidden")),
        P(("expert", "hidden"), None),
        P(None, ("expert", "hidden")),
        P(("expert", "hidden")),
        P(None, ("expert", "hidden")),
        P(("expert", "hidden")),
        P(("expert", "hidden"), None),
        P("expert"),
        P("expert", None),
        P(None, "expert", "hidden"),
        P(None, "hidden", "expert"),
    )
    return jax.shard_map(local, mesh=mesh, in_specs=in_specs, out_specs=out_specs, check_vma=False)
```

```python
import jax
import jax.numpy as jnp
from jax import lax
from jax.experimental import pallas as pl
from jax.experimental.pallas import tpu as pltpu
from jax.sharding import PartitionSpec as P

SINK_ITERS = 8
GROUP = 8
LANES = 128
ROWS = 8
FAR = 1e30
LOG2E = 1.4426950408889634
epsilon = 1e-05
f32 = jnp.float32
bf16 = jnp.bfloat16


def product(left, right):
    return jnp.dot(left, right, preferred_element_type=f32)


def ein(spec, left, right):
    return jnp.einsum(spec, left, right, preferred_element_type=f32)


def rms_scale(values):
    return lax.rsqrt(jnp.mean(values * values, axis=-1, keepdims=True) + epsilon)


def swap(values, axis, bits):
    size = lax.axis_size(axis)
    return lax.ppermute(values, axis, [(i, i ^ bits) for i in range(size)])


def gather_direct(values, axis):
    size = lax.axis_size(axis)
    if size > GROUP:
        return lax.all_gather(values, axis)
    place = lax.axis_index(axis)
    whole = jnp.zeros((size,) + values.shape, values.dtype)
    for r in range(size):
        piece = swap(values, axis, r) if r > 0 else values
        whole = lax.dynamic_update_slice(whole, piece[None], (place ^ r,) + (0,) * values.ndim)
    return whole


def gather_small(values, axis):
    size = lax.axis_size(axis)
    copies = jnp.broadcast_to(values[None], (size,) + values.shape)
    return lax.all_to_all(copies, axis, 0, 0, tiled=True)


def scatter_sum(values, axis):
    size = values.shape[0]
    order = jnp.arange(size) ^ lax.axis_index(axis)
    values = jnp.take(values, order, axis=0)
    bits = 1
    while size > 1:
        size //= 2
        pairs = values.reshape((size, 2) + values.shape[1:])
        values = pairs[:, 0] + swap(pairs[:, 1].astype(bf16), axis, bits).astype(f32)
        bits *= 2
    return values[0]


def hidden_sum(values):
    half = values.shape[0] // 2
    place = lax.axis_index("hidden") % 2
    kept = lax.dynamic_slice_in_dim(values, place * half, half, 0)
    given = lax.dynamic_slice_in_dim(values, (1 - place) * half, half, 0)
    total = kept.astype(bf16).astype(f32) + swap(given.astype(bf16), "hidden", 1).astype(f32)
    low = total.astype(bf16)
    low = (low.astype(f32) + swap(low, "hidden", 2).astype(f32)).astype(bf16)
    other = swap(low, "hidden", 1)
    return jnp.where(
        place == 0, jnp.concatenate([low, other]), jnp.concatenate([other, low])
    ).astype(f32)


def hidden_sum_small(values):
    return jnp.sum(lax.all_gather(values, "hidden"), axis=0)


def causal_conv(values, segment, kernel, offset):
    taps = kernel.shape[0]
    length = values.shape[0]
    result = offset[None, :] + kernel[taps - 1][None, :] * values
    for delay in range(1, taps):
        moved = jnp.concatenate(
            [jnp.zeros((delay, values.shape[1]), values.dtype), values[: length - delay]], axis=0
        )
        moved_seg = jnp.concatenate([jnp.full((delay,), -1, jnp.int32), segment[: length - delay]])
        same = (moved_seg == segment).astype(values.dtype)
        result = result + kernel[taps - 1 - delay][None, :] * moved * same[:, None]
    return result


def softplus(values):
    return jnp.maximum(values, 0.0) + jnp.log1p(jnp.exp(-jnp.abs(values)))


def sigmoid(values):
    return 1.0 / (1.0 + jnp.exp(-values))


def put(ref, values):
    width = values.shape[1]
    ref[:, :width] = values
    if ref.shape[1] > width:
        ref[:, width:] = jnp.zeros((values.shape[0], ref.shape[1] - width), ref.dtype)


def widen(tile, width):
    return jnp.concatenate([tile] * (width // LANES), axis=1)


def fold(values):
    total = values[:, :LANES]
    for k in range(1, values.shape[1] // LANES):
        total = total + values[:, k * LANES : (k + 1) * LANES]
    return total


def scan_forward_body(
    pre, act, gate, basis_b, basis_c, bias, decay, skip, keep,
    mixed, out, states, far_steps, inputs, rates, sums,
):
    width = far_steps.shape[1]
    channels = pre.shape[1]
    step = softplus(pre[...] + bias[...])
    put(far_steps, jnp.where(keep[...] > 0, step, FAR))
    put(inputs, step * act[...])
    put(rates, -LOG2E * jnp.exp(decay[...]))
    rate = rates[...]

    def block(i, memory):
        base = pl.multiple_of(i * ROWS, ROWS)
        step_rows = far_steps[pl.ds(base, ROWS), :]
        input_rows = inputs[pl.ds(base, ROWS), :]
        rows = []
        for j in range(ROWS):
            factor = jnp.exp2(step_rows[j : j + 1] * rate)
            memory = factor * memory + input_rows[j : j + 1] * widen(basis_b[base + j], width)
            states[base + j] = memory
            rows.append(jnp.sum(widen(basis_c[base + j], width) * memory, axis=0, keepdims=True))
        sums[pl.ds(base, ROWS), :] = jnp.concatenate(rows, axis=0)
        return memory

    lax.fori_loop(0, pre.shape[0] // ROWS, block, jnp.zeros(rate.shape, f32))
    total = sums[:, :channels]
    out[...] = total
    silu = gate[...] * sigmoid(gate[...])
    mixed[...] = ((total + skip[...] * act[...]) * silu).astype(bf16)


def scan_backward_body(
    grad, out, act, gate, pre, bias, decay, skip, keep, basis_b, basis_c, states,
    grad_act, grad_gate, grad_pre, part_b, part_c, grad_bias, grad_decay, grad_skip,
    far_steps, steps, inputs, outer, rates, sum_input, sum_step,
):
    width = far_steps.shape[1]
    channels = pre.shape[1]
    step = softplus(pre[...] + bias[...])
    put(far_steps, jnp.where(keep[...] > 0, step, FAR))
    put(steps, step)
    put(inputs, step * act[...])
    put(rates, -jnp.exp(decay[...]))
    shade = sigmoid(gate[...])
    through = grad[...] * gate[...] * shade
    put(outer, through)
    grad_gate[...] = (
        grad[...]
        * (out[...] + skip[...] * act[...])
        * (shade * (1.0 + gate[...] * (1.0 - shade)))
    ).astype(bf16)
    grad_skip[...] = jnp.sum(through * act[...], axis=0, keepdims=True)
    rate = rates[...]
    quick = rate * LOG2E
    blocks = pre.shape[0] // ROWS

    def block(i, carried):
        later, rate_sum = carried
        base = pl.multiple_of((blocks - 1 - i) * ROWS, ROWS)
        far_rows = far_steps[pl.ds(base, ROWS), :]
        step_rows = steps[pl.ds(base, ROWS), :]
        input_rows = inputs[pl.ds(base, ROWS), :]
        outer_rows = outer[pl.ds(base, ROWS), :]
        input_sums = [None] * ROWS
        step_sums = [None] * ROWS
        for j in reversed(range(ROWS)):
            tile_b = widen(basis_b[base + j], width)
            outside = outer_rows[j : j + 1]
            inside = input_rows[j : j + 1]
            state = states[base + j]
            flow = widen(basis_c[base + j], width) * outside + later
            later = jnp.exp2(far_rows[j : j + 1] * quick) * flow
            part_c[base + j] = fold(outside * state)
            part_b[base + j] = fold(flow * inside)
            input_sums[j] = jnp.sum(flow * tile_b, axis=0, keepdims=True)
            turned = flow * (state - inside * tile_b)
            step_sums[j] = jnp.sum(turned * rate, axis=0, keepdims=True)
            rate_sum = rate_sum + turned * step_rows[j : j + 1]
        sum_input[pl.ds(base, ROWS), :] = jnp.concatenate(input_sums, axis=0)
        sum_step[pl.ds(base, ROWS), :] = jnp.concatenate(step_sums, axis=0)
        return later, rate_sum

    zero = jnp.zeros(rate.shape, f32)
    _, rate_sum = lax.fori_loop(0, blocks, block, (zero, zero))
    grad_decay[...] = (rate_sum * rate)[:, :channels]
    back_input = sum_input[:, :channels]
    grad_act[...] = outer[:, :channels] * skip[...] + back_input * step
    grad_step = (back_input * act[...] + sum_step[:, :channels]) * sigmoid(pre[...] + bias[...])
    grad_pre[...] = grad_step.astype(bf16)
    grad_bias[...] = jnp.sum(grad_step, axis=0, keepdims=True)


def shape_of(*dims):
    return jax.ShapeDtypeStruct(dims, f32)


def scan_forward(pre, act, gate, basis_b, basis_c, bias, decay, skip, keep):
    positions, channels = pre.shape
    entries = decay.shape[0]
    width = -(-channels // LANES) * LANES
    return pl.pallas_call(
        scan_forward_body,
        out_shape=(
            jax.ShapeDtypeStruct((positions, channels), bf16),
            shape_of(positions, channels),
            shape_of(positions, entries, width),
        ),
        scratch_shapes=[
            pltpu.VMEM((positions, width), f32),
            pltpu.VMEM((positions, width), f32),
            pltpu.VMEM((entries, width), f32),
            pltpu.VMEM((positions, width), f32),
        ],
        compiler_params=pltpu.CompilerParams(vmem_limit_bytes=48 * 2**20),
        name="scan_forward",
    )(pre, act, gate, basis_b, basis_c, bias, decay, skip, keep)


def scan_backward(
    grad, out, act, gate, pre, bias, decay, skip, keep, basis_b, basis_c, states
):
    positions, channels = pre.shape
    entries, width = states.shape[1:]
    wide = pltpu.VMEM((positions, width), f32)
    return pl.pallas_call(
        scan_backward_body,
        out_shape=(
            shape_of(positions, channels),
            jax.ShapeDtypeStruct((positions, channels), bf16),
            jax.ShapeDtypeStruct((positions, channels), bf16),
            shape_of(positions, entries, LANES),
            shape_of(positions, entries, LANES),
            shape_of(1, channels),
            shape_of(entries, channels),
            shape_of(1, channels),
        ),
        scratch_shapes=[wide, wide, wide, wide, pltpu.VMEM((entries, width), f32), wide, wide],
        compiler_params=pltpu.CompilerParams(vmem_limit_bytes=56 * 2**20),
        name="scan_backward",
    )(grad, out, act, gate, pre, bias, decay, skip, keep, basis_b, basis_c, states)


def sinkhorn_body(place, packed, gates, grad_logits, all_grads):
    experts = grad_logits.shape[0]
    start = jnp.exp(packed[:, 0, :experts, :])
    codes = packed[:, 0, experts : experts + 1, :]
    grad_gates = jnp.sum(packed[:, :, experts + 1 : experts + 2, :], axis=1)
    valid = (codes >= 0).astype(f32)
    onehot = (lax.broadcasted_iota(jnp.int32, start.shape, 1).astype(f32) == codes).astype(f32)
    weights = start
    history = []
    for _ in range(SINK_ITERS):
        columns = jnp.sum(jnp.sum(weights * valid, axis=2, keepdims=True), axis=0, keepdims=True)
        scaled = weights / columns
        row_sums = jnp.sum(scaled, axis=1, keepdims=True)
        weights = scaled / row_sums
        history.append((columns, scaled, row_sums, weights))
    gates[...] = experts * jnp.sum(weights * onehot, axis=1, keepdims=True)
    grads = experts * grad_gates * onehot
    for columns, scaled, row_sums, result in reversed(history):
        grads = (grads - jnp.sum(grads * result, axis=1, keepdims=True)) / row_sums
        term = jnp.sum(jnp.sum(grads * scaled, axis=2, keepdims=True), axis=0, keepdims=True)
        grads = (grads - valid * term) / columns
    all_grads[...] = grads * start
    grad_logits[...] = all_grads[place[0]]


def sinkhorn(place, packed, experts):
    count, _, _, positions = packed.shape
    return pl.pallas_call(
        sinkhorn_body,
        in_specs=[pl.BlockSpec(memory_space=pltpu.SMEM), pl.BlockSpec(memory_space=pltpu.VMEM)],
        out_shape=(shape_of(count, 1, positions), shape_of(experts, positions)),
        scratch_shapes=[pltpu.VMEM((count, experts, positions), f32)],
        compiler_params=pltpu.CompilerParams(vmem_limit_bytes=48 * 2**20),
        name="sinkhorn",
    )(place, packed)


def dot(left, right, left_dim=1, right_dim=0):
    return lax.dot_general(
        left, right, (((left_dim,), (right_dim,)), ((), ())), preferred_element_type=f32
    )


def slots_of(codes, experts, capacity):
    positions = codes.shape[1]
    member = lax.broadcasted_iota(jnp.int32, (experts, positions), 0).astype(f32) == codes
    member = member.astype(bf16)
    shape = (positions, positions)
    prior = lax.broadcasted_iota(jnp.int32, shape, 0) < lax.broadcasted_iota(jnp.int32, shape, 1)
    before = dot(member, prior.astype(f32).astype(bf16))
    rank = jnp.sum(before * member.astype(f32), axis=0, keepdims=True)
    return jnp.where(codes >= 0, codes * capacity + rank, -1.0)


def picks(slots, first, count):
    shape = (count, slots.shape[1])
    return (lax.broadcasted_iota(jnp.int32, shape, 0) + first).astype(f32) == slots


def gelu_pair(values):
    root = 0.7978845608028654
    square = values * values
    bent = jnp.tanh(root * values * (1.0 + 0.044715 * square))
    half = 0.5 * (1.0 + bent)
    slope = half + 0.5 * values * (1.0 - bent * bent) * root * (1.0 + 3 * 0.044715 * square)
    return values * half, slope


def experts_body(codes, rows, grads, up, down, out, back, gate_sum, slots, outs, backs):
    step = pl.program_id(0)
    experts = pl.num_programs(0)
    capacity = outs.shape[0] // experts

    @pl.when(step == 0)
    def _():
        slots[...] = slots_of(codes[...], experts, capacity)
        gate_sum[...] = jnp.zeros_like(gate_sum)

    first = pl.multiple_of(step * capacity, capacity)
    chosen = picks(slots[...], first, capacity).astype(f32)
    pick = chosen.astype(bf16)
    sent = dot(pick, rows[...]).astype(bf16)
    sent_grad = dot(pick, grads[...]).astype(bf16)
    active, slope = gelu_pair(dot(sent, up[0]))
    plain = dot(sent_grad, down[0], 1, 1)
    low = active.astype(bf16)
    gate_slots = jnp.sum(low.astype(f32) * plain, axis=1, keepdims=True)
    gate_sum[...] += jnp.sum(chosen * gate_slots, axis=0, keepdims=True)
    outs[pl.ds(first, capacity), :] = dot(low, down[0]).astype(bf16)
    backs[pl.ds(first, capacity), :] = dot((plain * slope).astype(bf16), up[0], 1, 1).astype(bf16)

    @pl.when(step == experts - 1)
    def _():
        every = picks(slots[...], 0, outs.shape[0]).astype(f32).astype(bf16)
        out[...] = dot(every, outs[...], 0, 0).astype(bf16)
        back[...] = dot(every, backs[...], 0, 0).astype(bf16)


def whole(shape):
    return pl.BlockSpec(shape, lambda i: (0,) * len(shape), pipeline_mode=pl.Buffered(1))


def experts_local(codes, rows, grads, up, down):
    positions, width = rows.shape
    experts, _, hidden = up.shape
    slots = 3 * positions // 2
    low = jax.ShapeDtypeStruct((positions, width), bf16)
    return pl.pallas_call(
        experts_body,
        grid=(experts,),
        in_specs=[
            whole((1, positions)),
            whole((positions, width)),
            whole((positions, width)),
            pl.BlockSpec((1, width, hidden), lambda i: (i, 0, 0)),
            pl.BlockSpec((1, hidden, width), lambda i: (i, 0, 0)),
        ],
        out_specs=(whole((positions, width)), whole((positions, width)), whole((1, positions))),
        out_shape=(low, low, shape_of(1, positions)),
        scratch_shapes=[
            pltpu.VMEM((1, positions), f32),
            pltpu.VMEM((slots, width), bf16),
            pltpu.VMEM((slots, width), bf16),
        ],
        compiler_params=pltpu.CompilerParams(vmem_limit_bytes=40 * 2**20),
        name="experts_local",
    )(codes, rows, grads, up, down)


def expert_grads_body(
    codes, gates, rows, grads, own_rows, own_grads, up, down, up_grad, down_grad,
    sent, sent_grads, own_sent, own_sent_grads,
):
    step = pl.program_id(0)
    experts = pl.num_programs(0)
    count, _, positions = codes.shape
    capacity = sent.shape[1] // count

    @pl.when(step == 0)
    def _():
        for r in range(count):
            slots = slots_of(codes[r], experts, capacity)
            chosen = picks(slots, 0, sent.shape[0] * capacity).astype(f32)
            gate = jnp.sum(chosen * gates[r], axis=1, keepdims=True)
            pick = chosen.astype(bf16)
            part = pl.ds(r * positions, positions)
            place = pl.ds(r * capacity, capacity)
            for source, target, scale in (
                (rows, sent, None),
                (own_rows, own_sent, None),
                (grads, sent_grads, gate),
                (own_grads, own_sent_grads, gate),
            ):
                moved = dot(pick, source[part, :])
                moved = (moved if scale is None else moved * scale).astype(bf16)
                for i in range(sent.shape[0]):
                    target[i, place, :] = moved[i * capacity : (i + 1) * capacity]

    active, slope = gelu_pair(dot(sent[step], up[0]))
    grad_pre = (dot(sent_grads[step], down[0], 1, 1) * slope).astype(bf16)
    up_grad[0] = dot(own_sent[step], grad_pre, 0, 0)
    down_grad[0] = dot(active.astype(bf16), own_sent_grads[step], 0, 0)


def expert_grads(codes, gates, rows, grads, own_rows, own_grads, up, down):
    count, _, positions = codes.shape
    total, width = rows.shape
    block = own_rows.shape[1]
    experts, _, hidden = up.shape
    slots = count * (3 * positions // (2 * experts))
    return pl.pallas_call(
        expert_grads_body,
        grid=(experts,),
        in_specs=[
            whole((count, 1, positions)),
            whole((count, 1, positions)),
            whole((total, width)),
            whole((total, width)),
            whole((total, block)),
            whole((total, block)),
            pl.BlockSpec((1, width, hidden), lambda i: (i, 0, 0)),
            pl.BlockSpec((1, hidden, width), lambda i: (i, 0, 0)),
        ],
        out_specs=(
            pl.BlockSpec((1, block, hidden), lambda i: (i, 0, 0)),
            pl.BlockSpec((1, hidden, block), lambda i: (i, 0, 0)),
        ),
        out_shape=(shape_of(experts, block, hidden), shape_of(experts, hidden, block)),
        scratch_shapes=[
            pltpu.VMEM((experts, slots, width), bf16),
            pltpu.VMEM((experts, slots, width), bf16),
            pltpu.VMEM((experts, slots, block), bf16),
            pltpu.VMEM((experts, slots, block), bf16),
        ],
        compiler_params=pltpu.CompilerParams(vmem_limit_bytes=58 * 2**20),
        name="expert_grads",
    )(codes, gates, rows, grads, own_rows, own_grads, up, down)


def local(
    tokens,
    cotangent,
    seq_lengths,
    routes,
    mixer_gain,
    proj_x,
    proj_z,
    conv_weight,
    conv_bias,
    state_proj,
    step_proj,
    step_bias,
    decay_log,
    skip_gain,
    out_proj,
    moe_gain,
    router,
    expert_up,
    expert_down,
):
    devices = lax.axis_size("expert")
    hidden = lax.axis_size("hidden")
    index = lax.axis_index("expert")
    positions, width = tokens.shape
    block = mixer_gain.shape[0]
    experts = expert_up.shape[0]
    own_channels = proj_x.shape[1]
    channels = devices * own_channels
    rank = step_proj.shape[0]
    entries = decay_log.shape[0]
    taps = conv_weight.shape[0]

    places = jnp.arange(positions, dtype=jnp.int32)
    first = seq_lengths[0, 0]
    ending = first + seq_lengths[0, 1]
    segment = (places >= first).astype(jnp.int32) + (places >= ending).astype(jnp.int32)
    valid = places < ending
    valid_float = valid.astype(f32)
    earlier = jnp.concatenate([jnp.full((1,), -1, jnp.int32), segment[:-1]])
    persist = (segment == earlier).astype(f32)
    codes = jnp.where(valid, routes[:, 0].astype(f32), -1.0)[None]

    weight_x = gather_direct(proj_x.T, "expert").reshape(channels, width)
    later = lax.all_gather(jnp.concatenate([proj_z.T, out_proj]), "expert")
    weight_z = later[:, :own_channels].reshape(channels, width)
    out_full = later[:, own_channels:].reshape(channels, width)
    vectors = jnp.concatenate([mixer_gain[None], moe_gain[None], router.T])
    small = [
        conv_weight,
        conv_bias[None],
        step_bias[None],
        skip_gain[None],
        decay_log,
        step_proj,
        state_proj.T,
    ]
    count = sum(piece.shape[0] for piece in small)
    spare = -(-vectors.size // own_channels) * own_channels - vectors.size
    small.append(jnp.pad(vectors.reshape(-1), (0, spare)).reshape(-1, own_channels))
    small = gather_small(jnp.concatenate(small), "expert")
    vectors = small[:, count:].reshape(devices, -1)[:, : vectors.size]
    vectors = vectors.reshape(devices, -1, block).transpose(1, 0, 2).reshape(-1, width)
    gain_one = vectors[0].astype(f32)
    gain_two = vectors[1].astype(f32)
    router_full = vectors[2:]
    small = small[:, :count].transpose(1, 0, 2).reshape(count, channels)
    conv_kernel = small[:taps].astype(f32)
    conv_offset = small[taps].astype(f32)
    step_shift = small[taps + 1 : taps + 2].astype(f32)
    skip_full = small[taps + 2 : taps + 3].astype(f32)
    decay_full = small[taps + 3 : taps + 3 + entries].astype(f32)
    step_full = small[taps + 3 + entries : taps + 3 + entries + rank]
    state_full = small[taps + 3 + entries + rank :]

    resid = tokens.astype(f32)
    scale_one = rms_scale(resid)
    unit_one = resid * scale_one
    normed = (unit_one * gain_one[None, :]).astype(bf16)
    inner_x = ein("td,cd->tc", normed, weight_x)
    activity_low = jax.nn.silu(causal_conv(inner_x, segment, conv_kernel, conv_offset)).astype(bf16)
    activity = activity_low.astype(f32)
    projected = hidden_sum_small(ein("tc,kc->tk", activity_low, state_full))
    inner_z = ein("td,cd->tc", normed, weight_z)
    rank_low = projected[:, :rank].astype(bf16)
    in_b = projected[:, rank : rank + entries]
    in_c = projected[:, rank + entries :]
    basis_b = jnp.broadcast_to(in_b[:, :, None], (positions, entries, LANES))
    basis_c = jnp.broadcast_to(in_c[:, :, None], (positions, entries, LANES))
    step_pre = product(rank_low, step_full)
    keep = persist[:, None]
    mixed, scanned, states = scan_forward(
        step_pre, activity, inner_z, basis_b, basis_c, step_shift, decay_full, skip_full, keep
    )
    branch = hidden_sum(product(mixed, out_full))
    hidden_res = resid + branch
    scale_two = rms_scale(hidden_res)
    unit_two = hidden_res * scale_two
    normed_two = (unit_two * gain_two[None, :]).astype(bf16)

    rows = jnp.concatenate([normed, cotangent, normed_two], axis=1)
    quarter = positions // hidden
    rows = lax.dynamic_slice_in_dim(rows, lax.axis_index("hidden") * quarter, quarter, 0)
    rows = lax.all_gather(rows, ("expert", "hidden"), tiled=True)

    logits = ein("ed,td->et", router_full, normed_two)
    out_part, back_part, gate_part = experts_local(
        codes, normed_two, cotangent, expert_up, expert_down
    )
    packed = jnp.concatenate(
        [logits, codes, gate_part, jnp.zeros((ROWS - 2, positions), f32)]
    )
    packed = gather_small(packed, ("expert", "hidden"))
    packed = packed.reshape((devices, hidden) + packed.shape[1:])
    plain_in = hidden_sum(back_part)
    returned = hidden_sum(out_part)
    gates, grad_logits = sinkhorn(index[None], packed, experts)
    gate_values = lax.dynamic_index_in_dim(gates, index, 0, keepdims=False)[0]
    layer_out = (valid_float[:, None] * (hidden_res + gate_values[:, None] * returned)).astype(bf16)
    grad_expert_in = plain_in * (gate_values * valid_float)[:, None]

    grad_logits = grad_logits.astype(bf16)
    router_grad = ein("td,et->ed", normed_two, grad_logits)
    grad_normed_two = ein("et,ed->td", grad_logits, router_full) + grad_expert_in
    grad_out = cotangent.astype(f32) * valid_float[:, None]
    gain_two_grad = jnp.sum(grad_normed_two * unit_two, axis=0)
    grad_unit_two = grad_normed_two * gain_two[None, :]
    grad_hidden = grad_out + scale_two * (
        grad_unit_two - unit_two * jnp.mean(grad_unit_two * unit_two, axis=-1, keepdims=True)
    )
    grad_branch = grad_hidden.astype(bf16)
    grad_mixed = ein("td,cd->tc", grad_branch, out_full)
    out_grad = ein("tc,td->cd", mixed, grad_branch).reshape(devices, own_channels, width)
    out_grad = scatter_sum(out_grad, "expert")
    (
        grad_act_scan,
        grad_z_low,
        grad_step_low,
        part_b,
        part_c,
        step_bias_grad,
        decay_grad,
        skip_grad,
    ) = scan_backward(
        grad_mixed,
        scanned,
        activity,
        inner_z,
        step_pre,
        step_shift,
        decay_full,
        skip_full,
        keep,
        basis_b,
        basis_c,
        states,
    )

    def cut(values):
        return values.astype(bf16).reshape(-1, devices, own_channels).transpose(1, 0, 2)

    step_proj_grad = ein("tr,tc->rc", rank_low, grad_step_low)
    grad_rank = ein("tc,rc->tr", grad_step_low, step_full)
    grad_projected = hidden_sum_small(
        jnp.concatenate([grad_rank, jnp.sum(part_b, axis=2), jnp.sum(part_c, axis=2)], axis=1)
    )
    grad_proj_low = grad_projected.astype(bf16)
    vector_grads = jnp.concatenate([gain_two_grad[None], router_grad]).astype(bf16)
    vector_grads = vector_grads.reshape(-1, devices, block).transpose(1, 0, 2)
    shared = [
        cut(jnp.concatenate([grad_z_low, step_bias_grad.astype(bf16)])),
        cut(jnp.concatenate([skip_grad, decay_grad, step_proj_grad])),
        vector_grads.reshape(devices, -1, own_channels),
    ]
    early = lax.all_to_all(jnp.concatenate(shared, axis=1), "expert", 0, 0, tiled=True)

    state_grad = ein("tc,tk->kc", activity_low, grad_proj_low)
    grad_activity = grad_act_scan + ein("tk,kc->tc", grad_proj_low, state_full)

    def conv_fn(values, kernel, offset):
        return jax.nn.silu(causal_conv(values, segment, kernel, offset))

    _, conv_back = jax.vjp(conv_fn, inner_x, conv_kernel, conv_offset)
    grad_inner_x, conv_weight_grad, conv_bias_grad = conv_back(grad_activity)
    grad_x_low = grad_inner_x.astype(bf16)
    grad_normed_part = product(grad_x_low, weight_x) + product(grad_z_low, weight_z)
    gain_one_part = jnp.sum(grad_normed_part * unit_one, axis=0).astype(bf16)
    shared = [
        cut(grad_x_low),
        cut(jnp.concatenate([conv_weight_grad, conv_bias_grad[None], state_grad])),
        gain_one_part.reshape(devices, -1, own_channels),
    ]
    late = lax.all_to_all(jnp.concatenate(shared, axis=1), "expert", 0, 0, tiled=True)
    grad_normed = hidden_sum(grad_normed_part)
    grad_unit_one = grad_normed * gain_one[None, :]
    tokens_grad = grad_hidden + scale_one * (
        grad_unit_one - unit_one * jnp.mean(grad_unit_one * unit_one, axis=-1, keepdims=True)
    )

    early_sum = jnp.sum(early[:, positions:].astype(f32), axis=0)
    late_sum = jnp.sum(late[:, positions:].astype(f32), axis=0)
    vector_grads = early_sum[2 + entries + rank :].reshape(-1, block)
    gain_one_grad = hidden_sum_small(late_sum[taps + 1 + state_full.shape[0] :]).reshape(-1)
    inner_all = [part[:, :positions].reshape(-1, own_channels) for part in (late, early)]
    normed_all = rows[:, :width]
    proj_x_grad = ein("td,tc->dc", normed_all, inner_all[0])
    proj_z_grad = ein("td,tc->dc", normed_all, inner_all[1])

    def add_group(start):
        size = group * positions
        grads_all = lax.dynamic_slice(rows, (start * positions, width), (size, width))
        rows_all = lax.dynamic_slice(rows, (start * positions, 2 * width), (size, width))
        own = index * block
        return expert_grads(
            lax.dynamic_slice_in_dim(packed[:, 0, experts : experts + 1], start, group, 0),
            lax.dynamic_slice_in_dim(gates, start, group, 0),
            rows_all,
            grads_all,
            lax.dynamic_slice_in_dim(rows_all, own, block, 1),
            lax.dynamic_slice_in_dim(grads_all, own, block, 1),
            expert_up,
            expert_down,
        )

    group = min(devices, GROUP)
    if group == devices:
        up_grad, down_grad = add_group(0)
    else:

        def add(total, start):
            part = add_group(start)
            return (total[0] + part[0], total[1] + part[1]), None

        zero = (
            jnp.zeros((experts, block, expert_up.shape[2]), f32),
            jnp.zeros((experts, expert_down.shape[1], block), f32),
        )
        (up_grad, down_grad), _ = lax.scan(add, zero, jnp.arange(0, devices, group))

    return (
        layer_out,
        tokens_grad,
        gain_one_grad,
        proj_x_grad,
        proj_z_grad,
        late_sum[:taps],
        late_sum[taps],
        late_sum[taps + 1 : taps + 1 + state_full.shape[0]].T,
        early_sum[2 + entries : 2 + entries + rank],
        early_sum[0],
        early_sum[2 : 2 + entries],
        early_sum[1],
        out_grad,
        vector_grads[0],
        vector_grads[1:].T,
        up_grad,
        down_grad,
    )


def solution(mesh):
    in_specs = (
        P("expert", None),
        P("expert", None),
        P("expert", None),
        P("expert", None),
        P("expert"),
        P(None, ("expert", "hidden")),
        P(None, ("expert", "hidden")),
        P(None, ("expert", "hidden")),
        P(("expert", "hidden")),
        P(("expert", "hidden"), None),
        P(None, ("expert", "hidden")),
        P(("expert", "hidden")),
        P(None, ("expert", "hidden")),
        P(("expert", "hidden")),
        P(("expert", "hidden"), None),
        P("expert"),
        P("expert", None),
        P(None, None, "hidden"),
        P(None, "hidden", None),
    )
    out_specs = (
        P("expert", None),
        P("expert", None),
        P("expert"),
        P(None, ("expert", "hidden")),
        P(None, ("expert", "hidden")),
        P(None, ("expert", "hidden")),
        P(("expert", "hidden")),
        P(("expert", "hidden"), None),
        P(None, ("expert", "hidden")),
        P(("expert", "hidden")),
        P(None, ("expert", "hidden")),
        P(("expert", "hidden")),
        P(("expert", "hidden"), None),
        P("expert"),
        P("expert", None),
        P(None, "expert", "hidden"),
        P(None, "hidden", "expert"),
    )
    return jax.shard_map(local, mesh=mesh, in_specs=in_specs, out_specs=out_specs, check_vma=False)
```

```python
import functools

import jax
import jax.numpy as jnp
from jax import lax
from jax.experimental import pallas as pl
from jax.experimental.pallas import tpu as pltpu
from jax.sharding import PartitionSpec as P

SINK_ITERS = 8
GROUP = 8
LANES = 128
ROWS = 8
FAR = 1e30
LOG2E = 1.4426950408889634
epsilon = 1e-05
f32 = jnp.float32
bf16 = jnp.bfloat16


def dot(left, right, left_dim=1, right_dim=0):
    return lax.dot_general(
        left, right, (((left_dim,), (right_dim,)), ((), ())), preferred_element_type=f32
    )


def shape_of(*dims):
    return jax.ShapeDtypeStruct(dims, f32)


def low_of(*dims):
    return jax.ShapeDtypeStruct(dims, bf16)


def call(body, name, out_shape, scratch=(), scalars=0, operands=(), flops=0, limit=56, parts={}, after=0, known=False, **grid):
    if not grid:
        specs = [pl.BlockSpec(memory_space=pltpu.SMEM)] * scalars
        specs += [pl.BlockSpec(memory_space=pltpu.VMEM)] * (len(operands) - scalars)
        grid = {"in_specs": specs}
        if parts:
            specs[scalars:] = [whole(v.shape) for v in operands[scalars:]]
            for at, half in parts.items():
                specs[at] = column_half(operands[at], half)
            if after:
                specs[-after:] = [pl.BlockSpec(memory_space=pl.ANY)] * after
            grid.update(grid=(1,), out_specs=tuple(whole(v.shape) for v in out_shape))
    return pl.pallas_call(
        body,
        out_shape=out_shape,
        scratch_shapes=list(scratch),
        compiler_params=pltpu.CompilerParams(vmem_limit_bytes=limit * 2**20),
        cost_estimate=pl.CostEstimate(flops=flops if known else 0, bytes_accessed=0, transcendentals=0),
        name=name,
        **grid,
    )(*operands)


def whole(shape):
    return pl.BlockSpec(shape, lambda *i: (0,) * len(shape), pipeline_mode=pl.Buffered(1))


def column_half(array, half):
    rows, columns = array.shape
    return pl.BlockSpec(
        (rows, columns // 2), lambda i: (0, half), pipeline_mode=pl.Buffered(1)
    )


def swap(values, axis, bits):
    size = lax.axis_size(axis)
    return lax.ppermute(values, axis, [(i, i ^ bits) for i in range(size)])


def gather_direct(values, axis):
    size = lax.axis_size(axis)
    if size > GROUP:
        return lax.all_gather(values, axis)
    place = lax.axis_index(axis)
    whole = jnp.zeros((size,) + values.shape, values.dtype)
    for r in range(size):
        piece = swap(values, axis, r) if r > 0 else values
        whole = lax.dynamic_update_slice(whole, piece[None], (place ^ r,) + (0,) * values.ndim)
    return whole


def gather_small(values, axis):
    size = lax.axis_size(axis)
    copies = jnp.broadcast_to(values[None], (size,) + values.shape)
    return lax.all_to_all(copies, axis, 0, 0, tiled=True)


def hidden_pieces(piece):
    near = swap(piece, "hidden", 1)
    far = swap(piece, "hidden", 2)
    return piece, near, far, swap(far, "hidden", 1)


def nothing(*refs):
    pass


def after(values, *others):
    anywhere = pl.BlockSpec(memory_space=pl.ANY)
    return pl.pallas_call(
        nothing,
        out_shape=jax.ShapeDtypeStruct(values.shape, values.dtype),
        in_specs=[anywhere] * (1 + len(others)),
        out_specs=anywhere,
        input_output_aliases={0: 0},
        cost_estimate=pl.CostEstimate(flops=0, bytes_accessed=0, transcendentals=0),
        name="after",
    )(values, *others)


def hidden_halves(values):
    half = values.shape[0] // 2
    place = lax.axis_index("hidden") % 2
    kept = lax.dynamic_slice_in_dim(values, place * half, half, 0)
    given = lax.dynamic_slice_in_dim(values, (1 - place) * half, half, 0)
    low = (kept.astype(f32) + swap(given, "hidden", 1).astype(f32)).astype(bf16)
    low = (low.astype(f32) + swap(low, "hidden", 2).astype(f32)).astype(bf16)
    return low, swap(low, "hidden", 1)


def hidden_sum(values):
    low, other = hidden_halves(values)
    place = lax.axis_index("hidden") % 2
    return jnp.where(
        place == 0, jnp.concatenate([low, other]), jnp.concatenate([other, low])
    ).astype(f32)


def softplus(values):
    return jnp.maximum(values, 0.0) + jnp.log1p(jnp.exp(-jnp.abs(values)))


def sigmoid(values):
    return 1.0 / (1.0 + jnp.exp(-values))


def rms_scale(values):
    return lax.rsqrt(jnp.mean(values * values, axis=-1, keepdims=True) + epsilon)


def put(ref, values):
    width = values.shape[1]
    ref[:, :width] = values
    if ref.shape[1] > width:
        ref[:, width:] = jnp.zeros((values.shape[0], ref.shape[1] - width), ref.dtype)


def widen(tile, width):
    return jnp.concatenate([tile] * (width // LANES), axis=1)


def fold(values):
    total = values[:, :LANES]
    for k in range(1, values.shape[1] // LANES):
        total = total + values[:, k * LANES : (k + 1) * LANES]
    return total


def padded(count):
    return -(-count // LANES) * LANES


def same_segment(lengths, positions, delay):
    places = lax.broadcasted_iota(jnp.int32, (positions, 1), 0)
    first = lengths[0, 0]
    ending = first + lengths[0, 1]

    def segment(at):
        return (at >= first).astype(jnp.int32) + (at >= ending).astype(jnp.int32)

    same = (segment(places) == segment(places - delay)) & (places >= delay)
    return same.astype(f32)


def causal_conv(values, shifted, kernel, offset, lengths):
    positions = values.shape[0]
    taps = kernel.shape[0]
    shifted[:ROWS, :] = jnp.zeros((ROWS, values.shape[1]), f32)
    shifted[ROWS : ROWS + positions, :] = values
    result = offset + kernel[taps - 1 : taps] * values
    moved = [values]
    for delay in range(1, taps):
        part = shifted[ROWS - delay : ROWS - delay + positions, :]
        part = part * same_segment(lengths, positions, delay)
        moved.append(part)
        result = result + kernel[taps - 1 - delay : taps - delay] * part
    return result, moved


def column_tile(ref, first, entries, base):
    start = pl.multiple_of(base // LANES * LANES, LANES)
    tile = ref[first : first + entries, pl.ds(start, LANES)]
    return pltpu.roll(tile, lax.rem(LANES - lax.rem(base, LANES), LANES), 1)


def lane(tile, j, width):
    return jnp.broadcast_to(tile[:, j : j + 1], (tile.shape[0], width))


class Sizes:
    def __init__(self, entries, rank, taps, state):
        self.entries, self.rank, self.taps, self.state = entries, rank, taps, state
        self.step = entries
        self.proj = entries + rank
        self.conv = entries + rank + state
        self.rows = self.conv + ROWS
        self.vectors = 2 * ROWS


def mixer_in_body(
    sizes, lengths, places, tokens, cotangent, weight, pack,
    normed, inner, activity, part, small, vectors, share, shifted,
):
    devices, _, own = pack.shape
    for k in range(devices):
        piece = pack[k].astype(f32)
        small[:, k * own : (k + 1) * own] = piece[: sizes.rows]
        for half in range(2):
            at = (2 * k + half) * own
            row = sizes.rows + half * sizes.vectors
            vectors[:, at : at + own] = piece[row : row + sizes.vectors]
    values = tokens[...].astype(f32)
    low = (values * rms_scale(values) * vectors[0:1, :]).astype(bf16)
    normed[...] = low
    half = share.shape[0] // 2
    share[:half, :] = normed[pl.ds(pl.multiple_of(places[1] * half, half), half), :]
    size = half // 2
    for k in range(2):
        at = pl.multiple_of((places[0] ^ (2 * k)) * size, size)
        share[half + k * size : half + (k + 1) * size, :] = cotangent[pl.ds(at, size), :]
    values = dot(low, weight[...], 1, 1)
    inner[...] = values
    kernel = small[sizes.conv : sizes.conv + sizes.taps, :]
    offset = small[sizes.conv + sizes.taps : sizes.conv + sizes.taps + 1, :]
    result, _ = causal_conv(values, shifted, kernel, offset, lengths)
    low = (result * sigmoid(result)).astype(bf16)
    activity[...] = low
    part[...] = dot(low, small[sizes.proj : sizes.conv, :].astype(bf16), 1, 1)


def mixer_in(sizes, lengths, places, tokens, cotangent, weight, pack):
    positions, width = tokens.shape
    channels = weight.shape[0]
    return call(
        functools.partial(mixer_in_body, sizes),
        "mixer_in",
        (
            low_of(positions, width),
            shape_of(positions, channels),
            low_of(positions, channels),
            shape_of(positions, sizes.state),
            shape_of(sizes.rows, channels),
            shape_of(sizes.vectors, width),
            low_of(positions, width),
        ),
        [pltpu.VMEM((positions + 2 * ROWS, channels), f32)],
        2,
        (lengths, places, tokens, cotangent, weight, pack),
        3 * positions * width * channels,
    )


def scan_forward_body(
    sizes, lengths, parts, activity, small, out, states, pre, basis, rank_low,
    far_steps, inputs, rates, sums, wide,
):
    width = far_steps.shape[1]
    positions, channels = activity.shape
    entries, rank = sizes.entries, sizes.rank
    projected = jnp.sum(parts[...], axis=0)
    put(wide, projected)
    basis[...] = wide[...].T
    low = projected[:, :rank].astype(bf16)
    rank_low[...] = low
    values = dot(low, small[sizes.step : sizes.proj, :].astype(bf16))
    pre[...] = values
    at = sizes.conv + sizes.taps + 1
    step = softplus(values + small[at : at + 1, :])
    put(far_steps, jnp.where(same_segment(lengths, positions, 1) > 0, step, FAR))
    put(inputs, step * activity[...].astype(f32))
    put(rates, -LOG2E * jnp.exp(small[:entries, :]))
    rate = rates[...]

    def block(i, memory):
        base = pl.multiple_of(i * ROWS, ROWS)
        step_rows = far_steps[pl.ds(base, ROWS), :]
        input_rows = inputs[pl.ds(base, ROWS), :]
        tile_b = column_tile(basis, rank, entries, base)
        tile_c = column_tile(basis, rank + entries, entries, base)
        rows = []
        for j in range(ROWS):
            factor = jnp.exp2(step_rows[j : j + 1] * rate)
            memory = factor * memory + input_rows[j : j + 1] * lane(tile_b, j, width)
            states[base + j] = memory
            rows.append(jnp.sum(lane(tile_c, j, width) * memory, axis=0, keepdims=True))
        sums[pl.ds(base, ROWS), :] = jnp.concatenate(rows, axis=0)
        return memory

    lax.fori_loop(0, positions // ROWS, block, jnp.zeros(rate.shape, f32))
    out[...] = sums[:, :channels]


def scan_forward(sizes, lengths, parts, activity, small):
    positions, channels = activity.shape
    lanes = padded(channels)
    rows = pltpu.VMEM((positions, lanes), f32)
    state_lanes = padded(sizes.state)
    return call(
        functools.partial(scan_forward_body, sizes),
        "scan_forward",
        (
            shape_of(positions, channels),
            shape_of(positions, sizes.entries, lanes),
            shape_of(positions, channels),
            shape_of(state_lanes, positions),
            low_of(positions, sizes.rank),
        ),
        [rows, rows, pltpu.VMEM((sizes.entries, lanes), f32), rows, pltpu.VMEM((positions, state_lanes), f32)],
        1,
        (lengths, parts, activity, small),
        20 * positions * channels * sizes.entries * 16,
    )


def mixer_out_body(sizes, out, activity, normed, weight_z, weight_out, small, mixed, gate, branch):
    shade = dot(normed[...], weight_z[...], 1, 1)
    gate[...] = shade
    at = sizes.conv + sizes.taps + 2
    values = out[...] + small[at : at + 1, :] * activity[...].astype(f32)
    low = (values * (shade * sigmoid(shade))).astype(bf16)
    mixed[...] = low
    branch[...] = dot(low, weight_out[...]).astype(bf16)


def mixer_out(sizes, out, activity, normed, weights, small):
    positions, channels = activity.shape
    width = normed.shape[1]
    return call(
        functools.partial(mixer_out_body, sizes),
        "mixer_out",
        (low_of(positions, channels), shape_of(positions, channels), low_of(positions, width)),
        operands=(out, activity, normed, weights, weights, small),
        flops=4 * positions * width * channels,
        parts={3: 0, 4: 1},
    )


def slots_of(codes, experts, capacity):
    positions = codes.shape[1]
    member = lax.broadcasted_iota(jnp.int32, (experts, positions), 0).astype(f32) == codes
    member = member.astype(f32)
    shape = (positions, positions)
    prior = lax.broadcasted_iota(jnp.int32, shape, 0) < lax.broadcasted_iota(jnp.int32, shape, 1)
    before = dot(member.astype(bf16), prior.astype(f32).astype(bf16))
    rank = jnp.sum(before * member, axis=0, keepdims=True)
    return jnp.where(codes >= 0, codes * capacity + rank, -1.0)


def picks(slots, first, count):
    shape = (count, slots.shape[1])
    return ((lax.broadcasted_iota(jnp.int32, shape, 0) + first).astype(f32) == slots).astype(f32)


def gelu_pair(values):
    root = 0.7978845608028654
    square = values * values
    bent = jnp.tanh(root * values * (1.0 + 0.044715 * square))
    half = 0.5 * (1.0 + bent)
    slope = half + 0.5 * values * (1.0 - bent * bent) * root * (1.0 + 3 * 0.044715 * square)
    return values * half, slope


def middle_body(
    places, tokens, low, other, vectors, codes, cotangent,
    resid, normed_two, sent, sent_grad, share, logits,
):
    half = low.shape[0]
    experts = logits.shape[0]
    capacity = sent.shape[0] // experts
    resid[pl.ds(pl.multiple_of(places[1] * half, half), half), :] = low[...].astype(f32)
    resid[pl.ds(pl.multiple_of((1 - places[1]) * half, half), half), :] = other[...].astype(f32)
    values = tokens[...].astype(f32) + resid[...]
    resid[...] = values
    rows = (values * rms_scale(values) * vectors[1:2, :]).astype(bf16)
    normed_two[...] = rows
    logits[...] = dot(vectors[2 : 2 + experts, :].astype(bf16), rows, 1, 1)
    every = picks(slots_of(codes[...], experts, capacity), 0, sent.shape[0]).astype(bf16)
    sent[...] = dot(every, rows).astype(bf16)
    sent_grad[...] = dot(every, cotangent[...]).astype(bf16)
    size = share.shape[0] // 2
    for k in range(2):
        at = pl.multiple_of((places[0] ^ (2 * k)) * size, size)
        share[k * size : (k + 1) * size, :] = normed_two[pl.ds(at, size), :]


def middle(places, tokens, low, other, vectors, codes, cotangent, experts):
    positions, width = tokens.shape
    slots = 3 * positions // 2
    return call(
        middle_body,
        "middle",
        (
            shape_of(positions, width),
            low_of(positions, width),
            low_of(slots, width),
            low_of(slots, width),
            low_of(positions // 2, width),
            shape_of(experts, positions),
        ),
        (),
        1,
        (places, tokens, low, other, vectors, codes, cotangent),
        4 * positions * width * slots,
    )


def experts_body(
    codes, logits, rows, grads, up, down, out, back, packed, slots, outs, backs
):
    step = pl.program_id(0)
    experts = pl.num_programs(0)
    capacity = rows.shape[0]
    count = logits.shape[0]

    @pl.when(step == 0)
    def _():
        slots[...] = slots_of(codes[...], experts, capacity)
        packed[:count, :] = logits[...]
        packed[count:, :] = jnp.zeros((packed.shape[0] - count, packed.shape[1]), f32)
        packed[count : count + 1, :] = codes[...]

    first = pl.multiple_of(step * capacity, capacity)
    active, slope = gelu_pair(dot(rows[...], up[0]))
    plain = dot(grads[...], down[0], 1, 1)
    low = active.astype(bf16)
    gate_slots = jnp.sum(low.astype(f32) * plain, axis=1, keepdims=True)
    chosen = picks(slots[...], first, capacity)
    packed[count + 1 : count + 2, :] += jnp.sum(chosen * gate_slots, axis=0, keepdims=True)
    outs[pl.ds(first, capacity), :] = dot(low, down[0]).astype(bf16)
    backs[pl.ds(first, capacity), :] = dot((plain * slope).astype(bf16), up[0], 1, 1).astype(bf16)

    @pl.when(step == experts - 1)
    def _():
        every = picks(slots[...], 0, outs.shape[0]).astype(bf16)
        out[...] = dot(every, outs[...], 0, 0).astype(bf16)
        back[...] = dot(every, backs[...], 0, 0).astype(bf16)


def experts_local(codes, logits, rows, grads, up, down):
    slots, width = rows.shape
    experts, _, hidden = up.shape
    positions = codes.shape[1]
    capacity = slots // experts
    return call(
        experts_body,
        "experts_local",
        (
            low_of(positions, width),
            low_of(positions, width),
            shape_of(2 * ROWS, positions),
        ),
        [
            pltpu.VMEM((1, positions), f32),
            pltpu.VMEM((slots, width), bf16),
            pltpu.VMEM((slots, width), bf16),
        ],
        operands=(codes, logits, rows, grads, up, down),
        flops=8 * slots * width * hidden,
        limit=40,
        grid=(experts,),
        in_specs=[
            whole((1, positions)),
            whole((experts, positions)),
            pl.BlockSpec((capacity, width), lambda i: (i, 0)),
            pl.BlockSpec((capacity, width), lambda i: (i, 0)),
            pl.BlockSpec((1, width, hidden), lambda i: (i, 0, 0)),
            pl.BlockSpec((1, hidden, width), lambda i: (i, 0, 0)),
        ],
        out_specs=(
            whole((positions, width)),
            whole((positions, width)),
            whole((2 * ROWS, positions)),
        ),
    )


def expert_grads_body(
    places, codes, gates, *refs,
):
    rows, grads = refs[:2], refs[2:4]
    up, down, up_grad, down_grad, sent, sent_grad, gate_slots = refs[4:]
    step = pl.program_id(0)
    experts, total, width = sent.shape
    count, _, positions = codes.shape
    capacity = total // count
    block = up_grad.shape[1]
    window = min(padded(block + LANES), width)

    @pl.when(step == 0)
    def _():
        for r in range(count):
            chosen = picks(slots_of(codes[r], experts, capacity), 0, experts * capacity)
            pick = chosen.astype(bf16)
            gate = jnp.sum(chosen * gates[r], axis=1, keepdims=True)
            part = pl.ds(r * capacity, capacity)
            for pieces, target in ((rows, sent), (grads, sent_grad)):
                whole_rows = jnp.concatenate([piece[r] for piece in pieces], axis=0)
                moved = dot(pick, whole_rows).astype(bf16)
                for i in range(experts):
                    target[i, part, :] = moved[i * capacity : (i + 1) * capacity]
            for i in range(experts):
                gate_slots[i, part, :] = jnp.broadcast_to(
                    gate[i * capacity : (i + 1) * capacity], (capacity, LANES)
                )

    gate = gate_slots[step][:, :1]
    active, slope = gelu_pair(dot(sent[step], up[0]))
    plain = dot(sent_grad[step], down[0], 1, 1)
    grad_pre = (plain * slope * gate).astype(bf16)
    scaled = (active * gate).astype(bf16)
    start = jnp.minimum(places[2] * block // LANES * LANES, width - window)
    shift = lax.rem(window - (places[2] * block - start), window)
    own = pl.ds(pl.multiple_of(start, LANES), window)
    up_grad[0] = pltpu.roll(dot(sent[step, :, own], grad_pre, 0, 0), shift, 0)[:block]
    down_grad[0] = pltpu.roll(dot(sent_grad[step, :, own], scaled, 0, 0), shift, 0)[:block]


def expert_grads(places, codes, gates, rows, grads, up, down, block):
    count, _, positions = codes.shape
    experts, width, hidden = up.shape
    slots = count * (3 * positions // (2 * experts))
    shape = (experts, block, hidden)
    out = pl.BlockSpec((1, block, hidden), lambda i: (i, 0, 0))
    half = whole((count, positions // 2, width))
    second = pl.BlockSpec(
        (count, positions // 2, width), lambda i: (0, 1, 0), pipeline_mode=pl.Buffered(1)
    )
    return call(
        expert_grads_body,
        "expert_grads",
        (shape_of(*shape), shape_of(*shape)),
        [
            pltpu.VMEM((experts, slots, width), bf16),
            pltpu.VMEM((experts, slots, width), bf16),
            pltpu.VMEM((experts, slots, LANES), f32),
        ],
        operands=(places, codes, gates, *rows, *grads, up, down),
        flops=12 * experts * slots * width * hidden,
        known=True,
        limit=54,
        grid=(experts,),
        in_specs=[
            pl.BlockSpec(memory_space=pltpu.SMEM),
            whole((count, 1, positions)),
            whole((count, 1, positions)),
            *([half] * 2),
            *([second] * 2),
            pl.BlockSpec((1, width, hidden), lambda i: (i, 0, 0)),
            pl.BlockSpec((1, hidden, width), lambda i: (i, 0, 0)),
        ],
        out_specs=(out, out),
    )


def sinkhorn(packed, experts):
    start = jnp.exp(packed[:, 0, :experts, :])
    codes = packed[:, 0, experts : experts + 1, :]
    grad_gates = jnp.sum(packed[:, :, experts + 1 : experts + 2, :], axis=1)
    valid = (codes >= 0).astype(f32)
    onehot = (lax.broadcasted_iota(jnp.int32, start.shape, 1).astype(f32) == codes).astype(f32)
    weights = start
    history = []
    for _ in range(SINK_ITERS):
        columns = jnp.sum(jnp.sum(weights * valid, axis=2, keepdims=True), axis=0, keepdims=True)
        scaled = weights / columns
        row_sums = jnp.sum(scaled, axis=1, keepdims=True)
        weights = scaled / row_sums
        history.append((columns, scaled, row_sums, weights))
    gates = experts * jnp.sum(weights * onehot, axis=1, keepdims=True)
    grads = experts * grad_gates * onehot
    for columns, scaled, row_sums, result in reversed(history):
        grads = (grads - jnp.sum(grads * result, axis=1, keepdims=True)) / row_sums
        term = jnp.sum(jnp.sum(grads * scaled, axis=2, keepdims=True), axis=0, keepdims=True)
        grads = (grads - valid * term) / columns
    return gates, grads * start


def backward_body(
    sizes, lengths, places, packed, low, other, vectors, resid, normed_two, cotangent, mixed,
    weight_out, out, activity, gate, pre, small, basis, states, rank_low,
    gates, grad_resid, out_grad, grad_act, grad_gate, grad_part, early,
    all_gates, all_grads, branch_grad, far_steps, steps, inputs, outer, rates, sum_input,
    sum_step, sums, shares, square,
):
    positions, width = resid.shape
    channels = activity.shape[1]
    lanes = far_steps.shape[1]
    entries, rank = sizes.entries, sizes.rank
    devices, own, _ = early.shape
    experts = all_grads.shape[1]
    half = low.shape[0]

    every_gate, every_grad = sinkhorn(packed, experts)
    gates[...] = every_gate
    all_gates[...] = every_gate
    all_grads[...] = every_grad
    grad_logits = all_grads[places[2]].astype(bf16)
    square[...] = jnp.broadcast_to(all_gates[places[2]], square.shape)
    gate_column = square[...].T[:, :1]

    branch_grad[pl.ds(pl.multiple_of(places[1] * half, half), half), :] = low[...].astype(f32)
    branch_grad[pl.ds(pl.multiple_of((1 - places[1]) * half, half), half), :] = other[...].astype(f32)
    at = lax.broadcasted_iota(jnp.int32, (positions, 1), 0)
    valid = (at < lengths[0, 0] + lengths[0, 1]).astype(f32)
    grad_two = dot(grad_logits, vectors[2 : 2 + experts, :].astype(bf16), 0, 0)
    grad_two = grad_two + branch_grad[...] * (gate_column * valid)
    values = resid[...]
    scale = rms_scale(values)
    unit = values * scale
    shares[...] = jnp.zeros_like(shares)
    shares[0:1, :] = jnp.sum(grad_two * unit, axis=0, keepdims=True)
    shares[ROWS : ROWS + experts, :] = dot(grad_logits, normed_two[...])
    scaled = grad_two * vectors[1:2, :]
    total = cotangent[...].astype(f32) * valid + scale * (
        scaled - unit * jnp.mean(scaled * unit, axis=-1, keepdims=True)
    )
    grad_resid[...] = total
    branch = total.astype(bf16)
    out_grad[...] = dot(mixed[...], branch, 0, 0).astype(bf16)
    grad = dot(branch, weight_out[...], 1, 1)

    row = sizes.conv + sizes.taps + 1
    shifted = pre[...] + small[row : row + 1, :]
    skip = small[row + 1 : row + 2, :]
    step = softplus(shifted)
    act = activity[...].astype(f32)
    put(far_steps, jnp.where(same_segment(lengths, positions, 1) > 0, step, FAR))
    put(steps, step)
    put(inputs, step * act)
    put(rates, -jnp.exp(small[:entries, :]))
    level = gate[...]
    shade = sigmoid(level)
    through = grad * level * shade
    put(outer, through)
    grad_level = grad * (out[...] + skip * act) * (shade * (1.0 + level * (1.0 - shade)))
    grad_gate[...] = grad_level.astype(bf16)
    put(sum_input, grad_level)
    turned = sum_input[...].T
    for k in range(devices):
        early[k, :, :positions] = turned[k * own : (k + 1) * own].astype(bf16)
    sums[...] = jnp.zeros_like(sums)
    skip_row = entries + rank + 1
    sums[skip_row : skip_row + 1, :channels] = jnp.sum(through * act, axis=0, keepdims=True)
    rate = rates[...]
    quick = rate * LOG2E
    blocks = positions // ROWS
    grad_part[...] = jnp.zeros_like(grad_part)
    lane_ids = lax.broadcasted_iota(jnp.int32, (entries, LANES), 1)

    def block(i, carried):
        later, rate_sum = carried
        base = pl.multiple_of((blocks - 1 - i) * ROWS, ROWS)
        far_rows = far_steps[pl.ds(base, ROWS), :]
        step_rows = steps[pl.ds(base, ROWS), :]
        input_rows = inputs[pl.ds(base, ROWS), :]
        outer_rows = outer[pl.ds(base, ROWS), :]
        columns_b = column_tile(basis, rank, entries, base)
        columns_c = column_tile(basis, rank + entries, entries, base)
        input_sums = [None] * ROWS
        step_sums = [None] * ROWS
        found_b = jnp.zeros((entries, LANES), f32)
        found_c = jnp.zeros((entries, LANES), f32)
        for j in reversed(range(ROWS)):
            tile_b = lane(columns_b, j, lanes)
            outside = outer_rows[j : j + 1]
            inside = input_rows[j : j + 1]
            state = states[base + j]
            flow = lane(columns_c, j, lanes) * outside + later
            later = jnp.exp2(far_rows[j : j + 1] * quick) * flow
            in_b = jnp.sum(fold(flow * inside), axis=1, keepdims=True)
            in_c = jnp.sum(fold(outside * state), axis=1, keepdims=True)
            found_b = jnp.where(lane_ids == j, in_b, found_b)
            found_c = jnp.where(lane_ids == j, in_c, found_c)
            input_sums[j] = jnp.sum(flow * tile_b, axis=0, keepdims=True)
            change = flow * (state - inside * tile_b)
            step_sums[j] = jnp.sum(change * rate, axis=0, keepdims=True)
            rate_sum = rate_sum + change * step_rows[j : j + 1]
        sum_input[pl.ds(base, ROWS), :] = jnp.concatenate(input_sums, axis=0)
        sum_step[pl.ds(base, ROWS), :] = jnp.concatenate(step_sums, axis=0)
        start = pl.multiple_of(base // LANES * LANES, LANES)
        shift = lax.rem(base, LANES)
        for first, found in ((0, found_b), (entries, found_c)):
            basis_grad = square.at[first : first + entries, pl.ds(start, LANES)]
            basis_grad[...] += pltpu.roll(found, shift, 1)
        return later, rate_sum

    square[...] = jnp.zeros_like(square)
    zero = jnp.zeros(rate.shape, f32)
    _, rate_sum = lax.fori_loop(0, blocks, block, (zero, zero))
    sums[:entries, :] = rate_sum * rate
    back_input = sum_input[:, :channels]
    grad_act[...] = outer[:, :channels] * skip + back_input * step
    grad_step = (back_input * act + sum_step[:, :channels]) * sigmoid(shifted)
    grad_low = grad_step.astype(bf16)
    sums[entries + rank : entries + rank + 1, :channels] = jnp.sum(grad_step, axis=0, keepdims=True)
    sums[entries : entries + rank, :channels] = dot(rank_low[...], grad_low, 0, 0)
    grad_part[:, :rank] = dot(grad_low, small[sizes.step : sizes.proj, :].astype(bf16), 1, 1)
    grad_part[:, rank : rank + 2 * entries] = square[...].T[:, : 2 * entries]
    turned = sums[...].T
    spread = shares[...].T
    side = padded(sizes.vectors) - 2 * sizes.vectors
    for k in range(devices):
        early[k, :, positions : positions + side] = turned[k * own : (k + 1) * own, :side].astype(bf16)
        for piece in range(2):
            to = positions + side + piece * sizes.vectors
            source = (2 * k + piece) * own
            early[k, :, to : to + sizes.vectors] = spread[source : source + own].astype(bf16)


def backward(sizes, operands, experts, devices):
    (_, _, packed, _, _, _, resid, _, _, mixed, _, _, activity) = operands[:13]
    positions, width = resid.shape
    channels = activity.shape[1]
    lanes = padded(channels)
    rows = pltpu.VMEM((positions, lanes), f32)
    return call(
        functools.partial(backward_body, sizes),
        "backward",
        (
            shape_of(devices, 1, positions),
            shape_of(positions, width),
            low_of(channels, width),
            shape_of(positions, channels),
            low_of(positions, channels),
            shape_of(positions, padded(sizes.state)),
            low_of(devices, channels // devices, positions + LANES),
        ),
        [
            pltpu.VMEM((devices, 1, positions), f32),
            pltpu.VMEM((devices, experts, positions), f32),
            pltpu.VMEM((positions, width), f32),
            rows,
            rows,
            rows,
            rows,
            pltpu.VMEM((sizes.entries, lanes), f32),
            rows,
            rows,
            pltpu.VMEM((LANES, lanes), f32),
            pltpu.VMEM((sizes.vectors, width), f32),
            pltpu.VMEM((LANES, positions), f32),
        ],
        2,
        operands,
        40 * positions * width * channels,
        parts={10: 1},
    )


def mixer_back_body(
    sizes, lengths, parts, grad_act, activity, inner, small, weight_x, weight_z, grad_z, tokens,
    early, expert_out, out_grad, _near, both, late, shifted, wide, sums, shares,
):
    positions, channels = activity.shape
    devices, own, lanes = early.shape
    late[:, :, lanes : 2 * lanes] = early[...]
    late[:, :, 2 * lanes :] = out_grad[...]
    both[:positions, :] = expert_out[...]
    taps = sizes.taps
    low = jnp.sum(parts[...], axis=0)[:, : sizes.state].astype(bf16)
    state_grad = dot(activity[...], low, 0, 0)
    grad = grad_act[...] + dot(low, small[sizes.proj : sizes.conv, :].astype(bf16))
    kernel = small[sizes.conv : sizes.conv + taps, :]
    offset = small[sizes.conv + taps : sizes.conv + taps + 1, :]
    result, moved = causal_conv(inner[...], shifted, kernel, offset, lengths)
    shade = sigmoid(result)
    grad = grad * (shade * (1.0 + result * (1.0 - shade)))
    sums[...] = jnp.zeros_like(sums)
    sums[taps : taps + 1, :channels] = jnp.sum(grad, axis=0, keepdims=True)
    total = kernel[taps - 1 : taps] * grad
    shifted[positions : positions + ROWS, :] = jnp.zeros((ROWS, channels), f32)
    for delay in range(taps):
        row = taps - 1 - delay
        sums[row : row + 1, :channels] = jnp.sum(grad * moved[delay], axis=0, keepdims=True)
        if delay > 0:
            shifted[:positions, :] = grad * same_segment(lengths, positions, delay)
            total = total + kernel[row : row + 1] * shifted[delay : delay + positions, :]
    grad_x = total.astype(bf16)
    put(wide, total)
    turned = wide[...].T
    part = dot(grad_x, weight_x[...]) + dot(grad_z[...], weight_z[...])
    both[positions:, :] = part.astype(bf16)
    values = tokens[...].astype(f32)
    shares[...] = jnp.broadcast_to(
        jnp.sum(part * (values * rms_scale(values)), axis=0, keepdims=True), shares.shape
    )
    spread = shares[...].T
    turned_sums = sums[...].T
    at = positions + sizes.state
    for k in range(devices):
        rows = slice(k * own, (k + 1) * own)
        late[k, :, :positions] = turned[rows].astype(bf16)
        late[k, :, positions:at] = state_grad[rows].astype(bf16)
        late[k, :, at : at + ROWS] = turned_sums[rows].astype(bf16)
        for piece in range(2):
            to = at + (1 + piece) * ROWS
            source = (2 * k + piece) * own
            late[k, :, to : to + ROWS] = spread[source : source + own].astype(bf16)


def mixer_back(sizes, operands):
    activity, tokens, early = operands[3], operands[9], operands[10]
    positions, width = tokens.shape
    channels = activity.shape[1]
    return call(
        functools.partial(mixer_back_body, sizes),
        "mixer_back",
        (low_of(2 * positions, width), low_of(*early.shape[:2], 2 * early.shape[2] + width)),
        [
            pltpu.VMEM((positions + 2 * ROWS, channels), f32),
            pltpu.VMEM((positions, padded(channels)), f32),
            pltpu.VMEM((ROWS, padded(channels)), f32),
            pltpu.VMEM((ROWS, width), f32),
        ],
        1,
        operands,
        6 * positions * width * channels,
        parts={7: 0},
        after=1,
    )


def proj_grads_body(
    sizes, places, both, *refs,
):
    half, other, _ = refs[:3]
    grad_x, grad_z, state, conv, bias, gain_one, decay, proj, step_bias, skip, gain_two = refs[3:14]
    router, out, late_sum, early_sum = refs[14:]
    step = pl.program_id(0)
    count, own, lanes = both.shape
    width = half.shape[2]
    lanes = lanes - width
    size = half.shape[1]
    positions = 2 * size
    total_x = total_z = None
    add_late = add_early = add_out = None
    for r in range(count):
        part_x = part_z = 0.0
        for place, rows in ((places[1], half), (1 - places[1], other)):
            at = pl.multiple_of(place * size, size)
            part_x += dot(both[r, :, pl.ds(at, size)], rows[r])
            part_z += dot(both[r, :, pl.ds(at + lanes // 2, size)], rows[r])
        more_late = both[r, :, positions : lanes // 2].astype(f32)
        more_early = both[r, :, lanes // 2 + positions : lanes].astype(f32)
        more_out = both[r, :, lanes:].astype(f32)
        if r == 0:
            total_x, total_z, add_late, add_early = part_x, part_z, more_late, more_early
            add_out = more_out
        else:
            total_x, total_z = total_x + part_x, total_z + part_z
            add_late, add_early = add_late + more_late, add_early + more_early
            add_out = add_out + more_out

    @pl.when(step == 0)
    def _():
        grad_x[...] = total_x
        grad_z[...] = total_z
        out[...] = add_out
        late_sum[...] = jnp.zeros_like(late_sum)
        early_sum[...] = jnp.zeros_like(early_sum)
        late_sum[:own, :] = add_late
        early_sum[:own, :] = add_early

    @pl.when(step > 0)
    def _():
        grad_x[...] += total_x
        grad_z[...] += total_z
        out[...] += add_out
        late_sum[:own, :] += add_late
        early_sum[:own, :] += add_early

    @pl.when(step == pl.num_programs(0) - 1)
    def _():
        state[...] = late_sum[:own, : sizes.state]
        turned = late_sum[...].T[sizes.state :, :own]
        conv[...] = turned[: sizes.taps]
        bias[...] = turned[sizes.taps : sizes.taps + 1]
        gain_one[:, :own] = turned[ROWS : ROWS + 1]
        gain_one[:, own:] = turned[2 * ROWS : 2 * ROWS + 1]
        turned = early_sum[...].T[:, :own]
        at = sizes.entries + sizes.rank
        decay[...] = turned[: sizes.entries]
        proj[...] = turned[sizes.entries : at]
        step_bias[...] = turned[at : at + 1]
        skip[...] = turned[at + 1 : at + 2]
        for half_at, columns in ((0, slice(0, own)), (sizes.vectors, slice(own, 2 * own))):
            row = LANES - 2 * sizes.vectors + half_at
            gain_two[:, columns] = turned[row : row + 1]
            router[:, columns] = turned[row + ROWS : row + ROWS + router.shape[0]]


def proj_grads(sizes, experts, places, both, half, other, after):
    devices, own, lanes = both.shape
    width = half.shape[2]
    size = half.shape[1] // 2
    group = min(devices, GROUP)
    shapes = (
        (own, width),
        (own, width),
        (own, sizes.state),
        (sizes.taps, own),
        (1, own),
        (1, 2 * own),
        (sizes.entries, own),
        (sizes.rank, own),
        (1, own),
        (1, own),
        (1, 2 * own),
        (experts, 2 * own),
        (own, width),
    )
    few = pl.BlockSpec((group, own, lanes), lambda i: (i, 0, 0))
    return call(
        functools.partial(proj_grads_body, sizes),
        "proj_grads",
        tuple(shape_of(*shape) for shape in shapes),
        [
            pltpu.VMEM((padded(own), LANES), f32),
            pltpu.VMEM((padded(own), LANES), f32),
        ],
        operands=(places, both, half, other, after),
        flops=8 * devices * size * width * own,
        limit=40,
        grid=(devices // group,),
        in_specs=[
            pl.BlockSpec(memory_space=pltpu.SMEM),
            few,
            pl.BlockSpec((group, size, width), lambda i: (i, 0, 0)),
            pl.BlockSpec((group, size, width), lambda i: (i, 0, 0)),
            pl.BlockSpec(memory_space=pl.ANY),
        ],
        out_specs=tuple(whole(shape) for shape in shapes),
    )


def local(
    tokens,
    cotangent,
    seq_lengths,
    routes,
    mixer_gain,
    proj_x,
    proj_z,
    conv_weight,
    conv_bias,
    state_proj,
    step_proj,
    step_bias,
    decay_log,
    skip_gain,
    out_proj,
    moe_gain,
    router,
    expert_up,
    expert_down,
):
    devices = lax.axis_size("expert")
    hidden = lax.axis_size("hidden")
    index = lax.axis_index("expert")
    place = lax.axis_index("hidden")
    positions, width = tokens.shape
    block = mixer_gain.shape[0]
    experts = expert_up.shape[0]
    own = proj_x.shape[1]
    channels = devices * own
    taps = conv_weight.shape[0]
    sizes = Sizes(decay_log.shape[0], step_proj.shape[0], taps, state_proj.shape[1])
    places = jnp.stack([place, place % 2, index])

    valid = jnp.arange(positions, dtype=jnp.int32) < seq_lengths[0, 0] + seq_lengths[0, 1]
    codes = jnp.where(valid, routes[:, 0].astype(f32), -1.0)[None]

    later = jnp.concatenate([proj_z.T, out_proj], axis=1)
    later, turned_x = lax.optimization_barrier((later, proj_x.T))
    weights = lax.all_gather(later, "expert").reshape(channels, 2 * width)
    weight_x = gather_direct(turned_x, "expert").reshape(channels, width)
    vectors = jnp.concatenate([mixer_gain[None], moe_gain[None], router.T])
    vectors = jnp.pad(vectors, ((0, sizes.vectors - vectors.shape[0]), (0, 0)))
    few = jnp.concatenate([conv_weight, conv_bias[None], step_bias[None], skip_gain[None]])
    pack = [
        decay_log,
        step_proj,
        state_proj.T,
        jnp.pad(few, ((0, ROWS - few.shape[0]), (0, 0))),
        vectors[:, :own],
        vectors[:, own:],
    ]
    pack = gather_small(jnp.concatenate(pack), "expert")

    normed, inner_x, activity, part, small, vectors, share = mixer_in(
        sizes, seq_lengths, places, tokens, cotangent, weight_x, pack
    )
    parts = lax.all_gather(part, "hidden")
    scanned, states, step_pre, basis, rank_low = scan_forward(
        sizes, seq_lengths, parts, activity, small
    )
    quarter = positions // hidden
    share = lax.all_gather(share, "expert")
    mixed, gate_z, branch = mixer_out(sizes, scanned, activity, normed, weights, small)
    low, other = hidden_halves(branch)
    resid, normed_two, sent, sent_grad, own_half, logits = middle(
        places, tokens, low, other, vectors, codes, cotangent, experts
    )
    own_half = lax.all_gather(own_half, "expert")
    out_part, back_part, packed = experts_local(
        codes, logits, sent, sent_grad, expert_up, expert_down
    )
    packed = gather_small(packed, ("expert", "hidden"))
    packed = packed.reshape((devices, hidden) + packed.shape[1:])
    low, other = hidden_halves(back_part)
    share = after(share, packed, other)
    near = swap(share, "hidden", 1)
    operands = (
        seq_lengths, places, packed, low, other, vectors, resid, normed_two, cotangent, mixed,
        weights, scanned, activity, gate_z, step_pre, small, basis, states, rank_low,
    )
    gates, grad_resid, out_grad, grad_act, grad_z, grad_part, early = backward(
        sizes, operands, experts, devices
    )
    parts = lax.all_gather(grad_part, "hidden")
    both, late = mixer_back(
        sizes,
        (
            seq_lengths, parts, grad_act, activity, inner_x, small, weight_x, weights, grad_z,
            tokens, early, out_part, out_grad.reshape(devices, own, width), near,
        ),
    )
    late = lax.all_to_all(late, "expert", 0, 0, tiled=True)
    low, other = hidden_halves(both)
    first = place % 2 == 0
    returned = jnp.where(first, low, other).astype(f32)
    grad_normed = jnp.where(first, other, low).astype(f32)
    values = tokens.astype(f32)
    scale = rms_scale(values)
    unit = values * scale
    scaled = grad_normed * vectors[0:1]
    tokens_grad = grad_resid + scale * (
        scaled - unit * jnp.mean(scaled * unit, axis=-1, keepdims=True)
    )
    gate_values = lax.dynamic_index_in_dim(gates, index, 0, keepdims=False)[0]
    layer_out = valid.astype(f32)[:, None] * (resid + gate_values[:, None] * returned)

    all_codes = packed[:, 0, experts : experts + 1]
    halves = (own_half, swap(own_half, "hidden", 1))

    def by_piece(values):
        values = values.reshape(devices, 2, 2, quarter)
        values = jnp.where(place >= 2, values[:, ::-1], values)
        values = jnp.where(place % 2 == 1, values[:, :, ::-1], values)
        return values.transpose(0, 2, 1, 3).reshape(devices, 1, positions)

    group = min(devices, GROUP)
    pieces = (by_piece(all_codes), by_piece(gates), halves, (share, near))
    if group == devices:
        up_grad, down_grad = expert_grads(places, *pieces, expert_up, expert_down, block)
    else:

        def add(total, some):
            part = expert_grads(places, *some, expert_up, expert_down, block)
            return (total[0] + part[0], total[1] + part[1]), None

        grouped = jax.tree.map(lambda v: v.reshape((-1, group) + v.shape[1:]), pieces)
        zero = jnp.zeros((experts, block, expert_up.shape[2]), f32)
        (up_grad, down_grad), _ = lax.scan(add, (zero, zero), grouped)
    projected = proj_grads(sizes, experts, places, late, share, near, up_grad)
    grad_x, grad_zw, state_grad, conv_grad, conv_bias_grad, gain_one_grad = projected[:6]
    decay_grad, step_proj_grad, step_bias_grad, skip_grad, gain_two_grad = projected[6:11]
    router_grad, out_grad = projected[11:]
    gain_one_grad = jnp.sum(lax.all_gather(gain_one_grad, "hidden"), axis=0)
    return (
        layer_out.astype(bf16),
        tokens_grad,
        gain_one_grad.reshape(-1),
        grad_x.T,
        grad_zw.T,
        conv_grad,
        conv_bias_grad.reshape(-1),
        state_grad,
        step_proj_grad,
        step_bias_grad.reshape(-1),
        decay_grad,
        skip_grad.reshape(-1),
        out_grad,
        gain_two_grad.reshape(-1),
        router_grad.T,
        up_grad,
        down_grad.transpose(0, 2, 1),
    )


def solution(mesh):
    in_specs = (
        P("expert", None),
        P("expert", None),
        P("expert", None),
        P("expert", None),
        P("expert"),
        P(None, ("expert", "hidden")),
        P(None, ("expert", "hidden")),
        P(None, ("expert", "hidden")),
        P(("expert", "hidden")),
        P(("expert", "hidden"), None),
        P(None, ("expert", "hidden")),
        P(("expert", "hidden")),
        P(None, ("expert", "hidden")),
        P(("expert", "hidden")),
        P(("expert", "hidden"), None),
        P("expert"),
        P("expert", None),
        P(None, None, "hidden"),
        P(None, "hidden", None),
    )
    out_specs = (
        P("expert", None),
        P("expert", None),
        P("expert"),
        P(None, ("expert", "hidden")),
        P(None, ("expert", "hidden")),
        P(None, ("expert", "hidden")),
        P(("expert", "hidden")),
        P(("expert", "hidden"), None),
        P(None, ("expert", "hidden")),
        P(("expert", "hidden")),
        P(None, ("expert", "hidden")),
        P(("expert", "hidden")),
        P(("expert", "hidden"), None),
        P("expert"),
        P("expert", None),
        P(None, "expert", "hidden"),
        P(None, "hidden", "expert"),
    )
    return jax.shard_map(local, mesh=mesh, in_specs=in_specs, out_specs=out_specs, check_vma=False)
```

```python
import functools

import jax
import jax.numpy as jnp
from jax import lax
from jax.experimental import pallas as pl
from jax.experimental.pallas import tpu as pltpu
from jax.sharding import PartitionSpec as P

SINK_ITERS = 8
GROUP = 8
LANES = 128
ROWS = 8
FAR = 1e30
LOG2E = 1.4426950408889634
epsilon = 1e-05
f32 = jnp.float32
bf16 = jnp.bfloat16


def dot(left, right, left_dim=1, right_dim=0):
    return lax.dot_general(
        left, right, (((left_dim,), (right_dim,)), ((), ())), preferred_element_type=f32
    )


def shape_of(*dims):
    return jax.ShapeDtypeStruct(dims, f32)


def low_of(*dims):
    return jax.ShapeDtypeStruct(dims, bf16)


def call(body, name, out_shape, scratch=(), scalars=0, operands=(), flops=0, limit=60, parts={}, after=0, known=False, **grid):
    if not grid:
        specs = [pl.BlockSpec(memory_space=pltpu.SMEM)] * scalars
        specs += [pl.BlockSpec(memory_space=pltpu.VMEM)] * (len(operands) - scalars)
        grid = {"in_specs": specs}
        if parts:
            specs[scalars:] = [whole(v.shape) for v in operands[scalars:]]
            for at, half in parts.items():
                specs[at] = column_half(operands[at], half)
            if after:
                specs[-after:] = [pl.BlockSpec(memory_space=pl.ANY)] * after
            grid.update(grid=(1,), out_specs=tuple(whole(v.shape) for v in out_shape))
    return pl.pallas_call(
        body,
        out_shape=out_shape,
        scratch_shapes=list(scratch),
        compiler_params=pltpu.CompilerParams(vmem_limit_bytes=limit * 2**20),
        cost_estimate=pl.CostEstimate(flops=flops if known else 0, bytes_accessed=0, transcendentals=0),
        name=name,
        **grid,
    )(*operands)


def whole(shape):
    return pl.BlockSpec(shape, lambda *i: (0,) * len(shape), pipeline_mode=pl.Buffered(1))


def column_half(array, half):
    rows, columns = array.shape
    return pl.BlockSpec(
        (rows, columns // 2), lambda i: (0, half), pipeline_mode=pl.Buffered(1)
    )


def swap(values, axis, bits):
    size = lax.axis_size(axis)
    return lax.ppermute(values, axis, [(i, i ^ bits) for i in range(size)])


def gather_direct(values, axis):
    size = lax.axis_size(axis)
    if size > GROUP:
        return lax.all_gather(values, axis)
    place = lax.axis_index(axis)
    whole = jnp.zeros((size,) + values.shape, values.dtype)
    for r in range(size):
        piece = swap(values, axis, r) if r > 0 else values
        whole = lax.dynamic_update_slice(whole, piece[None], (place ^ r,) + (0,) * values.ndim)
    return whole


def gather_small(values, axis):
    size = lax.axis_size(axis)
    copies = jnp.broadcast_to(values[None], (size,) + values.shape)
    return lax.all_to_all(copies, axis, 0, 0, tiled=True)


def hidden_pieces(piece):
    near = swap(piece, "hidden", 1)
    far = swap(piece, "hidden", 2)
    return piece, near, far, swap(far, "hidden", 1)


def nothing(*refs):
    pass


def after(values, *others):
    anywhere = pl.BlockSpec(memory_space=pl.ANY)
    return pl.pallas_call(
        nothing,
        out_shape=jax.ShapeDtypeStruct(values.shape, values.dtype),
        in_specs=[anywhere] * (1 + len(others)),
        out_specs=anywhere,
        input_output_aliases={0: 0},
        cost_estimate=pl.CostEstimate(flops=0, bytes_accessed=0, transcendentals=0),
        name="after",
    )(values, *others)


def hidden_halves(kept, given, *others):
    low = (kept.astype(f32) + swap(given, "hidden", 1).astype(f32)).astype(bf16)
    far = swap(low, "hidden", 2)
    if others:
        far = after(far, *others)
    low = (low.astype(f32) + far.astype(f32)).astype(bf16)
    return low, swap(low, "hidden", 1)


def softplus(values):
    return jnp.maximum(values, 0.0) + jnp.log1p(jnp.exp(-jnp.abs(values)))


def sigmoid(values):
    return 1.0 / (1.0 + jnp.exp(-values))


def rms_scale(values):
    return lax.rsqrt(jnp.mean(values * values, axis=-1, keepdims=True) + epsilon)


def put(ref, values):
    width = values.shape[1]
    ref[:, :width] = values
    if ref.shape[1] > width:
        ref[:, width:] = jnp.zeros((values.shape[0], ref.shape[1] - width), ref.dtype)


def widen(tile, width):
    return jnp.concatenate([tile] * (width // LANES), axis=1)


def fold(values):
    total = values[:, :LANES]
    for k in range(1, values.shape[1] // LANES):
        total = total + values[:, k * LANES : (k + 1) * LANES]
    return total


def padded(count):
    return -(-count // LANES) * LANES


def same_segment(lengths, positions, delay):
    places = lax.broadcasted_iota(jnp.int32, (positions, 1), 0)
    first = lengths[0, 0]
    ending = first + lengths[0, 1]

    def segment(at):
        return (at >= first).astype(jnp.int32) + (at >= ending).astype(jnp.int32)

    same = (segment(places) == segment(places - delay)) & (places >= delay)
    return same.astype(f32)


def causal_conv(values, shifted, kernel, offset, lengths):
    positions = values.shape[0]
    taps = kernel.shape[0]
    shifted[:ROWS, :] = jnp.zeros((ROWS, values.shape[1]), f32)
    shifted[ROWS : ROWS + positions, :] = values
    result = offset + kernel[taps - 1 : taps] * values
    moved = [values]
    for delay in range(1, taps):
        part = shifted[ROWS - delay : ROWS - delay + positions, :]
        part = part * same_segment(lengths, positions, delay)
        moved.append(part)
        result = result + kernel[taps - 1 - delay : taps - delay] * part
    return result, moved


def column_tile(ref, first, entries, base):
    start = pl.multiple_of(base // LANES * LANES, LANES)
    tile = ref[first : first + entries, pl.ds(start, LANES)]
    return pltpu.roll(tile, lax.rem(LANES - lax.rem(base, LANES), LANES), 1)


def lane(tile, j, width):
    return jnp.broadcast_to(tile[:, j : j + 1], (tile.shape[0], width))


def split(values, place, kept, given):
    half = values.shape[0] // 2
    first = place == 0
    kept[...] = jnp.where(first, values[:half], values[half:]).astype(bf16)
    given[...] = jnp.where(first, values[half:], values[:half]).astype(bf16)


class Sizes:
    def __init__(self, entries, rank, taps, state):
        self.entries, self.rank, self.taps, self.state = entries, rank, taps, state
        self.step = entries
        self.proj = entries + rank
        self.conv = entries + rank + state
        self.rows = self.conv + ROWS
        self.vectors = 2 * ROWS


def mixer_in_body(
    sizes, lengths, places, tokens, cotangent, weight, pack,
    normed, inner, activity, part, small, vectors, share, shifted,
):
    devices, _, own = pack.shape
    for k in range(devices):
        piece = pack[k].astype(f32)
        small[:, k * own : (k + 1) * own] = piece[: sizes.rows]
        for half in range(2):
            at = (2 * k + half) * own
            row = sizes.rows + half * sizes.vectors
            vectors[:, at : at + own] = piece[row : row + sizes.vectors]
    values = tokens[...].astype(f32)
    low = (values * rms_scale(values) * vectors[0:1, :]).astype(bf16)
    normed[...] = low
    size = share.shape[0] // 2
    at = pl.ds(pl.multiple_of(places[0] * size, size), size)
    share[:size, :] = normed[at, :]
    share[size:, :] = cotangent[at, :]
    values = dot(low, weight[...], 1, 1)
    inner[...] = values
    kernel = small[sizes.conv : sizes.conv + sizes.taps, :]
    offset = small[sizes.conv + sizes.taps : sizes.conv + sizes.taps + 1, :]
    result, _ = causal_conv(values, shifted, kernel, offset, lengths)
    low = (result * sigmoid(result)).astype(bf16)
    activity[...] = low
    part[...] = dot(low, small[sizes.proj : sizes.conv, :].astype(bf16), 1, 1)


def mixer_in(sizes, lengths, places, tokens, cotangent, weight, pack):
    positions, width = tokens.shape
    channels = weight.shape[0]
    return call(
        functools.partial(mixer_in_body, sizes),
        "mixer_in",
        (
            low_of(positions, width),
            shape_of(positions, channels),
            low_of(positions, channels),
            shape_of(positions, sizes.state),
            shape_of(sizes.rows, channels),
            shape_of(sizes.vectors, width),
            low_of(positions // 2, width),
        ),
        [pltpu.VMEM((positions + 2 * ROWS, channels), f32)],
        2,
        (lengths, places, tokens, cotangent, weight, pack),
        3 * positions * width * channels,
    )


def scan_forward_body(
    sizes, lengths, parts, activity, small, out, states, pre, basis, rank_low,
    far_steps, inputs, rates, sums, wide,
):
    width = far_steps.shape[1]
    positions, channels = activity.shape
    entries, rank = sizes.entries, sizes.rank
    projected = jnp.sum(parts[...], axis=0)
    put(wide, projected)
    basis[...] = wide[...].T
    low = projected[:, :rank].astype(bf16)
    rank_low[...] = low
    values = dot(low, small[sizes.step : sizes.proj, :].astype(bf16))
    pre[...] = values
    at = sizes.conv + sizes.taps + 1
    step = softplus(values + small[at : at + 1, :])
    put(far_steps, jnp.where(same_segment(lengths, positions, 1) > 0, step, FAR))
    put(inputs, step * activity[...].astype(f32))
    put(rates, -LOG2E * jnp.exp(small[:entries, :]))
    rate = rates[...]

    def block(i, memory):
        base = pl.multiple_of(i * ROWS, ROWS)
        step_rows = far_steps[pl.ds(base, ROWS), :]
        input_rows = inputs[pl.ds(base, ROWS), :]
        tile_b = column_tile(basis, rank, entries, base)
        tile_c = column_tile(basis, rank + entries, entries, base)
        rows = []
        for j in range(ROWS):
            factor = jnp.exp2(step_rows[j : j + 1] * rate)
            memory = factor * memory + input_rows[j : j + 1] * lane(tile_b, j, width)
            states[base + j] = memory
            rows.append(jnp.sum(lane(tile_c, j, width) * memory, axis=0, keepdims=True))
        sums[pl.ds(base, ROWS), :] = jnp.concatenate(rows, axis=0)
        return memory

    lax.fori_loop(0, positions // ROWS, block, jnp.zeros(rate.shape, f32))
    out[...] = sums[:, :channels]


def scan_forward(sizes, lengths, parts, activity, small):
    positions, channels = activity.shape
    lanes = padded(channels)
    rows = pltpu.VMEM((positions, lanes), f32)
    state_lanes = padded(sizes.state)
    return call(
        functools.partial(scan_forward_body, sizes),
        "scan_forward",
        (
            shape_of(positions, channels),
            shape_of(positions, sizes.entries, lanes),
            shape_of(positions, channels),
            shape_of(state_lanes, positions),
            low_of(positions, sizes.rank),
        ),
        [rows, rows, pltpu.VMEM((sizes.entries, lanes), f32), rows, pltpu.VMEM((positions, state_lanes), f32)],
        1,
        (lengths, parts, activity, small),
        20 * positions * channels * sizes.entries * 16,
    )


def mixer_out_body(
    sizes, places, out, activity, normed, weight_z, weight_out, small, mixed, gate, kept, given
):
    shade = dot(normed[...], weight_z[...], 1, 1)
    gate[...] = shade
    at = sizes.conv + sizes.taps + 2
    values = out[...] + small[at : at + 1, :] * activity[...].astype(f32)
    low = (values * (shade * sigmoid(shade))).astype(bf16)
    mixed[...] = low
    split(dot(low, weight_out[...]), places[1], kept, given)


def mixer_out(sizes, places, out, activity, normed, weights, small):
    positions, channels = activity.shape
    width = normed.shape[1]
    return call(
        functools.partial(mixer_out_body, sizes),
        "mixer_out",
        (
            low_of(positions, channels),
            shape_of(positions, channels),
            low_of(positions // 2, width),
            low_of(positions // 2, width),
        ),
        scalars=1,
        operands=(places, out, activity, normed, weights, weights, small),
        flops=4 * positions * width * channels,
        parts={4: 0, 5: 1},
    )


def slots_of(codes, experts, capacity):
    positions = codes.shape[1]
    member = lax.broadcasted_iota(jnp.int32, (experts, positions), 0).astype(f32) == codes
    member = member.astype(f32)
    shape = (positions, positions)
    prior = lax.broadcasted_iota(jnp.int32, shape, 0) < lax.broadcasted_iota(jnp.int32, shape, 1)
    before = dot(member.astype(bf16), prior.astype(f32).astype(bf16))
    rank = jnp.sum(before * member, axis=0, keepdims=True)
    return jnp.where(codes >= 0, codes * capacity + rank, -1.0)


def picks(slots, first, count):
    shape = (count, slots.shape[1])
    return ((lax.broadcasted_iota(jnp.int32, shape, 0) + first).astype(f32) == slots).astype(f32)


def gelu_pair(values):
    root = 0.7978845608028654
    square = values * values
    bent = jnp.tanh(root * values * (1.0 + 0.044715 * square))
    half = 0.5 * (1.0 + bent)
    slope = half + 0.5 * values * (1.0 - bent * bent) * root * (1.0 + 3 * 0.044715 * square)
    return values * half, slope


def middle_body(
    places, tokens, low, other, vectors, codes, cotangent,
    resid, normed_two, sent, sent_grad, share, logits,
):
    half = low.shape[0]
    experts = logits.shape[0] - ROWS
    capacity = sent.shape[0] // experts
    resid[pl.ds(pl.multiple_of(places[1] * half, half), half), :] = low[...].astype(f32)
    resid[pl.ds(pl.multiple_of((1 - places[1]) * half, half), half), :] = other[...].astype(f32)
    values = tokens[...].astype(f32) + resid[...]
    resid[...] = values
    rows = (values * rms_scale(values) * vectors[1:2, :]).astype(bf16)
    normed_two[...] = rows
    logits[:experts, :] = dot(vectors[2 : 2 + experts, :].astype(bf16), rows, 1, 1)
    logits[experts:, :] = jnp.broadcast_to(codes[...], (ROWS, codes.shape[1]))
    every = picks(slots_of(codes[...], experts, capacity), 0, sent.shape[0]).astype(bf16)
    sent[...] = dot(every, rows).astype(bf16)
    sent_grad[...] = dot(every, cotangent[...]).astype(bf16)
    size = share.shape[0] // 2
    for k in range(2):
        at = pl.multiple_of((places[0] ^ (2 * k)) * size, size)
        share[k * size : (k + 1) * size, :] = normed_two[pl.ds(at, size), :]


def middle(places, tokens, low, other, vectors, codes, cotangent, experts):
    positions, width = tokens.shape
    slots = 3 * positions // 2
    return call(
        middle_body,
        "middle",
        (
            shape_of(positions, width),
            low_of(positions, width),
            low_of(slots, width),
            low_of(slots, width),
            low_of(positions // 2, width),
            shape_of(experts + ROWS, positions),
        ),
        (),
        1,
        (places, tokens, low, other, vectors, codes, cotangent),
        4 * positions * width * slots,
    )


def experts_body(
    places, codes, logits, rows, grads, up, down, out, kept, given, packed, slots, outs, backs, gate_row
):
    step = pl.program_id(0)
    experts = pl.num_programs(0)
    capacity = rows.shape[0]

    @pl.when(step == 0)
    def _():
        slots[...] = slots_of(codes[...], experts, capacity)
        gate_row[...] = jnp.zeros_like(gate_row)

    first = pl.multiple_of(step * capacity, capacity)
    active, slope = gelu_pair(dot(rows[...], up[0]))
    plain = dot(grads[...], down[0], 1, 1)
    low = active.astype(bf16)
    gate_slots = jnp.sum(low.astype(f32) * plain, axis=1, keepdims=True)
    chosen = picks(slots[...], first, capacity)
    gate_row[...] += jnp.sum(chosen * gate_slots, axis=0, keepdims=True)
    outs[pl.ds(first, capacity), :] = dot(low, down[0]).astype(bf16)
    backs[pl.ds(first, capacity), :] = dot((plain * slope).astype(bf16), up[0], 1, 1).astype(bf16)

    @pl.when(step == experts - 1)
    def _():
        every = picks(slots[...], 0, outs.shape[0]).astype(bf16)
        out[...] = dot(every, outs[...], 0, 0).astype(bf16)
        split(dot(every, backs[...], 0, 0), places[1], kept, given)
        packed[...] = logits[...]
        packed[experts + 1 : experts + 2, :] = gate_row[...]


def experts_local(places, codes, logits, rows, grads, up, down):
    slots, width = rows.shape
    experts, _, hidden = up.shape
    positions = codes.shape[1]
    capacity = slots // experts
    shapes = (
        low_of(positions, width),
        low_of(positions // 2, width),
        low_of(positions // 2, width),
        shape_of(*logits.shape),
    )
    return call(
        experts_body,
        "experts_local",
        shapes,
        [
            pltpu.VMEM((1, positions), f32),
            pltpu.VMEM((slots, width), bf16),
            pltpu.VMEM((slots, width), bf16),
            pltpu.VMEM((1, positions), f32),
        ],
        operands=(places, codes, logits, rows, grads, up, down),
        flops=8 * slots * width * hidden,
        grid=(experts,),
        in_specs=[
            pl.BlockSpec(memory_space=pltpu.SMEM),
            whole((1, positions)),
            whole(logits.shape),
            pl.BlockSpec((capacity, width), lambda i: (i, 0)),
            pl.BlockSpec((capacity, width), lambda i: (i, 0)),
            pl.BlockSpec((1, width, hidden), lambda i: (i, 0, 0)),
            pl.BlockSpec((1, hidden, width), lambda i: (i, 0, 0)),
        ],
        out_specs=tuple(whole(v.shape) for v in shapes),
    )


def expert_grads_body(
    places, codes, gates, *refs,
):
    rows, grads = refs[:2], refs[2:6]
    up, down, up_grad, down_grad, sent, sent_grad, gate_slots = refs[6:]
    step = pl.program_id(0)
    experts, total, width = sent.shape
    count, _, positions = codes.shape
    capacity = total // count
    quarter = positions // 4
    block = up_grad.shape[1]
    window = min(padded(block + LANES - 2 * ROWS), width)

    @pl.when(step == 0)
    def _():
        shape = (positions, positions)
        lanes = lax.broadcasted_iota(jnp.int32, shape, 1)
        part = lanes // quarter
        home = ((part % 2 * 2 + part // 2) ^ places[0]) * quarter + lanes % quarter
        order = (lax.broadcasted_iota(jnp.int32, shape, 0) == home).astype(f32).astype(bf16)
        for r in range(count):
            code = codes[r, experts : experts + 1, :]
            chosen = picks(slots_of(code, experts, capacity), 0, experts * capacity)
            pick = dot(chosen.astype(bf16), order).astype(bf16)
            gate = jnp.sum(chosen * gates[r], axis=1, keepdims=True)
            part = pl.ds(r * capacity, capacity)
            for pieces, target in ((rows, sent), (grads, sent_grad)):
                whole_rows = jnp.concatenate([piece[r] for piece in pieces], axis=0)
                moved = dot(pick, whole_rows).astype(bf16)
                for i in range(experts):
                    target[i, part, :] = moved[i * capacity : (i + 1) * capacity]
            for i in range(experts):
                gate_slots[i, part, :] = jnp.broadcast_to(
                    gate[i * capacity : (i + 1) * capacity], (capacity, LANES)
                )

    gate = gate_slots[step][:, :1]
    active, slope = gelu_pair(dot(sent[step], up[0]))
    plain = dot(sent_grad[step], down[0], 1, 1)
    grad_pre = (plain * slope * gate).astype(bf16)
    scaled = (active * gate).astype(bf16)
    start = jnp.minimum(places[2] * block // LANES * LANES, width - window)
    shift = lax.rem(window - (places[2] * block - start), window)
    own = pl.ds(pl.multiple_of(start, LANES), window)
    up_grad[0] = pltpu.roll(dot(sent[step, :, own], grad_pre, 0, 0), shift, 0)[:block]
    down_grad[0] = pltpu.roll(dot(sent_grad[step, :, own], scaled, 0, 0), shift, 0)[:block]


def expert_grads(places, codes, gates, rows, grads, up, down, block):
    count, _, positions = codes.shape
    experts, width, hidden = up.shape
    slots = count * (3 * positions // (2 * experts))
    shape = (experts, block, hidden)
    out = pl.BlockSpec((1, block, hidden), lambda i: (i, 0, 0))
    half = whole((count, positions // 2, width))

    def piece(values):
        last = values.shape[1] * 4 // positions - 1
        shape = (count, positions // 4, width)
        return pl.BlockSpec(shape, lambda i: (0, last, 0), pipeline_mode=pl.Buffered(1))

    return call(
        expert_grads_body,
        "expert_grads",
        (shape_of(*shape), shape_of(*shape)),
        [
            pltpu.VMEM((experts, slots, width), bf16),
            pltpu.VMEM((experts, slots, width), bf16),
            pltpu.VMEM((experts, slots, LANES), f32),
        ],
        operands=(places, codes, gates, *rows, *grads, up, down),
        flops=12 * experts * slots * width * hidden,
        known=True,
        grid=(experts,),
        in_specs=[
            pl.BlockSpec(memory_space=pltpu.SMEM),
            whole((count, codes.shape[1], positions)),
            whole((count, 1, positions)),
            half,
            half,
            *(piece(values) for values in grads),
            pl.BlockSpec((1, width, hidden), lambda i: (i, 0, 0)),
            pl.BlockSpec((1, hidden, width), lambda i: (i, 0, 0)),
        ],
        out_specs=(out, out),
    )


def sinkhorn(packed, gate_parts, experts):
    start = jnp.exp(packed[:, :experts, :])
    codes = packed[:, experts : experts + 1, :]
    grad_gates = jnp.sum(gate_parts[...], axis=0)
    valid = (codes >= 0).astype(f32)
    onehot = (lax.broadcasted_iota(jnp.int32, start.shape, 1).astype(f32) == codes).astype(f32)
    weights = start
    history = []
    for _ in range(SINK_ITERS):
        columns = jnp.sum(jnp.sum(weights * valid, axis=2, keepdims=True), axis=0, keepdims=True)
        scaled = weights / columns
        row_sums = jnp.sum(scaled, axis=1, keepdims=True)
        weights = scaled / row_sums
        history.append((columns, scaled, row_sums, weights))
    gates = experts * jnp.sum(weights * onehot, axis=1, keepdims=True)
    grads = experts * grad_gates * onehot
    for columns, scaled, row_sums, result in reversed(history):
        grads = (grads - jnp.sum(grads * result, axis=1, keepdims=True)) / row_sums
        term = jnp.sum(jnp.sum(grads * scaled, axis=2, keepdims=True), axis=0, keepdims=True)
        grads = (grads - valid * term) / columns
    return gates, grads * start


def backward_body(
    sizes, lengths, places, packed, gate_parts, low, other, vectors, resid, normed_two, cotangent, mixed,
    weight_out, out, activity, gate, pre, small, basis, states, rank_low,
    gates, grad_resid, out_grad, grad_act, grad_gate, grad_part, early,
    all_gates, all_grads, branch_grad, far_steps, steps, inputs, outer, rates, sum_input,
    sum_step, sums, shares, square,
):
    positions, width = resid.shape
    channels = activity.shape[1]
    lanes = far_steps.shape[1]
    entries, rank = sizes.entries, sizes.rank
    devices, own, _ = early.shape
    experts = all_grads.shape[1]
    half = low.shape[0]

    every_gate, every_grad = sinkhorn(packed, gate_parts, experts)
    gates[...] = every_gate
    all_gates[...] = every_gate
    all_grads[...] = every_grad
    grad_logits = all_grads[places[2]].astype(bf16)
    square[...] = jnp.broadcast_to(all_gates[places[2]], square.shape)
    gate_column = square[...].T[:, :1]

    branch_grad[pl.ds(pl.multiple_of(places[1] * half, half), half), :] = low[...].astype(f32)
    branch_grad[pl.ds(pl.multiple_of((1 - places[1]) * half, half), half), :] = other[...].astype(f32)
    at = lax.broadcasted_iota(jnp.int32, (positions, 1), 0)
    valid = (at < lengths[0, 0] + lengths[0, 1]).astype(f32)
    grad_two = dot(grad_logits, vectors[2 : 2 + experts, :].astype(bf16), 0, 0)
    grad_two = grad_two + branch_grad[...] * (gate_column * valid)
    values = resid[...]
    scale = rms_scale(values)
    unit = values * scale
    shares[...] = jnp.zeros_like(shares)
    shares[0:1, :] = jnp.sum(grad_two * unit, axis=0, keepdims=True)
    shares[ROWS : ROWS + experts, :] = dot(grad_logits, normed_two[...])
    scaled = grad_two * vectors[1:2, :]
    total = cotangent[...].astype(f32) * valid + scale * (
        scaled - unit * jnp.mean(scaled * unit, axis=-1, keepdims=True)
    )
    grad_resid[...] = total
    branch = total.astype(bf16)
    out_grad[...] = dot(mixed[...], branch, 0, 0).astype(bf16)
    grad = dot(branch, weight_out[...], 1, 1)

    row = sizes.conv + sizes.taps + 1
    shifted = pre[...] + small[row : row + 1, :]
    skip = small[row + 1 : row + 2, :]
    step = softplus(shifted)
    act = activity[...].astype(f32)
    put(far_steps, jnp.where(same_segment(lengths, positions, 1) > 0, step, FAR))
    put(steps, step)
    put(inputs, step * act)
    put(rates, -jnp.exp(small[:entries, :]))
    level = gate[...]
    shade = sigmoid(level)
    through = grad * level * shade
    put(outer, through)
    grad_level = grad * (out[...] + skip * act) * (shade * (1.0 + level * (1.0 - shade)))
    grad_gate[...] = grad_level.astype(bf16)
    put(sum_input, grad_level)
    turned = sum_input[...].T
    for k in range(devices):
        early[k, :, :positions] = turned[k * own : (k + 1) * own].astype(bf16)
    sums[...] = jnp.zeros_like(sums)
    skip_row = entries + rank + 1
    sums[skip_row : skip_row + 1, :channels] = jnp.sum(through * act, axis=0, keepdims=True)
    rate = rates[...]
    quick = rate * LOG2E
    blocks = positions // ROWS
    grad_part[...] = jnp.zeros_like(grad_part)
    lane_ids = lax.broadcasted_iota(jnp.int32, (entries, LANES), 1)

    def block(i, carried):
        later, rate_sum = carried
        base = pl.multiple_of((blocks - 1 - i) * ROWS, ROWS)
        far_rows = far_steps[pl.ds(base, ROWS), :]
        step_rows = steps[pl.ds(base, ROWS), :]
        input_rows = inputs[pl.ds(base, ROWS), :]
        outer_rows = outer[pl.ds(base, ROWS), :]
        columns_b = column_tile(basis, rank, entries, base)
        columns_c = column_tile(basis, rank + entries, entries, base)
        input_sums = [None] * ROWS
        step_sums = [None] * ROWS
        found_b = jnp.zeros((entries, LANES), f32)
        found_c = jnp.zeros((entries, LANES), f32)
        for j in reversed(range(ROWS)):
            tile_b = lane(columns_b, j, lanes)
            outside = outer_rows[j : j + 1]
            inside = input_rows[j : j + 1]
            state = states[base + j]
            flow = lane(columns_c, j, lanes) * outside + later
            later = jnp.exp2(far_rows[j : j + 1] * quick) * flow
            in_b = jnp.sum(fold(flow * inside), axis=1, keepdims=True)
            in_c = jnp.sum(fold(outside * state), axis=1, keepdims=True)
            found_b = jnp.where(lane_ids == j, in_b, found_b)
            found_c = jnp.where(lane_ids == j, in_c, found_c)
            input_sums[j] = jnp.sum(flow * tile_b, axis=0, keepdims=True)
            change = flow * (state - inside * tile_b)
            step_sums[j] = jnp.sum(change * rate, axis=0, keepdims=True)
            rate_sum = rate_sum + change * step_rows[j : j + 1]
        sum_input[pl.ds(base, ROWS), :] = jnp.concatenate(input_sums, axis=0)
        sum_step[pl.ds(base, ROWS), :] = jnp.concatenate(step_sums, axis=0)
        start = pl.multiple_of(base // LANES * LANES, LANES)
        shift = lax.rem(base, LANES)
        for first, found in ((0, found_b), (entries, found_c)):
            basis_grad = square.at[first : first + entries, pl.ds(start, LANES)]
            basis_grad[...] += pltpu.roll(found, shift, 1)
        return later, rate_sum

    square[...] = jnp.zeros_like(square)
    zero = jnp.zeros(rate.shape, f32)
    _, rate_sum = lax.fori_loop(0, blocks, block, (zero, zero))
    sums[:entries, :] = rate_sum * rate
    back_input = sum_input[:, :channels]
    grad_act[...] = outer[:, :channels] * skip + back_input * step
    grad_step = (back_input * act + sum_step[:, :channels]) * sigmoid(shifted)
    grad_low = grad_step.astype(bf16)
    sums[entries + rank : entries + rank + 1, :channels] = jnp.sum(grad_step, axis=0, keepdims=True)
    sums[entries : entries + rank, :channels] = dot(rank_low[...], grad_low, 0, 0)
    grad_part[:, :rank] = dot(grad_low, small[sizes.step : sizes.proj, :].astype(bf16), 1, 1)
    grad_part[:, rank : rank + 2 * entries] = square[...].T[:, : 2 * entries]
    turned = sums[...].T
    spread = shares[...].T
    side = padded(sizes.vectors) - 2 * sizes.vectors
    for k in range(devices):
        early[k, :, positions : positions + side] = turned[k * own : (k + 1) * own, :side].astype(bf16)
        for piece in range(2):
            to = positions + side + piece * sizes.vectors
            source = (2 * k + piece) * own
            early[k, :, to : to + sizes.vectors] = spread[source : source + own].astype(bf16)


def backward(sizes, operands, experts, devices):
    resid, activity = operands[7], operands[13]
    positions, width = resid.shape
    channels = activity.shape[1]
    lanes = padded(channels)
    rows = pltpu.VMEM((positions, lanes), f32)
    return call(
        functools.partial(backward_body, sizes),
        "backward",
        (
            shape_of(devices, 1, positions),
            shape_of(positions, width),
            low_of(channels, width),
            shape_of(positions, channels),
            low_of(positions, channels),
            shape_of(positions, padded(sizes.state)),
            low_of(devices, channels // devices, positions + LANES),
        ),
        [
            pltpu.VMEM((devices, 1, positions), f32),
            pltpu.VMEM((devices, experts, positions), f32),
            pltpu.VMEM((positions, width), f32),
            rows,
            rows,
            rows,
            rows,
            pltpu.VMEM((sizes.entries, lanes), f32),
            rows,
            rows,
            pltpu.VMEM((LANES, lanes), f32),
            pltpu.VMEM((sizes.vectors, width), f32),
            pltpu.VMEM((LANES, positions), f32),
        ],
        2,
        operands,
        40 * positions * width * channels,
        parts={11: 1},
    )


def mixer_back_body(
    sizes, lengths, places, parts, grad_act, activity, inner, small, weight_x, weight_z, grad_z, tokens,
    early, expert_out, out_grad, _grads, _rows, kept, given, late, shifted, wide, sums, shares,
):
    positions, channels = activity.shape
    devices, own, lanes = early.shape
    late[:, :, lanes : 2 * lanes] = early[...]
    late[:, :, 2 * lanes :] = out_grad[...]
    taps = sizes.taps
    low = jnp.sum(parts[...], axis=0)[:, : sizes.state].astype(bf16)
    state_grad = dot(activity[...], low, 0, 0)
    grad = grad_act[...] + dot(low, small[sizes.proj : sizes.conv, :].astype(bf16))
    kernel = small[sizes.conv : sizes.conv + taps, :]
    offset = small[sizes.conv + taps : sizes.conv + taps + 1, :]
    result, moved = causal_conv(inner[...], shifted, kernel, offset, lengths)
    shade = sigmoid(result)
    grad = grad * (shade * (1.0 + result * (1.0 - shade)))
    sums[...] = jnp.zeros_like(sums)
    sums[taps : taps + 1, :channels] = jnp.sum(grad, axis=0, keepdims=True)
    total = kernel[taps - 1 : taps] * grad
    shifted[positions : positions + ROWS, :] = jnp.zeros((ROWS, channels), f32)
    for delay in range(taps):
        row = taps - 1 - delay
        sums[row : row + 1, :channels] = jnp.sum(grad * moved[delay], axis=0, keepdims=True)
        if delay > 0:
            shifted[:positions, :] = grad * same_segment(lengths, positions, delay)
            total = total + kernel[row : row + 1] * shifted[delay : delay + positions, :]
    grad_x = total.astype(bf16)
    put(wide, total)
    turned = wide[...].T
    part = dot(grad_x, weight_x[...]) + dot(grad_z[...], weight_z[...])
    first = places[1] == 0
    low = part.astype(bf16)
    kept[...] = jnp.where(first, expert_out[...], low)
    given[...] = jnp.where(first, low, expert_out[...])
    values = tokens[...].astype(f32)
    shares[...] = jnp.broadcast_to(
        jnp.sum(part * (values * rms_scale(values)), axis=0, keepdims=True), shares.shape
    )
    spread = shares[...].T
    turned_sums = sums[...].T
    at = positions + sizes.state
    for k in range(devices):
        rows = slice(k * own, (k + 1) * own)
        late[k, :, :positions] = turned[rows].astype(bf16)
        late[k, :, positions:at] = state_grad[rows].astype(bf16)
        late[k, :, at : at + ROWS] = turned_sums[rows].astype(bf16)
        for piece in range(2):
            to = at + (1 + piece) * ROWS
            source = (2 * k + piece) * own
            late[k, :, to : to + ROWS] = spread[source : source + own].astype(bf16)


def mixer_back(sizes, operands):
    activity, tokens, early = operands[4], operands[10], operands[11]
    positions, width = tokens.shape
    channels = activity.shape[1]
    return call(
        functools.partial(mixer_back_body, sizes),
        "mixer_back",
        (low_of(positions, width), low_of(positions, width), low_of(*early.shape[:2], 2 * early.shape[2] + width)),
        [
            pltpu.VMEM((positions + 2 * ROWS, channels), f32),
            pltpu.VMEM((positions, padded(channels)), f32),
            pltpu.VMEM((ROWS, padded(channels)), f32),
            pltpu.VMEM((ROWS, width), f32),
        ],
        2,
        operands,
        6 * positions * width * channels,
        parts={8: 0},
        after=2,
    )


def proj_grads_body(
    sizes, places, both, *refs,
):
    pieces = refs[:4]
    grad_x, grad_z, state, conv, bias, gain_one, decay, proj, step_bias, skip, gain_two = refs[4:15]
    router, out, late_sum, early_sum, buffer = refs[15:]
    step = pl.program_id(0)
    count, own, lanes = both.shape
    _, size, width = pieces[0].shape
    lanes = lanes - width
    positions = 4 * size
    total_x = total_z = None
    add_late = add_early = add_out = None
    for r in range(count):
        for k, piece in enumerate(pieces):
            at = pl.multiple_of((places[0] ^ k) * size, size)
            buffer[r, pl.ds(at, size), :] = piece[r]
        part_x = dot(both[r, :, :positions], buffer[r])
        part_z = dot(both[r, :, lanes // 2 : lanes // 2 + positions], buffer[r])
        more_late = both[r, :, positions : lanes // 2].astype(f32)
        more_early = both[r, :, lanes // 2 + positions : lanes].astype(f32)
        more_out = both[r, :, lanes:].astype(f32)
        if r == 0:
            total_x, total_z, add_late, add_early = part_x, part_z, more_late, more_early
            add_out = more_out
        else:
            total_x, total_z = total_x + part_x, total_z + part_z
            add_late, add_early = add_late + more_late, add_early + more_early
            add_out = add_out + more_out

    @pl.when(step == 0)
    def _():
        grad_x[...] = total_x
        grad_z[...] = total_z
        out[...] = add_out
        late_sum[...] = jnp.zeros_like(late_sum)
        early_sum[...] = jnp.zeros_like(early_sum)
        late_sum[:own, :] = add_late
        early_sum[:own, :] = add_early

    @pl.when(step > 0)
    def _():
        grad_x[...] += total_x
        grad_z[...] += total_z
        out[...] += add_out
        late_sum[:own, :] += add_late
        early_sum[:own, :] += add_early

    @pl.when(step == pl.num_programs(0) - 1)
    def _():
        state[...] = late_sum[:own, : sizes.state]
        turned = late_sum[...].T[sizes.state :, :own]
        conv[...] = turned[: sizes.taps]
        bias[...] = turned[sizes.taps : sizes.taps + 1]
        gain_one[:, :own] = turned[ROWS : ROWS + 1]
        gain_one[:, own:] = turned[2 * ROWS : 2 * ROWS + 1]
        turned = early_sum[...].T[:, :own]
        at = sizes.entries + sizes.rank
        decay[...] = turned[: sizes.entries]
        proj[...] = turned[sizes.entries : at]
        step_bias[...] = turned[at : at + 1]
        skip[...] = turned[at + 1 : at + 2]
        for half_at, columns in ((0, slice(0, own)), (sizes.vectors, slice(own, 2 * own))):
            row = LANES - 2 * sizes.vectors + half_at
            gain_two[:, columns] = turned[row : row + 1]
            router[:, columns] = turned[row + ROWS : row + ROWS + router.shape[0]]


def proj_grads(sizes, experts, places, both, pieces):
    devices, own, lanes = both.shape
    _, size, width = pieces[-1].shape
    positions = 4 * size
    group = min(devices, GROUP)
    shapes = (
        (own, width),
        (own, width),
        (own, sizes.state),
        (sizes.taps, own),
        (1, own),
        (1, 2 * own),
        (sizes.entries, own),
        (sizes.rank, own),
        (1, own),
        (1, own),
        (1, 2 * own),
        (experts, 2 * own),
        (own, width),
    )
    few = pl.BlockSpec((group, own, lanes), lambda i: (i, 0, 0))
    return call(
        functools.partial(proj_grads_body, sizes),
        "proj_grads",
        tuple(shape_of(*shape) for shape in shapes),
        [
            pltpu.VMEM((padded(own), LANES), f32),
            pltpu.VMEM((padded(own), LANES), f32),
            pltpu.VMEM((group, positions, width), bf16),
        ],
        operands=(places, both, *pieces),
        flops=8 * devices * size * width * own,
        grid=(devices // group,),
        in_specs=[
            pl.BlockSpec(memory_space=pltpu.SMEM),
            few,
            *([pl.BlockSpec((group, size, width), lambda i: (i, 0, 0))] * 4),
        ],
        out_specs=tuple(whole(shape) for shape in shapes),
    )


def local(
    tokens,
    cotangent,
    seq_lengths,
    routes,
    mixer_gain,
    proj_x,
    proj_z,
    conv_weight,
    conv_bias,
    state_proj,
    step_proj,
    step_bias,
    decay_log,
    skip_gain,
    out_proj,
    moe_gain,
    router,
    expert_up,
    expert_down,
):
    devices = lax.axis_size("expert")
    hidden = lax.axis_size("hidden")
    index = lax.axis_index("expert")
    place = lax.axis_index("hidden")
    positions, width = tokens.shape
    block = mixer_gain.shape[0]
    experts = expert_up.shape[0]
    own = proj_x.shape[1]
    channels = devices * own
    taps = conv_weight.shape[0]
    sizes = Sizes(decay_log.shape[0], step_proj.shape[0], taps, state_proj.shape[1])
    places = jnp.stack([place, place % 2, index])

    valid = jnp.arange(positions, dtype=jnp.int32) < seq_lengths[0, 0] + seq_lengths[0, 1]
    codes = jnp.where(valid, routes[:, 0].astype(f32), -1.0)[None]

    later = jnp.concatenate([proj_z.T, out_proj], axis=1)
    later, turned_x = lax.optimization_barrier((later, proj_x.T))
    weights = lax.all_gather(later, "expert").reshape(channels, 2 * width)
    weight_x = gather_direct(turned_x, "expert").reshape(channels, width)
    vectors = jnp.concatenate([mixer_gain[None], moe_gain[None], router.T])
    vectors = jnp.pad(vectors, ((0, sizes.vectors - vectors.shape[0]), (0, 0)))
    few = jnp.concatenate([conv_weight, conv_bias[None], step_bias[None], skip_gain[None]])
    pack = [
        decay_log,
        step_proj,
        state_proj.T,
        jnp.pad(few, ((0, ROWS - few.shape[0]), (0, 0))),
        vectors[:, :own],
        vectors[:, own:],
    ]
    pack = gather_small(jnp.concatenate(pack), "expert")

    normed, inner_x, activity, part, small, vectors, share = mixer_in(
        sizes, seq_lengths, places, tokens, cotangent, weight_x, pack
    )
    parts = lax.all_gather(part, "hidden")
    scanned, states, step_pre, basis, rank_low = scan_forward(
        sizes, seq_lengths, parts, activity, small
    )
    quarter = positions // hidden
    share = lax.all_gather(share, "expert")
    mixed, gate_z, kept, given = mixer_out(
        sizes, places, scanned, activity, normed, weights, small
    )
    low, other = hidden_halves(kept, given)
    resid, normed_two, sent, sent_grad, own_half, logits = middle(
        places, tokens, low, other, vectors, codes, cotangent, experts
    )
    own_half = lax.all_gather(own_half, "expert")
    out_part, kept, given, packed = experts_local(
        places, codes, logits, sent, sent_grad, expert_up, expert_down
    )
    packed = gather_small(packed, "expert")
    gate_parts = lax.all_gather(packed[:, experts + 1 : experts + 2], "hidden")
    low, other = hidden_halves(kept, given, gate_parts)
    share = after(share, gate_parts, other)
    near = swap(share, "hidden", 1)
    far = swap(share[:, quarter:], "hidden", 2)
    operands = (
        seq_lengths, places, packed, gate_parts, low, other, vectors, resid, normed_two, cotangent, mixed,
        weights, scanned, activity, gate_z, step_pre, small, basis, states, rank_low,
    )
    gates, grad_resid, out_grad, grad_act, grad_z, grad_part, early = backward(
        sizes, operands, experts, devices
    )
    own_half = after(own_half, gates)
    parts = lax.all_gather(grad_part, "hidden")
    kept, given, late = mixer_back(
        sizes,
        (
            seq_lengths, places, parts, grad_act, activity, inner_x, small, weight_x, weights, grad_z,
            tokens, early, out_part, out_grad.reshape(devices, own, width),
            far, own_half,
        ),
    )
    late = lax.all_to_all(late, "expert", 0, 0, tiled=True)
    halves = (own_half, swap(own_half, "hidden", 1))

    last = swap(far, "hidden", 1)
    group = min(devices, GROUP)
    pieces = (packed, gates, halves, (share, far, near, last))
    if group == devices:
        up_grad, down_grad = expert_grads(places, *pieces, expert_up, expert_down, block)
    else:

        def add(total, some):
            part = expert_grads(places, *some, expert_up, expert_down, block)
            return (total[0] + part[0], total[1] + part[1]), None

        grouped = jax.tree.map(lambda v: v.reshape((-1, group) + v.shape[1:]), pieces)
        zero = jnp.zeros((experts, block, expert_up.shape[2]), f32)
        (up_grad, down_grad), _ = lax.scan(add, (zero, zero), grouped)
    low, other = hidden_halves(kept, given, up_grad)
    first = place % 2 == 0
    returned = jnp.where(first, low, other).astype(f32)
    grad_normed = jnp.where(first, other, low).astype(f32)
    values = tokens.astype(f32)
    scale = rms_scale(values)
    unit = values * scale
    scaled = grad_normed * vectors[0:1]
    tokens_grad = grad_resid + scale * (
        scaled - unit * jnp.mean(scaled * unit, axis=-1, keepdims=True)
    )
    gate_values = lax.dynamic_index_in_dim(gates, index, 0, keepdims=False)[0]
    layer_out = valid.astype(f32)[:, None] * (resid + gate_values[:, None] * returned)

    normed_far = swap(after(share[:, :quarter], kept), "hidden", 2)
    normed_pieces = (share, near, normed_far, swap(normed_far, "hidden", 1))
    projected = proj_grads(sizes, experts, places, late, normed_pieces)
    grad_x, grad_zw, state_grad, conv_grad, conv_bias_grad, gain_one_grad = projected[:6]
    decay_grad, step_proj_grad, step_bias_grad, skip_grad, gain_two_grad = projected[6:11]
    router_grad, out_grad = projected[11:]
    gain_one_grad = jnp.sum(lax.all_gather(gain_one_grad, "hidden"), axis=0)
    return (
        layer_out.astype(bf16),
        tokens_grad,
        gain_one_grad.reshape(-1),
        grad_x.T,
        grad_zw.T,
        conv_grad,
        conv_bias_grad.reshape(-1),
        state_grad,
        step_proj_grad,
        step_bias_grad.reshape(-1),
        decay_grad,
        skip_grad.reshape(-1),
        out_grad,
        gain_two_grad.reshape(-1),
        router_grad.T,
        up_grad,
        down_grad.transpose(0, 2, 1),
    )


def solution(mesh):
    in_specs = (
        P("expert", None),
        P("expert", None),
        P("expert", None),
        P("expert", None),
        P("expert"),
        P(None, ("expert", "hidden")),
        P(None, ("expert", "hidden")),
        P(None, ("expert", "hidden")),
        P(("expert", "hidden")),
        P(("expert", "hidden"), None),
        P(None, ("expert", "hidden")),
        P(("expert", "hidden")),
        P(None, ("expert", "hidden")),
        P(("expert", "hidden")),
        P(("expert", "hidden"), None),
        P("expert"),
        P("expert", None),
        P(None, None, "hidden"),
        P(None, "hidden", None),
    )
    out_specs = (
        P("expert", None),
        P("expert", None),
        P("expert"),
        P(None, ("expert", "hidden")),
        P(None, ("expert", "hidden")),
        P(None, ("expert", "hidden")),
        P(("expert", "hidden")),
        P(("expert", "hidden"), None),
        P(None, ("expert", "hidden")),
        P(("expert", "hidden")),
        P(None, ("expert", "hidden")),
        P(("expert", "hidden")),
        P(("expert", "hidden"), None),
        P("expert"),
        P("expert", None),
        P(None, "expert", "hidden"),
        P(None, "hidden", "expert"),
    )
    return jax.shard_map(local, mesh=mesh, in_specs=in_specs, out_specs=out_specs, check_vma=False)
```

```python
import functools

import jax
import jax.numpy as jnp
from jax import lax
from jax.experimental import pallas as pl
from jax.experimental.pallas import tpu as pltpu
from jax.sharding import PartitionSpec as P

SINK_ITERS = 8
GROUP = 8
LANES = 128
ROWS = 8
FAR = 1e30
LOG2E = 1.4426950408889634
epsilon = 1e-05
f32 = jnp.float32
bf16 = jnp.bfloat16


def dot(left, right, left_dim=1, right_dim=0):
    return lax.dot_general(
        left, right, (((left_dim,), (right_dim,)), ((), ())), preferred_element_type=f32
    )


def shape_of(*dims):
    return jax.ShapeDtypeStruct(dims, f32)


def low_of(*dims):
    return jax.ShapeDtypeStruct(dims, bf16)


def call(body, name, out_shape, scratch=(), scalars=0, operands=(), flops=0, limit=60, parts={}, after=0, known=False, **grid):
    if not grid:
        specs = [pl.BlockSpec(memory_space=pltpu.SMEM)] * scalars
        specs += [pl.BlockSpec(memory_space=pltpu.VMEM)] * (len(operands) - scalars)
        grid = {"in_specs": specs}
        if parts:
            specs[scalars:] = [whole(v.shape) for v in operands[scalars:]]
            for at, half in parts.items():
                specs[at] = column_half(operands[at], half)
            if after:
                specs[-after:] = [pl.BlockSpec(memory_space=pl.ANY)] * after
            grid.update(grid=(1,), out_specs=tuple(whole(v.shape) for v in out_shape))
    return pl.pallas_call(
        body,
        out_shape=out_shape,
        scratch_shapes=list(scratch),
        compiler_params=pltpu.CompilerParams(vmem_limit_bytes=limit * 2**20),
        cost_estimate=pl.CostEstimate(flops=flops if known else 0, bytes_accessed=0, transcendentals=0),
        name=name,
        **grid,
    )(*operands)


def whole(shape):
    return pl.BlockSpec(shape, lambda *i: (0,) * len(shape), pipeline_mode=pl.Buffered(1))


def column_half(array, half):
    rows, columns = array.shape
    return pl.BlockSpec(
        (rows, columns // 2), lambda i: (0, half), pipeline_mode=pl.Buffered(1)
    )


def swap(values, axis, bits):
    size = lax.axis_size(axis)
    return lax.ppermute(values, axis, [(i, i ^ bits) for i in range(size)])


def gather_direct(values, axis):
    size = lax.axis_size(axis)
    if size > GROUP:
        return lax.all_gather(values, axis)
    place = lax.axis_index(axis)
    whole = jnp.zeros((size,) + values.shape, values.dtype)
    for r in range(size):
        piece = swap(values, axis, r) if r > 0 else values
        whole = lax.dynamic_update_slice(whole, piece[None], (place ^ r,) + (0,) * values.ndim)
    return whole


def gather_small(values, axis):
    size = lax.axis_size(axis)
    copies = jnp.broadcast_to(values[None], (size,) + values.shape)
    return lax.all_to_all(copies, axis, 0, 0, tiled=True)


def hidden_pieces(piece):
    near = swap(piece, "hidden", 1)
    far = swap(piece, "hidden", 2)
    return piece, near, far, swap(far, "hidden", 1)


def nothing(*refs):
    pass


def after(values, *others):
    anywhere = pl.BlockSpec(memory_space=pl.ANY)
    return pl.pallas_call(
        nothing,
        out_shape=jax.ShapeDtypeStruct(values.shape, values.dtype),
        in_specs=[anywhere] * (1 + len(others)),
        out_specs=anywhere,
        input_output_aliases={0: 0},
        cost_estimate=pl.CostEstimate(flops=0, bytes_accessed=0, transcendentals=0),
        name="after",
    )(values, *others)


def hidden_halves(kept, given, *others):
    low = (kept.astype(f32) + swap(given, "hidden", 1).astype(f32)).astype(bf16)
    far = swap(low, "hidden", 2)
    if others:
        far = after(far, *others)
    low = (low.astype(f32) + far.astype(f32)).astype(bf16)
    return low, swap(low, "hidden", 1)


def softplus(values):
    return jnp.maximum(values, 0.0) + jnp.log1p(jnp.exp(-jnp.abs(values)))


def sigmoid(values):
    return 1.0 / (1.0 + jnp.exp(-values))


def rms_scale(values):
    return lax.rsqrt(jnp.mean(values * values, axis=-1, keepdims=True) + epsilon)


def put(ref, values):
    width = values.shape[1]
    ref[:, :width] = values
    if ref.shape[1] > width:
        ref[:, width:] = jnp.zeros((values.shape[0], ref.shape[1] - width), ref.dtype)


def widen(tile, width):
    return jnp.concatenate([tile] * (width // LANES), axis=1)


def fold(values):
    total = values[:, :LANES]
    for k in range(1, values.shape[1] // LANES):
        total = total + values[:, k * LANES : (k + 1) * LANES]
    return total


def padded(count):
    return -(-count // LANES) * LANES


def same_segment(lengths, positions, delay):
    places = lax.broadcasted_iota(jnp.int32, (positions, 1), 0)
    first = lengths[0, 0]
    ending = first + lengths[0, 1]

    def segment(at):
        return (at >= first).astype(jnp.int32) + (at >= ending).astype(jnp.int32)

    same = (segment(places) == segment(places - delay)) & (places >= delay)
    return same.astype(f32)


def causal_conv(values, shifted, kernel, offset, lengths):
    positions = values.shape[0]
    taps = kernel.shape[0]
    shifted[:ROWS, :] = jnp.zeros((ROWS, values.shape[1]), f32)
    shifted[ROWS : ROWS + positions, :] = values
    result = offset + kernel[taps - 1 : taps] * values
    moved = [values]
    for delay in range(1, taps):
        part = shifted[ROWS - delay : ROWS - delay + positions, :]
        part = part * same_segment(lengths, positions, delay)
        moved.append(part)
        result = result + kernel[taps - 1 - delay : taps - delay] * part
    return result, moved


def column_tile(ref, first, entries, base):
    start = pl.multiple_of(base // LANES * LANES, LANES)
    tile = ref[first : first + entries, pl.ds(start, LANES)]
    return pltpu.roll(tile, lax.rem(LANES - lax.rem(base, LANES), LANES), 1)


def lane(tile, j, width):
    return jnp.broadcast_to(tile[:, j : j + 1], (tile.shape[0], width))


def split(values, place, kept, given):
    half = values.shape[0] // 2
    first = place == 0
    kept[...] = jnp.where(first, values[:half], values[half:]).astype(bf16)
    given[...] = jnp.where(first, values[half:], values[:half]).astype(bf16)


class Sizes:
    def __init__(self, entries, rank, taps, state):
        self.entries, self.rank, self.taps, self.state = entries, rank, taps, state
        self.step = entries
        self.proj = entries + rank
        self.conv = entries + rank + state
        self.rows = self.conv + ROWS
        self.vectors = 2 * ROWS


def mixer_in_body(
    sizes, lengths, places, tokens, cotangent, weight, pack,
    normed, inner, activity, part, small, vectors, share, shifted,
):
    devices, _, own = pack.shape
    for k in range(devices):
        piece = pack[k].astype(f32)
        small[:, k * own : (k + 1) * own] = piece[: sizes.rows]
        for half in range(2):
            at = (2 * k + half) * own
            row = sizes.rows + half * sizes.vectors
            vectors[:, at : at + own] = piece[row : row + sizes.vectors]
    values = tokens[...].astype(f32)
    low = (values * rms_scale(values) * vectors[0:1, :]).astype(bf16)
    normed[...] = low
    size = share.shape[0] // 2
    at = pl.ds(pl.multiple_of(places[0] * size, size), size)
    share[:size, :] = normed[at, :]
    share[size:, :] = cotangent[at, :]
    values = dot(low, weight[...], 1, 1)
    inner[...] = values
    kernel = small[sizes.conv : sizes.conv + sizes.taps, :]
    offset = small[sizes.conv + sizes.taps : sizes.conv + sizes.taps + 1, :]
    result, _ = causal_conv(values, shifted, kernel, offset, lengths)
    low = (result * sigmoid(result)).astype(bf16)
    activity[...] = low
    part[...] = dot(low, small[sizes.proj : sizes.conv, :].astype(bf16), 1, 1).astype(bf16)


def mixer_in(sizes, lengths, places, tokens, cotangent, weight, pack):
    positions, width = tokens.shape
    channels = weight.shape[0]
    return call(
        functools.partial(mixer_in_body, sizes),
        "mixer_in",
        (
            low_of(positions, width),
            shape_of(positions, channels),
            low_of(positions, channels),
            low_of(positions, sizes.state),
            shape_of(sizes.rows, channels),
            shape_of(sizes.vectors, width),
            low_of(positions // 2, width),
        ),
        [pltpu.VMEM((positions + 2 * ROWS, channels), f32)],
        2,
        (lengths, places, tokens, cotangent, weight, pack),
        3 * positions * width * channels,
    )


def scan_forward_body(
    sizes, lengths, parts, activity, small, out, states, pre, basis, rank_low,
    far_steps, inputs, rates, sums, wide,
):
    width = far_steps.shape[1]
    positions, channels = activity.shape
    entries, rank = sizes.entries, sizes.rank
    projected = jnp.sum(parts[...].astype(f32), axis=0)
    put(wide, projected)
    basis[...] = wide[...].T
    low = projected[:, :rank].astype(bf16)
    rank_low[...] = low
    values = dot(low, small[sizes.step : sizes.proj, :].astype(bf16))
    pre[...] = values
    at = sizes.conv + sizes.taps + 1
    step = softplus(values + small[at : at + 1, :])
    put(far_steps, jnp.where(same_segment(lengths, positions, 1) > 0, step, FAR))
    put(inputs, step * activity[...].astype(f32))
    put(rates, -LOG2E * jnp.exp(small[:entries, :]))
    rate = rates[...]

    def block(i, memory):
        base = pl.multiple_of(i * ROWS, ROWS)
        step_rows = far_steps[pl.ds(base, ROWS), :]
        input_rows = inputs[pl.ds(base, ROWS), :]
        tile_b = column_tile(basis, rank, entries, base)
        tile_c = column_tile(basis, rank + entries, entries, base)
        rows = []
        for j in range(ROWS):
            factor = jnp.exp2(step_rows[j : j + 1] * rate)
            memory = factor * memory + input_rows[j : j + 1] * lane(tile_b, j, width)
            states[base + j] = memory
            rows.append(jnp.sum(lane(tile_c, j, width) * memory, axis=0, keepdims=True))
        sums[pl.ds(base, ROWS), :] = jnp.concatenate(rows, axis=0)
        return memory

    lax.fori_loop(0, positions // ROWS, block, jnp.zeros(rate.shape, f32))
    out[...] = sums[:, :channels]


def scan_forward(sizes, lengths, parts, activity, small):
    positions, channels = activity.shape
    lanes = padded(channels)
    rows = pltpu.VMEM((positions, lanes), f32)
    state_lanes = padded(sizes.state)
    return call(
        functools.partial(scan_forward_body, sizes),
        "scan_forward",
        (
            shape_of(positions, channels),
            shape_of(positions, sizes.entries, lanes),
            shape_of(positions, channels),
            shape_of(state_lanes, positions),
            low_of(positions, sizes.rank),
        ),
        [rows, rows, pltpu.VMEM((sizes.entries, lanes), f32), rows, pltpu.VMEM((positions, state_lanes), f32)],
        1,
        (lengths, parts, activity, small),
        20 * positions * channels * sizes.entries * 16,
    )


def mixer_out_body(
    sizes, places, out, activity, normed, weight_z, weight_out, small, mixed, gate, kept, given
):
    shade = dot(normed[...], weight_z[...], 1, 1)
    gate[...] = shade
    at = sizes.conv + sizes.taps + 2
    values = out[...] + small[at : at + 1, :] * activity[...].astype(f32)
    low = (values * (shade * sigmoid(shade))).astype(bf16)
    mixed[...] = low
    split(dot(low, weight_out[...]), places[1], kept, given)


def mixer_out(sizes, places, out, activity, normed, weights, small):
    positions, channels = activity.shape
    width = normed.shape[1]
    return call(
        functools.partial(mixer_out_body, sizes),
        "mixer_out",
        (
            low_of(positions, channels),
            shape_of(positions, channels),
            low_of(positions // 2, width),
            low_of(positions // 2, width),
        ),
        scalars=1,
        operands=(places, out, activity, normed, weights, weights, small),
        flops=4 * positions * width * channels,
        parts={4: 0, 5: 1},
    )


def slots_of(codes, experts, capacity):
    positions = codes.shape[1]
    member = lax.broadcasted_iota(jnp.int32, (experts, positions), 0).astype(f32) == codes
    member = member.astype(f32)
    shape = (positions, positions)
    prior = lax.broadcasted_iota(jnp.int32, shape, 0) < lax.broadcasted_iota(jnp.int32, shape, 1)
    before = dot(member.astype(bf16), prior.astype(f32).astype(bf16))
    rank = jnp.sum(before * member, axis=0, keepdims=True)
    return jnp.where(codes >= 0, codes * capacity + rank, -1.0)


def picks(slots, first, count):
    shape = (count, slots.shape[1])
    return ((lax.broadcasted_iota(jnp.int32, shape, 0) + first).astype(f32) == slots).astype(f32)


def gelu_pair(values):
    root = 0.7978845608028654
    square = values * values
    bent = jnp.tanh(root * values * (1.0 + 0.044715 * square))
    half = 0.5 * (1.0 + bent)
    slope = half + 0.5 * values * (1.0 - bent * bent) * root * (1.0 + 3 * 0.044715 * square)
    return values * half, slope


def middle_body(
    places, tokens, low, other, vectors, codes, cotangent,
    resid, normed_two, sent, sent_grad, share, logits,
):
    half = low.shape[0]
    experts = logits.shape[0] - ROWS
    capacity = sent.shape[0] // experts
    resid[pl.ds(pl.multiple_of(places[1] * half, half), half), :] = low[...].astype(f32)
    resid[pl.ds(pl.multiple_of((1 - places[1]) * half, half), half), :] = other[...].astype(f32)
    values = tokens[...].astype(f32) + resid[...]
    resid[...] = values
    rows = (values * rms_scale(values) * vectors[1:2, :]).astype(bf16)
    normed_two[...] = rows
    logits[:experts, :] = dot(vectors[2 : 2 + experts, :].astype(bf16), rows, 1, 1)
    logits[experts:, :] = jnp.broadcast_to(codes[...], (ROWS, codes.shape[1]))
    every = picks(slots_of(codes[...], experts, capacity), 0, sent.shape[0]).astype(bf16)
    sent[...] = dot(every, rows).astype(bf16)
    sent_grad[...] = dot(every, cotangent[...]).astype(bf16)
    size = share.shape[0] // 2
    for k in range(2):
        at = pl.multiple_of((places[0] ^ (2 * k)) * size, size)
        share[k * size : (k + 1) * size, :] = normed_two[pl.ds(at, size), :]


def middle(places, tokens, low, other, vectors, codes, cotangent, experts):
    positions, width = tokens.shape
    slots = 3 * positions // 2
    return call(
        middle_body,
        "middle",
        (
            shape_of(positions, width),
            low_of(positions, width),
            low_of(slots, width),
            low_of(slots, width),
            low_of(positions // 2, width),
            shape_of(experts + ROWS, positions),
        ),
        (),
        1,
        (places, tokens, low, other, vectors, codes, cotangent),
        4 * positions * width * slots,
    )


def experts_body(
    places, codes, logits, rows, grads, up, down, out, kept, given, packed, slots, outs, backs, gate_row
):
    step = pl.program_id(0)
    experts = pl.num_programs(0)
    capacity = rows.shape[0]

    @pl.when(step == 0)
    def _():
        slots[...] = slots_of(codes[...], experts, capacity)
        gate_row[...] = jnp.zeros_like(gate_row)

    first = pl.multiple_of(step * capacity, capacity)
    active, slope = gelu_pair(dot(rows[...], up[0]))
    plain = dot(grads[...], down[0], 1, 1)
    low = active.astype(bf16)
    gate_slots = jnp.sum(low.astype(f32) * plain, axis=1, keepdims=True)
    chosen = picks(slots[...], first, capacity)
    gate_row[...] += jnp.sum(chosen * gate_slots, axis=0, keepdims=True)
    outs[pl.ds(first, capacity), :] = dot(low, down[0]).astype(bf16)
    backs[pl.ds(first, capacity), :] = dot((plain * slope).astype(bf16), up[0], 1, 1).astype(bf16)

    @pl.when(step == experts - 1)
    def _():
        every = picks(slots[...], 0, outs.shape[0]).astype(bf16)
        out[...] = dot(every, outs[...], 0, 0).astype(bf16)
        split(dot(every, backs[...], 0, 0), places[1], kept, given)
        packed[...] = logits[...]
        packed[experts + 1 : experts + 2, :] = gate_row[...]


def experts_local(places, codes, logits, rows, grads, up, down):
    slots, width = rows.shape
    experts, _, hidden = up.shape
    positions = codes.shape[1]
    capacity = slots // experts
    shapes = (
        low_of(positions, width),
        low_of(positions // 2, width),
        low_of(positions // 2, width),
        shape_of(*logits.shape),
    )
    return call(
        experts_body,
        "experts_local",
        shapes,
        [
            pltpu.VMEM((1, positions), f32),
            pltpu.VMEM((slots, width), bf16),
            pltpu.VMEM((slots, width), bf16),
            pltpu.VMEM((1, positions), f32),
        ],
        operands=(places, codes, logits, rows, grads, up, down),
        flops=8 * slots * width * hidden,
        grid=(experts,),
        in_specs=[
            pl.BlockSpec(memory_space=pltpu.SMEM),
            whole((1, positions)),
            whole(logits.shape),
            pl.BlockSpec((capacity, width), lambda i: (i, 0)),
            pl.BlockSpec((capacity, width), lambda i: (i, 0)),
            pl.BlockSpec((1, width, hidden), lambda i: (i, 0, 0)),
            pl.BlockSpec((1, hidden, width), lambda i: (i, 0, 0)),
        ],
        out_specs=tuple(whole(v.shape) for v in shapes),
    )


def expert_grads_body(
    places, codes, gates, *refs,
):
    rows, grads = refs[:2], refs[2:6]
    up, down, up_grad, down_grad, sent, sent_grad, gate_slots = refs[6:]
    step = pl.program_id(0)
    experts, total, width = sent.shape
    count, _, positions = codes.shape
    capacity = total // count
    quarter = positions // 4
    block = up_grad.shape[1]
    window = min(padded(block + LANES - 2 * ROWS), width)

    @pl.when(step == 0)
    def _():
        shape = (positions, positions)
        lanes = lax.broadcasted_iota(jnp.int32, shape, 1)
        part = lanes // quarter
        home = ((part % 2 * 2 + part // 2) ^ places[0]) * quarter + lanes % quarter
        order = (lax.broadcasted_iota(jnp.int32, shape, 0) == home).astype(f32).astype(bf16)
        for r in range(count):
            code = codes[r, experts : experts + 1, :]
            chosen = picks(slots_of(code, experts, capacity), 0, experts * capacity)
            pick = dot(chosen.astype(bf16), order).astype(bf16)
            gate = jnp.sum(chosen * gates[r], axis=1, keepdims=True)
            part = pl.ds(r * capacity, capacity)
            for pieces, target in ((rows, sent), (grads, sent_grad)):
                whole_rows = jnp.concatenate([piece[r] for piece in pieces], axis=0)
                moved = dot(pick, whole_rows).astype(bf16)
                for i in range(experts):
                    target[i, part, :] = moved[i * capacity : (i + 1) * capacity]
            for i in range(experts):
                gate_slots[i, part, :] = jnp.broadcast_to(
                    gate[i * capacity : (i + 1) * capacity], (capacity, LANES)
                )

    gate = gate_slots[step][:, :1]
    active, slope = gelu_pair(dot(sent[step], up[0]))
    plain = dot(sent_grad[step], down[0], 1, 1)
    grad_pre = (plain * slope * gate).astype(bf16)
    scaled = (active * gate).astype(bf16)
    start = jnp.minimum(places[2] * block // LANES * LANES, width - window)
    shift = lax.rem(window - (places[2] * block - start), window)
    own = pl.ds(pl.multiple_of(start, LANES), window)
    up_grad[0] = pltpu.roll(dot(sent[step, :, own], grad_pre, 0, 0), shift, 0)[:block]
    down_grad[0] = pltpu.roll(dot(sent_grad[step, :, own], scaled, 0, 0), shift, 0)[:block]


def expert_grads(places, codes, gates, rows, grads, up, down, block):
    count, _, positions = codes.shape
    experts, width, hidden = up.shape
    slots = count * (3 * positions // (2 * experts))
    shape = (experts, block, hidden)
    out = pl.BlockSpec((1, block, hidden), lambda i: (i, 0, 0))
    half = whole((count, positions // 2, width))

    def piece(values):
        last = values.shape[1] * 4 // positions - 1
        shape = (count, positions // 4, width)
        return pl.BlockSpec(shape, lambda i: (0, last, 0), pipeline_mode=pl.Buffered(1))

    return call(
        expert_grads_body,
        "expert_grads",
        (shape_of(*shape), shape_of(*shape)),
        [
            pltpu.VMEM((experts, slots, width), bf16),
            pltpu.VMEM((experts, slots, width), bf16),
            pltpu.VMEM((experts, slots, LANES), f32),
        ],
        operands=(places, codes, gates, *rows, *grads, up, down),
        flops=12 * experts * slots * width * hidden,
        known=True,
        grid=(experts,),
        in_specs=[
            pl.BlockSpec(memory_space=pltpu.SMEM),
            whole((count, codes.shape[1], positions)),
            whole((count, 1, positions)),
            half,
            half,
            *(piece(values) for values in grads),
            pl.BlockSpec((1, width, hidden), lambda i: (i, 0, 0)),
            pl.BlockSpec((1, hidden, width), lambda i: (i, 0, 0)),
        ],
        out_specs=(out, out),
    )


def sinkhorn(packed, gate_parts, experts):
    start = jnp.exp(packed[:, :experts, :])
    codes = packed[:, experts : experts + 1, :]
    grad_gates = jnp.sum(gate_parts[...], axis=0)
    valid = (codes >= 0).astype(f32)
    onehot = (lax.broadcasted_iota(jnp.int32, start.shape, 1).astype(f32) == codes).astype(f32)
    weights = start
    history = []
    for _ in range(SINK_ITERS):
        columns = jnp.sum(jnp.sum(weights * valid, axis=2, keepdims=True), axis=0, keepdims=True)
        scaled = weights / columns
        row_sums = jnp.sum(scaled, axis=1, keepdims=True)
        weights = scaled / row_sums
        history.append((columns, scaled, row_sums, weights))
    gates = experts * jnp.sum(weights * onehot, axis=1, keepdims=True)
    grads = experts * grad_gates * onehot
    for columns, scaled, row_sums, result in reversed(history):
        grads = (grads - jnp.sum(grads * result, axis=1, keepdims=True)) / row_sums
        term = jnp.sum(jnp.sum(grads * scaled, axis=2, keepdims=True), axis=0, keepdims=True)
        grads = (grads - valid * term) / columns
    return gates, grads * start


def backward_body(
    sizes, lengths, places, packed, gate_parts, low, other, vectors, resid, normed_two, cotangent, mixed,
    weight_out, out, activity, gate, pre, small, basis, states, rank_low,
    gates, grad_resid, out_grad, grad_act, grad_gate, grad_part, early,
    all_gates, all_grads, branch_grad, far_steps, steps, inputs, outer, rates, sum_input,
    sum_step, sums, shares, square,
):
    positions, width = resid.shape
    channels = activity.shape[1]
    lanes = far_steps.shape[1]
    entries, rank = sizes.entries, sizes.rank
    devices, own, _ = early.shape
    experts = all_grads.shape[1]
    half = low.shape[0]

    every_gate, every_grad = sinkhorn(packed, gate_parts, experts)
    gates[...] = every_gate
    all_gates[...] = every_gate
    all_grads[...] = every_grad
    grad_logits = all_grads[places[2]].astype(bf16)
    square[...] = jnp.broadcast_to(all_gates[places[2]], square.shape)
    gate_column = square[...].T[:, :1]

    branch_grad[pl.ds(pl.multiple_of(places[1] * half, half), half), :] = low[...].astype(f32)
    branch_grad[pl.ds(pl.multiple_of((1 - places[1]) * half, half), half), :] = other[...].astype(f32)
    at = lax.broadcasted_iota(jnp.int32, (positions, 1), 0)
    valid = (at < lengths[0, 0] + lengths[0, 1]).astype(f32)
    grad_two = dot(grad_logits, vectors[2 : 2 + experts, :].astype(bf16), 0, 0)
    grad_two = grad_two + branch_grad[...] * (gate_column * valid)
    values = resid[...]
    scale = rms_scale(values)
    unit = values * scale
    shares[...] = jnp.zeros_like(shares)
    shares[0:1, :] = jnp.sum(grad_two * unit, axis=0, keepdims=True)
    shares[ROWS : ROWS + experts, :] = dot(grad_logits, normed_two[...])
    scaled = grad_two * vectors[1:2, :]
    total = cotangent[...].astype(f32) * valid + scale * (
        scaled - unit * jnp.mean(scaled * unit, axis=-1, keepdims=True)
    )
    grad_resid[...] = total
    branch = total.astype(bf16)
    out_grad[...] = dot(mixed[...], branch, 0, 0).astype(bf16)
    grad = dot(branch, weight_out[...], 1, 1)

    row = sizes.conv + sizes.taps + 1
    shifted = pre[...] + small[row : row + 1, :]
    skip = small[row + 1 : row + 2, :]
    step = softplus(shifted)
    act = activity[...].astype(f32)
    put(far_steps, jnp.where(same_segment(lengths, positions, 1) > 0, step, FAR))
    put(steps, step)
    put(inputs, step * act)
    put(rates, -jnp.exp(small[:entries, :]))
    level = gate[...]
    shade = sigmoid(level)
    through = grad * level * shade
    put(outer, through)
    grad_level = grad * (out[...] + skip * act) * (shade * (1.0 + level * (1.0 - shade)))
    grad_gate[...] = grad_level.astype(bf16)
    put(sum_input, grad_level)
    turned = sum_input[...].T
    for k in range(devices):
        early[k, :, :positions] = turned[k * own : (k + 1) * own].astype(bf16)
    sums[...] = jnp.zeros_like(sums)
    skip_row = entries + rank + 1
    sums[skip_row : skip_row + 1, :channels] = jnp.sum(through * act, axis=0, keepdims=True)
    rate = rates[...]
    quick = rate * LOG2E
    blocks = positions // ROWS
    grad_part[...] = jnp.zeros_like(grad_part)
    lane_ids = lax.broadcasted_iota(jnp.int32, (entries, LANES), 1)

    def block(i, carried):
        later, rate_sum = carried
        base = pl.multiple_of((blocks - 1 - i) * ROWS, ROWS)
        far_rows = far_steps[pl.ds(base, ROWS), :]
        step_rows = steps[pl.ds(base, ROWS), :]
        input_rows = inputs[pl.ds(base, ROWS), :]
        outer_rows = outer[pl.ds(base, ROWS), :]
        columns_b = column_tile(basis, rank, entries, base)
        columns_c = column_tile(basis, rank + entries, entries, base)
        input_sums = [None] * ROWS
        step_sums = [None] * ROWS
        found_b = jnp.zeros((entries, LANES), f32)
        found_c = jnp.zeros((entries, LANES), f32)
        for j in reversed(range(ROWS)):
            tile_b = lane(columns_b, j, lanes)
            outside = outer_rows[j : j + 1]
            inside = input_rows[j : j + 1]
            state = states[base + j]
            flow = lane(columns_c, j, lanes) * outside + later
            later = jnp.exp2(far_rows[j : j + 1] * quick) * flow
            in_b = jnp.sum(fold(flow * inside), axis=1, keepdims=True)
            in_c = jnp.sum(fold(outside * state), axis=1, keepdims=True)
            found_b = jnp.where(lane_ids == j, in_b, found_b)
            found_c = jnp.where(lane_ids == j, in_c, found_c)
            input_sums[j] = jnp.sum(flow * tile_b, axis=0, keepdims=True)
            change = flow * (state - inside * tile_b)
            step_sums[j] = jnp.sum(change * rate, axis=0, keepdims=True)
            rate_sum = rate_sum + change * step_rows[j : j + 1]
        sum_input[pl.ds(base, ROWS), :] = jnp.concatenate(input_sums, axis=0)
        sum_step[pl.ds(base, ROWS), :] = jnp.concatenate(step_sums, axis=0)
        start = pl.multiple_of(base // LANES * LANES, LANES)
        shift = lax.rem(base, LANES)
        for first, found in ((0, found_b), (entries, found_c)):
            basis_grad = square.at[first : first + entries, pl.ds(start, LANES)]
            basis_grad[...] += pltpu.roll(found, shift, 1)
        return later, rate_sum

    square[...] = jnp.zeros_like(square)
    zero = jnp.zeros(rate.shape, f32)
    _, rate_sum = lax.fori_loop(0, blocks, block, (zero, zero))
    sums[:entries, :] = rate_sum * rate
    back_input = sum_input[:, :channels]
    grad_act[...] = outer[:, :channels] * skip + back_input * step
    grad_step = (back_input * act + sum_step[:, :channels]) * sigmoid(shifted)
    grad_low = grad_step.astype(bf16)
    sums[entries + rank : entries + rank + 1, :channels] = jnp.sum(grad_step, axis=0, keepdims=True)
    sums[entries : entries + rank, :channels] = dot(rank_low[...], grad_low, 0, 0)
    grad_part[:, :rank] = dot(
        grad_low, small[sizes.step : sizes.proj, :].astype(bf16), 1, 1
    ).astype(bf16)
    grad_part[:, rank : rank + 2 * entries] = square[...].T[:, : 2 * entries].astype(bf16)
    turned = sums[...].T
    spread = shares[...].T
    side = padded(sizes.vectors) - 2 * sizes.vectors
    for k in range(devices):
        early[k, :, positions : positions + side] = turned[k * own : (k + 1) * own, :side].astype(bf16)
        for piece in range(2):
            to = positions + side + piece * sizes.vectors
            source = (2 * k + piece) * own
            early[k, :, to : to + sizes.vectors] = spread[source : source + own].astype(bf16)


def backward(sizes, operands, experts, devices):
    resid, activity = operands[7], operands[13]
    positions, width = resid.shape
    channels = activity.shape[1]
    lanes = padded(channels)
    rows = pltpu.VMEM((positions, lanes), f32)
    return call(
        functools.partial(backward_body, sizes),
        "backward",
        (
            shape_of(devices, 1, positions),
            shape_of(positions, width),
            low_of(channels, width),
            shape_of(positions, channels),
            low_of(positions, channels),
            low_of(positions, padded(sizes.state)),
            low_of(devices, channels // devices, positions + LANES),
        ),
        [
            pltpu.VMEM((devices, 1, positions), f32),
            pltpu.VMEM((devices, experts, positions), f32),
            pltpu.VMEM((positions, width), f32),
            rows,
            rows,
            rows,
            rows,
            pltpu.VMEM((sizes.entries, lanes), f32),
            rows,
            rows,
            pltpu.VMEM((LANES, lanes), f32),
            pltpu.VMEM((sizes.vectors, width), f32),
            pltpu.VMEM((LANES, positions), f32),
        ],
        2,
        operands,
        40 * positions * width * channels,
        parts={11: 1},
    )


def mixer_back_body(
    sizes, lengths, places, parts, grad_act, activity, inner, small, weight_x, weight_z, grad_z, tokens,
    early, expert_out, out_grad, _grads, _rows, kept, given, late, shifted, wide, sums, shares,
):
    positions, channels = activity.shape
    devices, own, lanes = early.shape
    late[:, :, lanes : 2 * lanes] = early[...]
    late[:, :, 2 * lanes :] = out_grad[...]
    taps = sizes.taps
    low = jnp.sum(parts[...].astype(f32), axis=0)[:, : sizes.state].astype(bf16)
    state_grad = dot(activity[...], low, 0, 0)
    grad = grad_act[...] + dot(low, small[sizes.proj : sizes.conv, :].astype(bf16))
    kernel = small[sizes.conv : sizes.conv + taps, :]
    offset = small[sizes.conv + taps : sizes.conv + taps + 1, :]
    result, moved = causal_conv(inner[...], shifted, kernel, offset, lengths)
    shade = sigmoid(result)
    grad = grad * (shade * (1.0 + result * (1.0 - shade)))
    sums[...] = jnp.zeros_like(sums)
    sums[taps : taps + 1, :channels] = jnp.sum(grad, axis=0, keepdims=True)
    total = kernel[taps - 1 : taps] * grad
    shifted[positions : positions + ROWS, :] = jnp.zeros((ROWS, channels), f32)
    for delay in range(taps):
        row = taps - 1 - delay
        sums[row : row + 1, :channels] = jnp.sum(grad * moved[delay], axis=0, keepdims=True)
        if delay > 0:
            shifted[:positions, :] = grad * same_segment(lengths, positions, delay)
            total = total + kernel[row : row + 1] * shifted[delay : delay + positions, :]
    grad_x = total.astype(bf16)
    put(wide, total)
    turned = wide[...].T
    part = dot(grad_x, weight_x[...]) + dot(grad_z[...], weight_z[...])
    first = places[1] == 0
    low = part.astype(bf16)
    kept[...] = jnp.where(first, expert_out[...], low)
    given[...] = jnp.where(first, low, expert_out[...])
    values = tokens[...].astype(f32)
    shares[...] = jnp.broadcast_to(
        jnp.sum(part * (values * rms_scale(values)), axis=0, keepdims=True), shares.shape
    )
    spread = shares[...].T
    turned_sums = sums[...].T
    at = positions + sizes.state
    for k in range(devices):
        rows = slice(k * own, (k + 1) * own)
        late[k, :, :positions] = turned[rows].astype(bf16)
        late[k, :, positions:at] = state_grad[rows].astype(bf16)
        late[k, :, at : at + ROWS] = turned_sums[rows].astype(bf16)
        for piece in range(2):
            to = at + (1 + piece) * ROWS
            source = (2 * k + piece) * own
            late[k, :, to : to + ROWS] = spread[source : source + own].astype(bf16)


def mixer_back(sizes, operands):
    activity, tokens, early = operands[4], operands[10], operands[11]
    positions, width = tokens.shape
    channels = activity.shape[1]
    return call(
        functools.partial(mixer_back_body, sizes),
        "mixer_back",
        (low_of(positions, width), low_of(positions, width), low_of(*early.shape[:2], 2 * early.shape[2] + width)),
        [
            pltpu.VMEM((positions + 2 * ROWS, channels), f32),
            pltpu.VMEM((positions, padded(channels)), f32),
            pltpu.VMEM((ROWS, padded(channels)), f32),
            pltpu.VMEM((ROWS, width), f32),
        ],
        2,
        operands,
        6 * positions * width * channels,
        parts={8: 0},
        after=2,
    )


def proj_grads_body(
    sizes, places, both, *refs,
):
    pieces = refs[:4]
    grad_x, grad_z, state, conv, bias, gain_one, decay, proj, step_bias, skip, gain_two = refs[4:15]
    router, out, late_sum, early_sum, buffer = refs[15:]
    step = pl.program_id(0)
    count, own, lanes = both.shape
    _, size, width = pieces[0].shape
    lanes = lanes - width
    positions = 4 * size
    total_x = total_z = None
    add_late = add_early = add_out = None
    for r in range(count):
        for k, piece in enumerate(pieces):
            at = pl.multiple_of((places[0] ^ k) * size, size)
            buffer[r, pl.ds(at, size), :] = piece[r]
        part_x = dot(both[r, :, :positions], buffer[r])
        part_z = dot(both[r, :, lanes // 2 : lanes // 2 + positions], buffer[r])
        more_late = both[r, :, positions : lanes // 2].astype(f32)
        more_early = both[r, :, lanes // 2 + positions : lanes].astype(f32)
        more_out = both[r, :, lanes:].astype(f32)
        if r == 0:
            total_x, total_z, add_late, add_early = part_x, part_z, more_late, more_early
            add_out = more_out
        else:
            total_x, total_z = total_x + part_x, total_z + part_z
            add_late, add_early = add_late + more_late, add_early + more_early
            add_out = add_out + more_out

    @pl.when(step == 0)
    def _():
        grad_x[...] = total_x
        grad_z[...] = total_z
        out[...] = add_out
        late_sum[...] = jnp.zeros_like(late_sum)
        early_sum[...] = jnp.zeros_like(early_sum)
        late_sum[:own, :] = add_late
        early_sum[:own, :] = add_early

    @pl.when(step > 0)
    def _():
        grad_x[...] += total_x
        grad_z[...] += total_z
        out[...] += add_out
        late_sum[:own, :] += add_late
        early_sum[:own, :] += add_early

    @pl.when(step == pl.num_programs(0) - 1)
    def _():
        state[...] = late_sum[:own, : sizes.state]
        turned = late_sum[...].T[sizes.state :, :own]
        conv[...] = turned[: sizes.taps]
        bias[...] = turned[sizes.taps : sizes.taps + 1]
        gain_one[:, :own] = turned[ROWS : ROWS + 1]
        gain_one[:, own:] = turned[2 * ROWS : 2 * ROWS + 1]
        turned = early_sum[...].T[:, :own]
        at = sizes.entries + sizes.rank
        decay[...] = turned[: sizes.entries]
        proj[...] = turned[sizes.entries : at]
        step_bias[...] = turned[at : at + 1]
        skip[...] = turned[at + 1 : at + 2]
        for half_at, columns in ((0, slice(0, own)), (sizes.vectors, slice(own, 2 * own))):
            row = LANES - 2 * sizes.vectors + half_at
            gain_two[:, columns] = turned[row : row + 1]
            router[:, columns] = turned[row + ROWS : row + ROWS + router.shape[0]]


def proj_grads(sizes, experts, places, both, pieces):
    devices, own, lanes = both.shape
    _, size, width = pieces[-1].shape
    positions = 4 * size
    group = min(devices, GROUP)
    shapes = (
        (own, width),
        (own, width),
        (own, sizes.state),
        (sizes.taps, own),
        (1, own),
        (1, 2 * own),
        (sizes.entries, own),
        (sizes.rank, own),
        (1, own),
        (1, own),
        (1, 2 * own),
        (experts, 2 * own),
        (own, width),
    )
    few = pl.BlockSpec((group, own, lanes), lambda i: (i, 0, 0))
    return call(
        functools.partial(proj_grads_body, sizes),
        "proj_grads",
        tuple(shape_of(*shape) for shape in shapes),
        [
            pltpu.VMEM((padded(own), LANES), f32),
            pltpu.VMEM((padded(own), LANES), f32),
            pltpu.VMEM((group, positions, width), bf16),
        ],
        operands=(places, both, *pieces),
        flops=8 * devices * size * width * own,
        grid=(devices // group,),
        in_specs=[
            pl.BlockSpec(memory_space=pltpu.SMEM),
            few,
            *([pl.BlockSpec((group, size, width), lambda i: (i, 0, 0))] * 4),
        ],
        out_specs=tuple(whole(shape) for shape in shapes),
    )


def local(
    tokens,
    cotangent,
    seq_lengths,
    routes,
    mixer_gain,
    proj_x,
    proj_z,
    conv_weight,
    conv_bias,
    state_proj,
    step_proj,
    step_bias,
    decay_log,
    skip_gain,
    out_proj,
    moe_gain,
    router,
    expert_up,
    expert_down,
):
    devices = lax.axis_size("expert")
    hidden = lax.axis_size("hidden")
    index = lax.axis_index("expert")
    place = lax.axis_index("hidden")
    positions, width = tokens.shape
    block = mixer_gain.shape[0]
    experts = expert_up.shape[0]
    own = proj_x.shape[1]
    channels = devices * own
    taps = conv_weight.shape[0]
    sizes = Sizes(decay_log.shape[0], step_proj.shape[0], taps, state_proj.shape[1])
    places = jnp.stack([place, place % 2, index])

    valid = jnp.arange(positions, dtype=jnp.int32) < seq_lengths[0, 0] + seq_lengths[0, 1]
    codes = jnp.where(valid, routes[:, 0].astype(f32), -1.0)[None]

    later = jnp.concatenate([proj_z.T, out_proj], axis=1)
    later, turned_x = lax.optimization_barrier((later, proj_x.T))
    weights = lax.all_gather(later, "expert").reshape(channels, 2 * width)
    weight_x = gather_direct(turned_x, "expert").reshape(channels, width)
    vectors = jnp.concatenate([mixer_gain[None], moe_gain[None], router.T])
    vectors = jnp.pad(vectors, ((0, sizes.vectors - vectors.shape[0]), (0, 0)))
    few = jnp.concatenate([conv_weight, conv_bias[None], step_bias[None], skip_gain[None]])
    pack = [
        decay_log,
        step_proj,
        state_proj.T,
        jnp.pad(few, ((0, ROWS - few.shape[0]), (0, 0))),
        vectors[:, :own],
        vectors[:, own:],
    ]
    pack = gather_small(jnp.concatenate(pack), "expert")

    normed, inner_x, activity, part, small, vectors, share = mixer_in(
        sizes, seq_lengths, places, tokens, cotangent, weight_x, pack
    )
    parts = lax.all_gather(part, "hidden")
    scanned, states, step_pre, basis, rank_low = scan_forward(
        sizes, seq_lengths, parts, activity, small
    )
    quarter = positions // hidden
    share = lax.all_gather(share, "expert")
    mixed, gate_z, kept, given = mixer_out(
        sizes, places, scanned, activity, normed, weights, small
    )
    low, other = hidden_halves(kept, given)
    resid, normed_two, sent, sent_grad, own_half, logits = middle(
        places, tokens, low, other, vectors, codes, cotangent, experts
    )
    own_half = lax.all_gather(own_half, "expert")
    out_part, kept, given, packed = experts_local(
        places, codes, logits, sent, sent_grad, expert_up, expert_down
    )
    packed = gather_small(packed, "expert")
    gate_parts = lax.all_gather(packed[:, experts + 1 : experts + 2], "hidden")
    low, other = hidden_halves(kept, given, gate_parts)
    share = after(share, gate_parts, other)
    near = swap(share, "hidden", 1)
    far = swap(share[:, quarter:], "hidden", 2)
    operands = (
        seq_lengths, places, packed, gate_parts, low, other, vectors, resid, normed_two, cotangent, mixed,
        weights, scanned, activity, gate_z, step_pre, small, basis, states, rank_low,
    )
    gates, grad_resid, out_grad, grad_act, grad_z, grad_part, early = backward(
        sizes, operands, experts, devices
    )
    own_half = after(own_half, gates)
    parts = lax.all_gather(grad_part, "hidden")
    kept, given, late = mixer_back(
        sizes,
        (
            seq_lengths, places, parts, grad_act, activity, inner_x, small, weight_x, weights, grad_z,
            tokens, early, out_part, out_grad.reshape(devices, own, width),
            far, own_half,
        ),
    )
    late = lax.all_to_all(late, "expert", 0, 0, tiled=True)
    halves = (own_half, swap(own_half, "hidden", 1))

    last = swap(far, "hidden", 1)
    group = min(devices, GROUP)
    pieces = (packed, gates, halves, (share, far, near, last))
    if group == devices:
        up_grad, down_grad = expert_grads(places, *pieces, expert_up, expert_down, block)
    else:

        def add(total, some):
            part = expert_grads(places, *some, expert_up, expert_down, block)
            return (total[0] + part[0], total[1] + part[1]), None

        grouped = jax.tree.map(lambda v: v.reshape((-1, group) + v.shape[1:]), pieces)
        zero = jnp.zeros((experts, block, expert_up.shape[2]), f32)
        (up_grad, down_grad), _ = lax.scan(add, (zero, zero), grouped)
    low, other = hidden_halves(kept, given, up_grad)
    first = place % 2 == 0
    returned = jnp.where(first, low, other).astype(f32)
    grad_normed = jnp.where(first, other, low).astype(f32)
    values = tokens.astype(f32)
    scale = rms_scale(values)
    unit = values * scale
    scaled = grad_normed * vectors[0:1]
    tokens_grad = grad_resid + scale * (
        scaled - unit * jnp.mean(scaled * unit, axis=-1, keepdims=True)
    )
    gate_values = lax.dynamic_index_in_dim(gates, index, 0, keepdims=False)[0]
    layer_out = valid.astype(f32)[:, None] * (resid + gate_values[:, None] * returned)

    normed_far = swap(after(share[:, :quarter], kept), "hidden", 2)
    normed_pieces = (share, near, normed_far, swap(normed_far, "hidden", 1))
    projected = proj_grads(sizes, experts, places, late, normed_pieces)
    grad_x, grad_zw, state_grad, conv_grad, conv_bias_grad, gain_one_grad = projected[:6]
    decay_grad, step_proj_grad, step_bias_grad, skip_grad, gain_two_grad = projected[6:11]
    router_grad, out_grad = projected[11:]
    gain_one_grad = jnp.sum(lax.all_gather(gain_one_grad, "hidden"), axis=0)
    return (
        layer_out.astype(bf16),
        tokens_grad,
        gain_one_grad.reshape(-1),
        grad_x.T,
        grad_zw.T,
        conv_grad,
        conv_bias_grad.reshape(-1),
        state_grad,
        step_proj_grad,
        step_bias_grad.reshape(-1),
        decay_grad,
        skip_grad.reshape(-1),
        out_grad,
        gain_two_grad.reshape(-1),
        router_grad.T,
        up_grad,
        down_grad.transpose(0, 2, 1),
    )


def solution(mesh):
    in_specs = (
        P("expert", None),
        P("expert", None),
        P("expert", None),
        P("expert", None),
        P("expert"),
        P(None, ("expert", "hidden")),
        P(None, ("expert", "hidden")),
        P(None, ("expert", "hidden")),
        P(("expert", "hidden")),
        P(("expert", "hidden"), None),
        P(None, ("expert", "hidden")),
        P(("expert", "hidden")),
        P(None, ("expert", "hidden")),
        P(("expert", "hidden")),
        P(("expert", "hidden"), None),
        P("expert"),
        P("expert", None),
        P(None, None, "hidden"),
        P(None, "hidden", None),
    )
    out_specs = (
        P("expert", None),
        P("expert", None),
        P("expert"),
        P(None, ("expert", "hidden")),
        P(None, ("expert", "hidden")),
        P(None, ("expert", "hidden")),
        P(("expert", "hidden")),
        P(("expert", "hidden"), None),
        P(None, ("expert", "hidden")),
        P(("expert", "hidden")),
        P(None, ("expert", "hidden")),
        P(("expert", "hidden")),
        P(("expert", "hidden"), None),
        P("expert"),
        P("expert", None),
        P(None, "expert", "hidden"),
        P(None, "hidden", "expert"),
    )
    return jax.shard_map(local, mesh=mesh, in_specs=in_specs, out_specs=out_specs, check_vma=False)
```
